512 devices in a mesh: gx: 16 (over x, z_lo), gy: 8 (over z_hi, core), gz: 4 (over y).
Axes of the slice: x: 4, y: 4, z: 16 (z_hi: 4, z_lo: 4; z = z_hi * 4 + z_lo), core: 2. Of those that a mesh axis runs over, the one named last changes fastest.
Arguments:
- coarse: float32 [16, 32, 16, 128], P(None, 'gx', 'gy', 'gz'), may hold values from -6 to 6
- cotangent: float32 [16, 128, 64, 512], P(None, 'gx', 'gy', 'gz'), may hold values from -6 to 6
- edge_in: float32 [16, 35], replicated, may hold values from -1 to 1
- edge_out: float32 [16, 16], replicated, may hold values from -1.5 to 1.5
- node_in: float32 [16, 32], replicated, may hold values from -1 to 1
- node_out: float32 [16, 16], replicated, may hold values from -1.5 to 1.5
- biases: float32 [3, 16], replicated, may hold values from -3 to 3
Outputs:
- grad_coarse: float32 [16, 32, 16, 128], P(None, 'gx', 'gy', 'gz')
- grad_edge_in: float32 [16, 35], replicated
- grad_edge_out: float32 [16, 16], replicated
- grad_node_in: float32 [16, 32], replicated
- grad_node_out: float32 [16, 16], replicated
- grad_biases: float32 [3, 16], replicated
The draws below stay inside these ranges and needn't reach their ends.
All inputs are finite; a program needn't handle non-finite values.
Results may differ from the reference program's by a relative error of at most 0.00023.
Values sent between devices are 32-bit elements; how exact they have to be, the bound alone decides.
A program may use at most 64 MiB of HBM per device.

```python
import jax
import jax.numpy as jnp
import numpy as np
from jax import lax

HIDDEN_FEATURES = 16
P_SIZE = 8
ELEMENTS_FIRST = 16
ELEMENTS_SECOND = 8
ELEMENTS_THIRD = 64
NX = 128
NY = 64
NZ = 512


def block_scale(stream_key, dims, cuts, smallest, top_value):
    factor_of, own = 1.0, jax.random.fold_in(stream_key, 6)
    for axis_at, shards_of in cuts:
        draws = jnp.exp(jax.random.uniform(jax.random.fold_in(own, axis_at), (shards_of,), jnp.float32, smallest / len(cuts), top_value / len(cuts)))
        factor_of = factor_of * jnp.repeat(draws, dims[axis_at] // shards_of).reshape([-1 if axis == axis_at else 1 for axis in range(len(dims))])
    return factor_of


def centred(own_key, extent, spread, reach, cuts=(), kind=jnp.bfloat16):
    values = jax.random.normal(own_key, extent, jnp.float32) * spread
    if len(cuts) > 0:
        values = block_scale(own_key, extent, cuts, -0.22, 0.18) * values
    return jnp.clip(values, min=-reach, max=reach).astype(kind)


def setup_inputs(seed: int = 0) -> dict:
    seeds = jax.random.split(jax.random.key(seed), 8)
    coarse = centred(seeds[0], (HIDDEN_FEATURES, 2 * ELEMENTS_FIRST, 2 * ELEMENTS_SECOND, 2 * ELEMENTS_THIRD), 1.0, 6.0, ((1, 16), (2, 8), (3, 4)), jnp.float32)
    cotangent = centred(seeds[1], (HIDDEN_FEATURES, NX, NY, NZ), 1.0, 6.0, ((1, 16), (2, 8), (3, 4)), jnp.float32)
    edge_in = centred(seeds[2], (HIDDEN_FEATURES, 2 * HIDDEN_FEATURES + 3), (2 * HIDDEN_FEATURES) ** -0.5, 1.0, (), jnp.float32)
    edge_out = centred(seeds[3], (HIDDEN_FEATURES, HIDDEN_FEATURES), HIDDEN_FEATURES ** -0.5, 1.5, (), jnp.float32)
    node_in = centred(seeds[4], (HIDDEN_FEATURES, 2 * HIDDEN_FEATURES), (2 * HIDDEN_FEATURES) ** -0.5, 1.0, (), jnp.float32)
    node_out = centred(seeds[5], (HIDDEN_FEATURES, HIDDEN_FEATURES), HIDDEN_FEATURES ** -0.5, 1.5, (), jnp.float32)
    biases = centred(seeds[6], (3, HIDDEN_FEATURES), 0.5, 3.0, (), jnp.float32)
    return {"coarse": coarse, "cotangent": cotangent, "edge_in": edge_in, "edge_out": edge_out, "node_in": node_in, "node_out": node_out, "biases": biases}


highest = lax.Precision.HIGHEST
gll_points = np.array([-1.0, -0.8717401485096066, -0.5917001814331423, -0.2092992179024789, 0.2092992179024789, 0.5917001814331423, 0.8717401485096066, 1.0])
lagrange_table = np.stack([(1.0 - gll_points) / 2.0, (1.0 + gll_points) / 2.0], 1)
plus_gaps = np.concatenate([np.diff(gll_points), np.zeros(1)])
minus_gaps = np.concatenate([np.zeros(1), -np.diff(gll_points)])
plus_allowed = np.concatenate([np.ones(7), np.zeros(1)])
minus_allowed = np.concatenate([np.zeros(1), np.ones(7)])

def count_lookup_grid(length, per_element, first_layer, all_layers, walled):
    position = jnp.arange(length, dtype=jnp.int32)
    within = position % per_element
    counts = jnp.where((within == 0) | (within == per_element - 1), 2.0, 1.0)
    if walled:
        global_layer = first_layer + position
        counts = jnp.where((global_layer == 0) | (global_layer == all_layers - 1), 1.0, counts)
    return counts.astype(jnp.float32)

def exterior_counts(count_x, count_y, count_z):
    return count_x[:, None, None] * count_y[None, :, None] * count_z[None, None, :]

def place_along(vector, axis_dim):
    dims_out = [1, 1, 1, 1]
    dims_out[axis_dim] = vector.shape[0]
    return vector.reshape(tuple(dims_out))

def assemble_axis(source, axis_dim, lower_rim, upper_rim, per_element):
    dims_in = source.shape
    blocks = dims_in[axis_dim] // per_element
    blocked = source.reshape(dims_in[:axis_dim] + (blocks, per_element) + dims_in[axis_dim + 1:])
    first_layers = lax.index_in_dim(blocked, 0, axis_dim + 1, keepdims=False)
    last_layers = lax.index_in_dim(blocked, per_element - 1, axis_dim + 1, keepdims=False)
    before = jnp.concatenate([lower_rim, lax.slice_in_dim(last_layers, 0, blocks - 1, axis=axis_dim)], axis_dim)
    following = jnp.concatenate([lax.slice_in_dim(first_layers, 1, blocks, axis=axis_dim), upper_rim], axis_dim)
    leading = (slice(None),) * (axis_dim + 1)
    blocked = blocked.at[leading + (0,)].add(before)
    blocked = blocked.at[leading + (per_element - 1,)].add(following)
    return blocked.reshape(dims_in)

def assemble_global(source, per_element):
    for axis_dim, periodic in ((1, True), (2, False), (3, True)):
        length = source.shape[axis_dim]
        lower_rim = lax.slice_in_dim(source, length - 1, length, axis=axis_dim)
        upper_rim = lax.slice_in_dim(source, 0, 1, axis=axis_dim)
        if not periodic:
            lower_rim = jnp.zeros_like(lower_rim)
            upper_rim = jnp.zeros_like(upper_rim)
        source = assemble_axis(source, axis_dim, lower_rim, upper_rim, per_element)
    return source

def shift_within(source, axis_dim, offset):
    length = source.shape[axis_dim]
    zeros_layer = jnp.zeros_like(lax.slice_in_dim(source, 0, 1, axis=axis_dim))
    if offset > 0:
        return jnp.concatenate([lax.slice_in_dim(source, 1, length, axis=axis_dim), zeros_layer], axis_dim)
    return jnp.concatenate([zeros_layer, lax.slice_in_dim(source, 0, length - 1, axis=axis_dim)], axis_dim)

def edge_geometry(count_x, count_y, count_z, per_element):
    counts = (count_x, count_y, count_z)
    multiple = exterior_counts(count_x, count_y, count_z)[None]
    entries = []
    for axis_dim in (1, 2, 3):
        along_counts = counts[axis_dim - 1]
        blocks = along_counts.shape[0] // per_element
        for offset, gap_table, allowed in ((1, plus_gaps, plus_allowed), (-1, minus_gaps, minus_allowed)):
            spacing = place_along(jnp.tile(jnp.asarray(gap_table, dtype=jnp.float32), blocks), axis_dim)
            mask_row = jnp.tile(jnp.asarray(allowed, dtype=jnp.float32), blocks) * along_counts
            weight = place_along(mask_row, axis_dim) / multiple
            entries.append((axis_dim, offset, spacing, weight))
    return entries

def refine(source):
    weights_1d = jnp.asarray(lagrange_table, dtype=jnp.float32)
    channels, size_x, size_y, size_z = source.shape
    source = source.reshape(channels, size_x // 2, 2, size_y, size_z)
    source = jnp.einsum('cepyz,ap->ceayz', source, weights_1d, precision=highest).reshape(channels, size_x * 4, size_y, size_z)
    source = source.reshape(channels, size_x * 4, size_y // 2, 2, size_z)
    source = jnp.einsum('cxepz,ap->cxeaz', source, weights_1d, precision=highest).reshape(channels, size_x * 4, size_y * 4, size_z)
    source = source.reshape(channels, size_x * 4, size_y * 4, size_z // 2, 2)
    source = jnp.einsum('cxyep,ap->cxyea', source, weights_1d, precision=highest)
    return source.reshape(channels, size_x * 4, size_y * 4, size_z * 4)

def messages(source, edge_in, edge_out, biases, geometry):
    channels = source.shape[0]
    own_part = jnp.einsum('oc,cxyz->oxyz', edge_in[:, :channels], source, precision=highest) + biases[0][:, None, None, None]
    other_part = jnp.einsum('oc,cxyz->oxyz', edge_in[:, channels:2 * channels], source, precision=highest)
    summed = jnp.zeros_like(own_part)
    weight_sum = jnp.zeros_like(geometry[0][3])
    for axis_dim, offset, spacing, weight in geometry:
        neighbour = shift_within(other_part, axis_dim, offset)
        column = edge_in[:, 2 * channels + axis_dim - 1][:, None, None, None]
        summed = summed + weight * jax.nn.elu(own_part + neighbour + spacing * column)
        weight_sum = weight_sum + weight
    mixed = jnp.einsum('oc,cxyz->oxyz', edge_out, summed, precision=highest)
    return mixed + biases[1][:, None, None, None] * weight_sum

def node_update(source, gathered, node_in, node_out, biases):
    channels = source.shape[0]
    hidden = jnp.einsum('oc,cxyz->oxyz', node_in[:, :channels], source, precision=highest)
    hidden = hidden + jnp.einsum('oc,cxyz->oxyz', node_in[:, channels:], gathered, precision=highest)
    hidden = hidden + biases[2][:, None, None, None]
    return source + jnp.einsum('oc,cxyz->oxyz', node_out, jax.nn.elu(hidden), precision=highest)

def reference(coarse, cotangent, edge_in, edge_out, node_in, node_out, biases):
    count_x = count_lookup_grid(NX, P_SIZE, 0, NX, False)
    count_y = count_lookup_grid(NY, P_SIZE, 0, NY, True)
    count_z = count_lookup_grid(NZ, P_SIZE, 0, NZ, False)
    coarse_multiplicity = exterior_counts(count_lookup_grid(2 * ELEMENTS_FIRST, 2, 0, 2 * ELEMENTS_FIRST, False), count_lookup_grid(2 * ELEMENTS_SECOND, 2, 0, 2 * ELEMENTS_SECOND, True), count_lookup_grid(2 * ELEMENTS_THIRD, 2, 0, 2 * ELEMENTS_THIRD, False))[None]
    geometry = edge_geometry(count_x, count_y, count_z, P_SIZE)

    def forward(coarse_in, e_first, e_second, n_first, n_second, bias_all):
        mean = assemble_global(coarse_in, 2) / coarse_multiplicity
        fine = refine(mean)
        local = messages(fine, e_first, e_second, bias_all, geometry)
        gathered = assemble_global(local, P_SIZE)
        return node_update(fine, gathered, n_first, n_second, bias_all)
    output, pullback = jax.vjp(forward, coarse, edge_in, edge_out, node_in, node_out, biases)
    gradients = pullback(cotangent)
    factor = float(NX * NY * NZ) ** (-0.5)
    return (gradients[0], gradients[1] * factor, gradients[2] * factor, gradients[3] * factor, gradients[4] * factor, gradients[5] * factor)
```

```python
import jax
import jax.numpy as jnp
import numpy as np
from jax import lax
from jax.experimental import pallas as pl
from jax.experimental.pallas import tpu as pltpu
from jax.sharding import PartitionSpec as P

MESH = pl.DeviceIdType.MESH
F32 = jnp.float32
BF16 = jnp.bfloat16
T = np.array(
    [
        -1.0,
        -0.8717401485096066,
        -0.5917001814331423,
        -0.2092992179024789,
        0.2092992179024789,
        0.5917001814331423,
        0.8717401485096066,
        1.0,
    ]
)
L0, L1 = (1.0 - T) / 2.0, (1.0 + T) / 2.0
LOG2E = float(np.log2(np.e))
LN2 = float(np.log(2.0))
GAP_UP = [float(T[i + 1] - T[i]) if i < 7 else float(T[1] - T[0]) for i in range(8)]
GAP_DOWN = [float(T[i - 1] - T[i]) if i > 0 else float(T[6] - T[7]) for i in range(8)]
Z_LOW = 4
CORES = 2
ABSENT = -1.0e5
SLOT = {0: 0, 1: 1, -1: 2, 2: 3}
STEPS = (-2, -1, 1, 2)

RZ, RZ_UP, RZ_DOWN, PROFILES, Y_STD, Y_NEXT, Y_GAP, DELTA = 0, 32, 64, 96, 136, 168, 296, 328
TABLE_ROWS = 376


def make_table():
    table = np.zeros((TABLE_ROWS, 128))
    for lane in range(128):
        e, a = divmod(lane, 8)
        table[RZ + e + 1, lane] += L0[a]
        table[RZ + e + 2, lane] += L1[a]
        if a < 7:
            table[RZ_UP + e + 1, lane] += L0[a + 1]
            table[RZ_UP + e + 2, lane] += L1[a + 1]
        else:
            table[RZ_UP + e + 2, lane] += L0[1]
            table[RZ_UP + e + 3, lane] += L1[1]
        if a > 0:
            table[RZ_DOWN + e + 1, lane] += L0[a - 1]
            table[RZ_DOWN + e + 2, lane] += L1[a - 1]
        else:
            table[RZ_DOWN + e, lane] += L0[6]
            table[RZ_DOWN + e + 1, lane] += L1[6]
        table[RZ_UP + 20, lane] = GAP_UP[a]
        table[RZ_DOWN + 20, lane] = GAP_DOWN[a]
    up = np.zeros((4, 8))
    down = np.zeros((4, 8))
    for y in range(8):
        if y < 7:
            up[1, y], up[2, y] = L0[y + 1], L1[y + 1]
        else:
            up[2, y], up[3, y] = L0[1], L1[1]
        if y > 0:
            down[1, y], down[2, y] = L0[y - 1], L1[y - 1]
        else:
            down[0, y], down[1, y] = L0[6], L1[6]
    for i, profile in enumerate((L1, up[2], up[3], down[2], down[0])):
        table[PROFILES + 8 * i : PROFILES + 8 * i + 8] = profile[:, None]
    for c in range(16):
        for y in range(8):
            lane = 8 * c + y
            table[Y_STD + c, lane] = L0[y]
            table[Y_STD + 16 + c, lane] = L1[y]
            for q in range(4):
                table[Y_NEXT + 16 * q + c, lane] = up[q, y]
                table[Y_NEXT + 64 + 16 * q + c, lane] = down[q, y]
            table[Y_GAP + c, lane] = GAP_UP[y]
            table[Y_GAP + 16 + c, lane] = GAP_DOWN[y]
            table[DELTA + c, lane] = 1.0
            table[DELTA + 16 + c, lane] = 1.0 if y == 0 else 0.0
            table[DELTA + 32 + c, lane] = 1.0 if y == 7 else 0.0
    return table.astype(np.float32)


NN = (((1,), (0,)), ((), ()))
NT = (((1,), (1,)), ((), ()))


def dot(a, b, dims=NN):
    return lax.dot_general(a, b, dims, preferred_element_type=F32)


def split(a):
    high = a.astype(BF16)
    return high, (a - high.astype(F32)).astype(BF16)


def mm(a, b, dims=NN):
    (ah, al), (bh, bl) = a, b
    return dot(ah, bh, dims) + (dot(ah, bl, dims) + dot(al, bh, dims))


def mm_exact(a, b, dims=NN):
    return dot(a[0], b, dims) + dot(a[1], b, dims)


def exact_mm(a, b, dims=NN):
    return dot(a, b[0], dims) + dot(a, b[1], dims)


def iota(shape, dim):
    return lax.broadcasted_iota(jnp.int32, shape, dim)


def ones_where(mask):
    return jnp.where(mask, 1.0, 0.0).astype(F32)


def spread(a, k):
    k = k % 4
    return a if k == 0 else pltpu.roll(a, 32 * k, 1)


def vertex_maps():
    row, col = iota((128, 128), 0), iota((128, 128), 1)
    layer, vertex = row % 32, col % 32 - 1
    same = (row // 32 == col // 32) & (vertex < 18)
    maps = []
    for shift in (0, 16, -16):
        v = vertex + shift
        maps.append(ones_where(same & ((layer == 2 * v - 1) | (layer == 2 * v))).astype(BF16))
    return maps


def make_main(sizes):
    n_x, n_y, n_z = sizes
    z_high = n_y // CORES
    n_layers = z_high * Z_LOW
    n_cols = n_x // Z_LOW
    n_plane = n_cols * n_z

    def kernel(
        coarse, cot_hbm, edge_in, edge_out, node_in, node_out, biases, table,
        out,
        cot, p0, zr, tb, xr, vx, yr, means, lhs_rows, rows, e_all, e_sum, s_all, hn_all, u_all, g_all, xf,
        gm, yb, gy_all, xb, gx_all, zb, payload, core_slot, col_slots, plane_slots, total,
        cot_sem, zf_s, zf_r, xf_s, xf_r, yf_s, yf_r, yb_s, yb_r, xb_s, xb_r, zb_s, zb_r,
        core_s, core_r, col_s, col_r, plane_s, plane_r, cast_s, cast_r,
    ):
        ix, iy, iz = lax.axis_index("gx"), lax.axis_index("gy"), lax.axis_index("gz")
        low = lax.rem(ix, Z_LOW)
        core = lax.rem(iy, CORES)
        layer = (iy // CORES) * Z_LOW + low
        on_core0 = core == 0
        is_root = on_core0 & (layer == 0)
        is_leaf = on_core0 & (layer != 0)

        def at_x(d):
            return (lax.rem(ix + (d + n_x), n_x), iy, iz)

        def at_y(d):
            return (ix, lax.rem(iy + (d + n_y), n_y), iz)

        def at_z(d):
            return (ix, iy, lax.rem(iz + (d + n_z), n_z))

        sibling = (ix, iy + 1 - 2 * core, iz)
        column_root = (ix - low, 0, iz)

        def in_column(k, c):
            return (ix + k % Z_LOW, (k // Z_LOW) * CORES + c, iz)

        def in_plane(k):
            col, row = k // n_z, k % n_z
            return (lax.rem(ix + Z_LOW * col, n_x), iy, lax.rem(iz + row, n_z))

        def send(src, dst, send_sem, recv_sem, device):
            return pltpu.make_async_remote_copy(
                src_ref=src, dst_ref=dst, send_sem=send_sem, recv_sem=recv_sem, device_id=device, device_id_type=MESH
            )

        def signal(device):
            pl.semaphore_signal(barrier, inc=1, device_id=device, device_id_type=MESH)

        load_cot = pltpu.make_async_copy(cot_hbm, cot, cot_sem)
        load_cot.start()
        barrier = pltpu.get_barrier_semaphore()
        for d in (-1, 1):
            signal(at_z(d))
        for d in STEPS:
            signal(at_x(d))
        for d in STEPS:
            signal(at_y(d))

        @pl.when(layer != 0)
        def _():
            signal(column_root)

        @pl.when(is_root)
        def _():
            for k in range(1, n_layers):
                signal(in_column(k, 0))
            for k in range(1, n_plane):
                signal(in_plane(k))

        expected = 10 + jnp.where(is_leaf, 1, 0) + jnp.where(is_root, CORES * (n_layers - 1) + n_plane - 1, 0)

        block = coarse[...]
        p0[...] = jnp.concatenate([block[:, p, q, :] for q in (0, 1) for p in (0, 1)], axis=1)
        pl.semaphore_wait(barrier, expected)

        z_sends = [
            send(p0, zr.at[0], zf_s.at[0], zf_r.at[0], at_z(1)),
            send(p0, zr.at[1], zf_s.at[1], zf_r.at[1], at_z(-1)),
        ]
        for c in z_sends:
            c.start()

        w_own, w_other = edge_in[:, 0:16], edge_in[:, 16:32]
        col_x, col_y, col_z = edge_in[:, 32:33], edge_in[:, 33:34], edge_in[:, 34:35]
        n_own, n_gathered = node_in[:, 0:16], node_in[:, 16:32]
        eye = ones_where(iota((16, 16), 0) == iota((16, 16), 1)).astype(BF16)
        delta = table[DELTA : DELTA + 16, :].astype(BF16)
        same_y = iota((128, 128), 0) % 8 == iota((128, 128), 1) % 8

        def transposed(w):
            return exact_mm(eye, split(w), NT)

        def widen(w):
            parts = []
            for part in split(w):
                left = dot(delta, part, (((0,), (0,)), ((), ()))).astype(BF16)
                parts.append(jnp.where(same_y, dot(left, delta), 0.0).astype(BF16))
            return tuple(parts)

        m1 = mm(split(n_gathered), split(edge_out[...]))
        m1_wide = widen(m1)
        m1_back = widen(transposed(m1))
        out_back = widen(transposed(node_out[...]))
        mix = split(jnp.concatenate([w_own, n_own, w_other], axis=0))
        mix_back = split(jnp.concatenate([transposed(n_own), transposed(w_own), transposed(w_other)], axis=1))
        bias_rows = biases[...]
        bias_cols = exact_mm(eye, split(bias_rows), NT)
        b0_col, b1_row, b2_col = bias_cols[:, 0:1], bias_rows[1:2, :], bias_cols[:, 2:3]
        nb_col = jnp.sum(n_gathered * b1_row, axis=1, keepdims=True)
        maps = vertex_maps()
        lane = iota((16, 128), 1)
        group, place = lane // 32, lane % 32
        gap_lane = ones_where((place == 20) & (group < 2))

        def blocks4(first):
            t = table[first : first + 32, :]
            zero = jnp.zeros((32, 128), F32)
            return split(
                jnp.concatenate(
                    [jnp.concatenate([t if i == j else zero for j in range(4)], axis=1) for i in range(4)], axis=0
                )
            )

        rz, rz_up, rz_down = blocks4(RZ), blocks4(RZ_UP), blocks4(RZ_DOWN)

        z_sends[0].wait_recv()
        z_sends[1].wait_recv()
        tb[...] = (
            mm_exact(split(p0[...]), maps[0])
            + mm_exact(split(zr[0]), maps[1])
            + mm_exact(split(zr[1]), maps[2])
        )
        x_sends = []
        for d in STEPS:
            i = STEPS.index(-d)
            x_sends.append(send(tb, xr.at[i], xf_s.at[i], xf_r.at[i], at_x(d)))
        for c in x_sends:
            c.start()

        load_cot.wait()
        for k in range(4):
            wide = jnp.concatenate([cot[:, 2 * k + i].reshape(128, 128) for i in (0, 1)], axis=1)
            u_all[:, :, 256 * k : 256 * k + 256] = mm(out_back, split(wide)).reshape(16, 8, 256)
        sum_all, sum_one = cot[:, 0], jnp.zeros((16, 8, 128), F32)
        for x in range(1, 8):
            sum_all = sum_all + cot[:, x]
            sum_one = sum_one + float(L1[x]) * cot[:, x]
        xf[:, :, 0:128] = sum_all - sum_one
        xf[:, :, 128:256] = sum_one

        for c in x_sends:
            c.wait_recv()
        x_blocks = {0: tb[...]}
        for i, d in enumerate(STEPS):
            x_blocks[d] = xr[i]
        for q in (0, 1):
            acc = jnp.zeros((16, 128), F32)
            for vertex in (-1, 0, 1, 2):
                for d in (vertex - 1, vertex):
                    moved = spread(x_blocks[d], SLOT[vertex] - (2 * q + vertex - d))
                    acc = acc + jnp.where(group == SLOT[vertex], moved, 0.0)
            vx[q] = acc
        y_sends = []
        for d in STEPS:
            i = STEPS.index(-d)
            qs = pl.ds(0, 2) if abs(d) == 1 else pl.ds(1 if d == 2 else 0, 1)
            y_sends.append(send(vx.at[qs], yr.at[i, qs], yf_s.at[i], yf_r.at[i], at_y(d)))
        for c in y_sends:
            c.start()

        def exists(d):
            return jnp.where((iy + d >= 0) & (iy + d < n_y), 1.0, 0.0).astype(F32)

        there = {d: exists(d) for d in (-2, -1, 0, 1, 2)}
        wall_low, wall_high = 1.0 - there[-1], 1.0 - there[1]
        y_index = iota((8, 128), 0)
        count = 6.0 - wall_low * ones_where(y_index == 0) - wall_high * ones_where(y_index == 7)
        ly, up1, up2, down1, down0 = (table[PROFILES + 8 * i : PROFILES + 8 * i + 8, :] for i in range(5))

        for c in y_sends:
            c.wait_recv()

        def y_block(d, q):
            return vx[q] if d == 0 else yr[STEPS.index(d), q] * there[d]

        for q in (-1, 0, 1, 2):
            copies = jnp.maximum(there[q - 1] + there[q], 1.0)
            means[q + 1] = (y_block(q - 1, 1) + y_block(q, 0)) * (0.25 / copies)

        mixed = mm(mix, split(jnp.concatenate([means[i] for i in range(4)], axis=1)))
        for i in range(4):
            lanes = slice(128 * i, 128 * i + 128)
            if i in (1, 2):
                lhs_rows[48 * (i - 1) : 48 * (i - 1) + 32, :] = mixed[0:32, lanes]
                lhs_rows[48 * (i - 1) + 32 : 48 * i, :] = mixed[32:48, lanes] + col_z * gap_lane
            else:
                first = 96 if i == 0 else 112
                lhs_rows[first : first + 16, :] = mixed[32:48, lanes]
        along = mm(split(lhs_rows[...]), rz)
        other01 = split(jnp.concatenate([lhs_rows[32:48, :], lhs_rows[80:96, :]], axis=0))
        along_up = mm(other01, (rz_up[0][:, 0:256], rz_up[1][:, 0:256]))
        along_down = mm(other01, (rz_down[0][:, 0:256], rz_down[1][:, 0:256]))

        def vertex_rows(field, q, vertex):
            first = {0: 0, 1: 48}[q] + 16 * field if q in (0, 1) else (96 if q == -1 else 112)
            s = SLOT[vertex]
            return along[first : first + 16, 128 * s : 128 * s + 128]

        def next_rows(source, q, vertex):
            return source[16 * q : 16 * q + 16, 128 * vertex : 128 * vertex + 128]

        def put(field, x, value):
            rows[pl.ds(128 * field + x, 16, stride=8), :] = value

        def line(a, b, t):
            return a + t * (b - a)

        for x in range(8):
            t = float(L1[x])
            here = float(T[x]) * col_x
            own = [
                (line(vertex_rows(0, q, 0), vertex_rows(0, q, 1), t) + (b0_col - here - (2 * q - 1.0) * col_y)) * LOG2E
                for q in (0, 1)
            ]
            put(0, x, own[0])
            put(1, x, own[1] - own[0])
            other = {
                q: (line(vertex_rows(2, q, 0), vertex_rows(2, q, 1), t) + (here + (2 * q - 1.0) * col_y)) * LOG2E
                for q in (-1, 0, 1, 2)
            }
            put(2, x, other[0])
            put(3, x, other[1] - other[0])
            put(5, x, (other[2] - other[0]) * there[1] + ABSENT * wall_high)
            put(6, x, (other[-1] - other[0]) * there[-1] + ABSENT * wall_low)
            for f, source in ((7, along_up), (9, along_down)):
                z = [
                    (line(next_rows(source, q, 0), next_rows(source, q, 1), t) + (here + (2 * q - 1.0) * col_y)) * LOG2E
                    for q in (0, 1)
                ]
                put(f, x, z[0])
                put(f + 1, x, z[1] - z[0])
            hn = [line(vertex_rows(1, q, 0), vertex_rows(1, q, 1), t) for q in (0, 1)]
            put(11, x, hn[0] + b2_col)
            put(12, x, hn[1] - hn[0])
            put(13, x, jnp.broadcast_to(nb_col, (16, 128)))
        for side, (a, b, t, at) in enumerate(((-1, 0, float(L1[6]), float(T[6]) - 2.0), (1, 2, float(L1[1]), float(T[1]) + 2.0))):
            other = [
                (line(vertex_rows(2, q, a), vertex_rows(2, q, b), t) + (at * col_x + (2 * q - 1.0) * col_y)) * LOG2E
                for q in (0, 1)
            ]
            put(4, 2 * side, other[0])
            put(4, 2 * side + 1, other[1] - other[0])

        def forward(c, carry):
            def row(field, x):
                return rows[pl.ds(128 * field + 8 * c + x, 1), :]

            other = [row(4, 0) + ly * row(4, 1)]
            for x in range(8):
                other.append(row(2, x) + ly * row(3, x))
            other.append(row(4, 2) + ly * row(4, 3))
            for x in range(8):
                own = row(0, x) + ly * row(1, x)
                a, d = row(2, x), row(3, x)
                senders = (
                    other[x + 2],
                    other[x],
                    a + up1 * d + up2 * row(5, x),
                    a + down1 * d + down0 * row(6, x),
                    row(7, x) + ly * row(8, x),
                    row(9, x) + ly * row(10, x),
                )
                tops, decays = None, None
                for k, sender in enumerate(senders):
                    z = own + sender
                    decay = jnp.exp2(jnp.minimum(z, 0.0))
                    top = jnp.maximum(z, 0.0)
                    e_all[k, x, c] = decay
                    tops = top if tops is None else tops + top
                    decays = decay if decays is None else decays + decay
                e_sum[x, c] = decays
                s_all[c, :, 128 * x : 128 * x + 128] = LN2 * tops + (decays - count)
                hn_all[c, :, 128 * x : 128 * x + 128] = row(11, x) + ly * row(12, x) + count * row(13, x)
            return carry

        lax.fori_loop(0, 16, forward, 0)

        outer_out = jnp.zeros((128, 128), F32)
        outer_in = jnp.zeros((128, 128), F32)
        dh_all = jnp.zeros((16, 8, 128), F32)
        dh_one = jnp.zeros((16, 8, 128), F32)
        for k in range(4):
            lanes = slice(256 * k, 256 * k + 256)
            s = split(s_all[:, :, lanes].reshape(128, 256))
            h = mm(m1_wide, s) + hn_all[:, :, lanes].reshape(128, 256)
            decay = jnp.exp(jnp.minimum(h, 0.0))
            a = jnp.maximum(h, 0.0) + (decay - 1.0)
            dh = decay * u_all[:, :, lanes].reshape(128, 256)
            dh_parts = split(dh)
            g_all[:, :, lanes] = mm(m1_back, dh_parts).reshape(16, 8, 256)
            wide = jnp.concatenate([cot[:, 2 * k + i].reshape(128, 128) for i in (0, 1)], axis=1)
            outer_out = outer_out + mm(split(wide), split(a), NT)
            outer_in = outer_in + mm(dh_parts, s, NT)
            for i in (0, 1):
                part = dh[:, 128 * i : 128 * i + 128].reshape(16, 8, 128)
                dh_all = dh_all + part
                dh_one = dh_one + float(L1[2 * k + i]) * part
        xf[:, :, 256:384] = dh_all - dh_one
        xf[:, :, 384:512] = dh_one

        def backward(c, carry):
            g = [g_all[c, :, 128 * x : 128 * x + 128] for x in range(8)]
            own = [g[x] * e_sum[x, c] for x in range(8)]

            def bz(k, x):
                return g[x] * e_all[k, x, c]

            def save(i, value):
                xf[c, :, 128 * i : 128 * i + 128] = value

            def reduce(first, values):
                everything, one = values[0], float(L1[1]) * values[1]
                for x in range(1, 8):
                    everything = everything + values[x]
                for x in range(2, 8):
                    one = one + float(L1[x]) * values[x]
                save(first, everything - one)
                save(first + 1, one)

            reduce(4, own)
            ups = [bz(0, x) for x in range(8)]
            downs = [bz(1, x) for x in range(8)]
            acc = GAP_UP[0] * ups[0] + GAP_DOWN[0] * downs[0]
            for x in range(1, 8):
                acc = acc + GAP_UP[x] * ups[x] + GAP_DOWN[x] * downs[x]
            save(6, acc)
            at = [downs[1]] + [ups[x - 1] + downs[x + 1] for x in range(1, 7)] + [ups[6]]
            everything, one = at[0], float(L1[1]) * at[1]
            for x in range(1, 8):
                everything = everything + at[x]
            for x in range(2, 8):
                one = one + float(L1[x]) * at[x]
            save(7, everything - one + float(L1[6]) * downs[0])
            save(8, one + float(L0[1]) * ups[7])
            save(9, float(L0[6]) * downs[0])
            save(10, float(L1[1]) * ups[7])
            for k in range(4):
                reduce(11 + 2 * k, [bz(2 + k, x) for x in range(8)])
            return carry

        lax.fori_loop(0, 16, backward, 0)

        def along_z(first, n, by):
            return mm(
                split(xf[:, :, 128 * first : 128 * (first + n)].reshape(128, 128 * n)),
                (by[0][:, 0 : 128 * n], by[1][:, 0 : 128 * n]),
                NT,
            )

        z1 = along_z(0, 4, rz)
        z2 = along_z(4, 3, rz)
        z3 = along_z(7, 4, rz) + along_z(15, 2, rz_up) + along_z(17, 2, rz_down)
        z4 = along_z(11, 4, rz)
        counting = (
            6.0 * table[DELTA : DELTA + 16, :]
            - wall_low * table[DELTA + 16 : DELTA + 32, :]
            - wall_high * table[DELTA + 32 : DELTA + 48, :]
        )
        left = split(jnp.concatenate([table[Y_STD : Y_STD + 32, :], counting], axis=0))
        std = mm(left, split(jnp.concatenate([z1, z2, z3], axis=1)))
        nxt = mm(split(table[Y_NEXT : Y_NEXT + 160, :]), split(z4))

        low_half, low_lanes = group < 2, ones_where(group < 2)
        fields = {}
        for q in (0, 1):
            r = slice(16 * q, 16 * q + 16)
            fields[q] = (std[r, 0:128], std[r, 128:256], std[r, 256:384])
        others = {}
        for q in (-1, 0, 1, 2):
            r_up = slice(16 * (q + 1), 16 * (q + 1) + 16)
            r_down = slice(64 + 16 * (q + 1), 64 + 16 * (q + 1) + 16)
            both = jnp.where(low_half, nxt[r_up, :] + pltpu.roll(nxt[r_down, :], 64, 1), 0.0)
            others[q] = both + fields[q][2] if q in (0, 1) else both

        zero = jnp.zeros((16, 128), F32)
        stacked = []
        for q in (-1, 0, 1, 2):
            if q in (0, 1):
                dh_q = jnp.where(low_half, pltpu.roll(fields[q][0], 64, 1), 0.0)
                own_q = jnp.where(low_half, fields[q][1], 0.0)
            else:
                dh_q, own_q = zero, zero
            stacked.append(jnp.concatenate([dh_q, own_q, others[q]], axis=0))
        back = mm(mix_back, split(jnp.concatenate(stacked, axis=1)))
        for q in (-1, 0, 1, 2):
            value = back[:, 128 * (q + 1) : 128 * (q + 2)]
            if q in (0, 1):
                value = value + jnp.where(low_half, fields[q][0], 0.0)
            gm[q + 1] = value
        y_back = []
        for d in STEPS:
            i = STEPS.index(-d)
            if abs(d) == 1:
                src, dst = gm.at[pl.ds(2 if d == 1 else 0, 2)], yb.at[i]
            else:
                src, dst = gm.at[pl.ds(3 if d == 2 else 0, 1)], yb.at[i, pl.ds(0 if d == 2 else 1, 1)]
            y_back.append(send(src, dst, yb_s.at[i], yb_r.at[i], at_y(d)))
        for c in y_back:
            c.start()

        summed_out = jnp.where(same_y, outer_out, 0.0)
        summed_in = jnp.where(same_y, outer_in, 0.0)
        big = exact_mm(delta, split(jnp.concatenate([summed_out, summed_in], axis=1)))
        r2, c2 = iota((128, 256), 0), iota((128, 256), 1)
        placing = ones_where((c2 // 128 * 16 + c2 % 128 // 8) == r2).astype(BF16)
        part = mm_exact(split(big), placing, NT)
        r8, l8 = iota((8, 128), 0), iota((8, 128), 1)

        def marked(r, mask):
            return ones_where((r8 == r) & mask)

        def right(first, rows16, special):
            pieces = []
            if rows16 is None:
                pieces.append(jnp.zeros((80, 128), F32))
            else:
                if first > 0:
                    pieces.append(jnp.zeros((first, 128), F32))
                pieces.append(rows16)
                if first < 64:
                    pieces.append(jnp.zeros((64 - first, 128), F32))
            pieces += [special, jnp.zeros((40, 128), F32)]
            return jnp.concatenate(pieces, axis=0)

        lefts, rights = [], []
        none8 = jnp.zeros((8, 128), F32)
        for q in (-1, 0, 1, 2):
            m = means[q + 1]
            if q in (0, 1):
                lefts.append(fields[q][0])
                rights.append(right(32, jnp.where(low_half, 0.0, pltpu.roll(m, 64, 1)), marked(4, l8 >= 64)))
                lefts.append(fields[q][1])
                rights.append(right(48, m * low_lanes, marked(3, l8 < 64) + marked(0, (l8 >= 64) & (l8 < 96))))
            lefts.append(others[q])
            rights.append(right(64, m, marked(2, (l8 % 32 == 20) & (l8 < 64)) if q in (0, 1) else none8))
        lefts += [std[32:48, 0:128], nxt[128:144, :], nxt[144:160, :]]
        rights += [
            right(0, None, marked(5, l8 >= 64)),
            right(0, None, marked(1, l8 < 64)),
            right(0, None, marked(1, l8 >= 64)),
        ]
        payload[...] = part + mm(split(jnp.concatenate(lefts, axis=1)), split(jnp.concatenate(rights, axis=1)), NT)

        to_core0 = send(payload, core_slot, core_s, core_r, sibling)
        to_root = send(payload, col_slots.at[jnp.maximum(layer - 1, 0)], col_s, col_r.at[jnp.maximum(layer - 1, 0)], column_root)

        @pl.when(core == 1)
        def _():
            to_core0.start()

        @pl.when(on_core0)
        def _():
            to_core0.wait_recv()
            payload[...] = payload[...] + core_slot[...]

        @pl.when(is_leaf)
        def _():
            to_root.start()

        for c in y_back:
            c.wait_recv()
        for q in (0, 1):
            value = gm[q + 1]
            for d in (-2, -1, 1, 2):
                if (d, q) not in ((-2, 1), (2, 0)):
                    value = value + yb[STEPS.index(d), q] * there[d]
            gy_all[q] = value
        x_back = []
        for d in STEPS:
            i = STEPS.index(-d)
            x_back.append(send(gy_all, xb.at[i], xb_s.at[i], xb_r.at[i], at_x(d)))
        for c in x_back:
            c.start()

        my_place = (ix // Z_LOW) * n_z + iz
        to_plane = [
            send(plane_slots.at[my_place], plane_slots.at[my_place], plane_s.at[k], plane_r.at[k], in_plane(k))
            for k in range(1, n_plane)
        ]

        @pl.when(is_root)
        def _():
            value = payload[...]
            for k in range(n_layers - 1):
                send(payload, col_slots.at[k], col_s, col_r.at[k], in_column(k + 1, 0)).wait_recv()
                value = value + col_slots[k]
            plane_slots[my_place] = value
            for c in to_plane:
                c.start()

        for c in x_back:
            c.wait_recv()
        for q in (0, 1):
            value = gy_all[q]
            for d in (-2, -1, 1, 2):
                for p in (0, 1):
                    vertex = p - d
                    if vertex in SLOT:
                        moved = spread(xb[STEPS.index(d), q], p - SLOT[vertex])
                        value = value + jnp.where(group == p, moved, 0.0)
            gx_all[q] = jnp.where(low_half, value, 0.0)
        z_back = [
            send(gx_all, zb.at[0], zb_s.at[0], zb_r.at[0], at_z(1)),
            send(gx_all, zb.at[1], zb_s.at[1], zb_r.at[1], at_z(-1)),
        ]
        for c in z_back:
            c.start()

        to_all = [
            send(total, total, cast_s.at[CORES * k + c], cast_r, in_column(k, c))
            for k in range(n_layers)
            for c in range(CORES)
            if (k, c) != (0, 0)
        ]

        @pl.when(is_root)
        def _():
            for k, c in enumerate(to_plane):
                c.wait_recv()
            value = plane_slots[0]
            for k in range(1, n_plane):
                value = value + plane_slots[k]
            total[...] = value
            for c in to_all:
                c.start()

        for c in z_back:
            c.wait_recv()
        for q in (0, 1):
            value = (
                mm_exact(split(gx_all[q]), maps[0], NT)
                + mm_exact(split(zb[0, q]), maps[2], NT)
                + mm_exact(split(zb[1, q]), maps[1], NT)
            )
            neighbour = there[-1] if q == 0 else there[1]
            out[16 * q : 16 * q + 16, :] = value * (0.25 / (1.0 + neighbour))

        @pl.when(jnp.logical_not(is_root))
        def _():
            to_all[0].wait_recv()

        out[32:48, :] = total[...]

        for c in z_sends + x_sends + y_sends + y_back + x_back + z_back:
            c.wait_send()

        @pl.when(core == 1)
        def _():
            to_core0.wait_send()

        @pl.when(is_leaf)
        def _():
            to_root.wait_send()

        @pl.when(is_root)
        def _():
            for c in to_plane + to_all:
                c.wait_send()

    block = pltpu.VMEM((16, 128), F32)

    def blocks(*lead):
        return pltpu.VMEM(lead + (16, 128), F32)

    dma = pltpu.SemaphoreType.DMA
    scratch = [
        pltpu.VMEM((16, 8, 8, 128), F32),
        block,
        blocks(2),
        block,
        blocks(4),
        blocks(2),
        blocks(4, 2),
        blocks(4),
        pltpu.VMEM((128, 128), F32),
        pltpu.VMEM((14 * 128, 128), F32),
        pltpu.VMEM((6, 8, 16, 8, 128), F32),
        pltpu.VMEM((8, 16, 8, 128), F32),
        pltpu.VMEM((16, 8, 1024), F32),
        pltpu.VMEM((16, 8, 1024), F32),
        pltpu.VMEM((16, 8, 1024), F32),
        pltpu.VMEM((16, 8, 1024), F32),
        pltpu.VMEM((16, 8, 19 * 128), F32),
        blocks(4),
        blocks(4, 2),
        blocks(2),
        blocks(4, 2),
        blocks(2),
        blocks(2, 2),
        block,
        block,
        blocks(n_layers - 1),
        blocks(n_plane),
        block,
        dma,
        dma((2,)), dma((2,)), dma((4,)), dma((4,)), dma((4,)), dma((4,)),
        dma((4,)), dma((4,)), dma((4,)), dma((4,)), dma((2,)), dma((2,)),
        dma, dma, dma, dma((n_layers - 1,)), dma((n_plane,)), dma((n_plane,)), dma((CORES * n_layers,)), dma,
    ]
    vmem = pl.BlockSpec(memory_space=pltpu.VMEM)
    return pl.pallas_call(
        kernel,
        out_shape=jax.ShapeDtypeStruct((48, 128), F32),
        in_specs=[vmem, pl.BlockSpec(memory_space=pl.ANY)] + [vmem] * 6,
        out_specs=vmem,
        scratch_shapes=scratch,
        compiler_params=pltpu.CompilerParams(
            collective_id=0, has_side_effects=True, vmem_limit_bytes=40 * 1024 * 1024
        ),
    )


def make_finish(factor):
    def kernel(packed, edge_out, node_in, biases, grad_coarse, g_edge_in, g_edge_out, g_node_in, g_node_out, g_biases):
        for q in (0, 1):
            block = packed[16 * q : 16 * q + 16, :]
            for p in (0, 1):
                grad_coarse[:, p, q, :] = block[:, 32 * p : 32 * p + 32]
        total = packed[32:48, :] * factor
        g_node_out[...] = total[:, 0:16]
        g_edge_in[...] = total[:, 48:83]
        n_gathered = node_in[:, 16:32]
        eye = ones_where(iota((16, 16), 0) == iota((16, 16), 1)).astype(BF16)
        n_back = exact_mm(eye, split(n_gathered), NT)
        back = mm(split(n_back), split(total))
        g_edge_out[...] = back[:, 16:32]
        outer_in = total[:, 16:32]
        g_node_in[:, 0:16] = total[:, 32:48]
        g_node_in[:, 16:32] = mm(split(outer_in), split(edge_out[...]), NT) + total[:, 85:86] * biases[1:2, :]
        rows = jnp.concatenate([total, back], axis=1)
        r, c = iota((8, 256), 0), iota((8, 256), 1)
        pick = ones_where(((r == 0) & (c == 83)) | ((r == 1) & (c == 128 + 85)) | ((r == 2) & (c == 84))).astype(BF16)
        g_biases[...] = exact_mm(pick, split(rows), NT)[0:3, :]

    vmem = pl.BlockSpec(memory_space=pltpu.VMEM)
    shapes = ((16, 2, 2, 32), (16, 35), (16, 16), (16, 32), (16, 16), (3, 16))
    return pl.pallas_call(
        kernel,
        out_shape=[jax.ShapeDtypeStruct(s, F32) for s in shapes],
        in_specs=[vmem] * 4,
        out_specs=[vmem] * 6,
    )


def solution(mesh):
    sizes = (mesh.shape["gx"], mesh.shape["gy"], mesh.shape["gz"])
    table = make_table()

    def on_device(coarse, cotangent, edge_in, edge_out, node_in, node_out, biases):
        nodes = cotangent.shape[1] * cotangent.shape[2] * cotangent.shape[3] * sizes[0] * sizes[1] * sizes[2]
        packed = make_main(sizes)(
            coarse, cotangent, edge_in, edge_out, node_in, node_out, biases, jnp.asarray(table)
        )
        return tuple(make_finish(float(nodes) ** -0.5)(packed, edge_out, node_in, biases))

    placed = (P(None, "gx", "gy", "gz"), P(None, "gx", "gy", "gz"), P(), P(), P(), P(), P())
    return jax.shard_map(
        on_device,
        mesh=mesh,
        in_specs=placed,
        out_specs=(P(None, "gx", "gy", "gz"), P(), P(), P(), P(), P()),
        check_vma=False,
    )
```

```python
import jax
import jax.numpy as jnp
import numpy as np
from jax import lax
from jax.experimental import pallas as pl
from jax.experimental.pallas import tpu as pltpu
from jax.sharding import PartitionSpec as P

MESH = pl.DeviceIdType.MESH
F32 = jnp.float32
BF16 = jnp.bfloat16
T = np.array(
    [
        -1.0,
        -0.8717401485096066,
        -0.5917001814331423,
        -0.2092992179024789,
        0.2092992179024789,
        0.5917001814331423,
        0.8717401485096066,
        1.0,
    ]
)
L0, L1 = (1.0 - T) / 2.0, (1.0 + T) / 2.0
LOG2E = float(np.log2(np.e))
LN2 = float(np.log(2.0))
GAP_UP = [float(T[i + 1] - T[i]) if i < 7 else float(T[1] - T[0]) for i in range(8)]
GAP_DOWN = [float(T[i - 1] - T[i]) if i > 0 else float(T[6] - T[7]) for i in range(8)]
Z_LOW = 4
CORES = 2
ABSENT = -1.0e5
SLOT = {0: 0, 1: 1, -1: 2, 2: 3}
STEPS = (-2, -1, 1, 2)

RZ, RZ_UP, RZ_DOWN, PROFILES, Y_STD, Y_NEXT, Y_GAP, DELTA = 0, 32, 64, 96, 136, 168, 296, 328
TABLE_ROWS = 376


def make_table():
    table = np.zeros((TABLE_ROWS, 128))
    for lane in range(128):
        e, a = divmod(lane, 8)
        table[RZ + e + 1, lane] += L0[a]
        table[RZ + e + 2, lane] += L1[a]
        if a < 7:
            table[RZ_UP + e + 1, lane] += L0[a + 1]
            table[RZ_UP + e + 2, lane] += L1[a + 1]
        else:
            table[RZ_UP + e + 2, lane] += L0[1]
            table[RZ_UP + e + 3, lane] += L1[1]
        if a > 0:
            table[RZ_DOWN + e + 1, lane] += L0[a - 1]
            table[RZ_DOWN + e + 2, lane] += L1[a - 1]
        else:
            table[RZ_DOWN + e, lane] += L0[6]
            table[RZ_DOWN + e + 1, lane] += L1[6]
        table[RZ_UP + 20, lane] = GAP_UP[a]
        table[RZ_DOWN + 20, lane] = GAP_DOWN[a]
    up = np.zeros((4, 8))
    down = np.zeros((4, 8))
    for y in range(8):
        if y < 7:
            up[1, y], up[2, y] = L0[y + 1], L1[y + 1]
        else:
            up[2, y], up[3, y] = L0[1], L1[1]
        if y > 0:
            down[1, y], down[2, y] = L0[y - 1], L1[y - 1]
        else:
            down[0, y], down[1, y] = L0[6], L1[6]
    for i, profile in enumerate((L1, up[2], up[3], down[2], down[0])):
        table[PROFILES + 8 * i : PROFILES + 8 * i + 8] = profile[:, None]
    for c in range(16):
        for y in range(8):
            lane = 8 * c + y
            table[Y_STD + c, lane] = L0[y]
            table[Y_STD + 16 + c, lane] = L1[y]
            for q in range(4):
                table[Y_NEXT + 16 * q + c, lane] = up[q, y]
                table[Y_NEXT + 64 + 16 * q + c, lane] = down[q, y]
            table[Y_GAP + c, lane] = GAP_UP[y]
            table[Y_GAP + 16 + c, lane] = GAP_DOWN[y]
            table[DELTA + c, lane] = 1.0
            table[DELTA + 16 + c, lane] = 1.0 if y == 0 else 0.0
            table[DELTA + 32 + c, lane] = 1.0 if y == 7 else 0.0
    return table.astype(np.float32)


NN = (((1,), (0,)), ((), ()))
NT = (((1,), (1,)), ((), ()))


def dot(a, b, dims=NN):
    return lax.dot_general(a, b, dims, preferred_element_type=F32)


def split(a):
    high = a.astype(BF16)
    return high, (a - high.astype(F32)).astype(BF16)


def mm(a, b, dims=NN):
    (ah, al), (bh, bl) = a, b
    return dot(ah, bh, dims) + (dot(ah, bl, dims) + dot(al, bh, dims))


def mm_exact(a, b, dims=NN):
    return dot(a[0], b, dims) + dot(a[1], b, dims)


def exact_mm(a, b, dims=NN):
    return dot(a, b[0], dims) + dot(a, b[1], dims)


def iota(shape, dim):
    return lax.broadcasted_iota(jnp.int32, shape, dim)


def ones_where(mask):
    return jnp.where(mask, 1.0, 0.0).astype(F32)


def spread(a, k):
    k = k % 4
    return a if k == 0 else pltpu.roll(a, 32 * k, 1)


def vertex_maps():
    row, col = iota((128, 128), 0), iota((128, 128), 1)
    layer, vertex = row % 32, col % 32 - 1
    same = (row // 32 == col // 32) & (vertex < 18)
    maps = []
    for shift in (0, 16, -16):
        v = vertex + shift
        maps.append(ones_where(same & ((layer == 2 * v - 1) | (layer == 2 * v))).astype(BF16))
    return maps


def make_main(sizes):
    n_x, n_y, n_z = sizes
    z_high = n_y // CORES
    n_layers = z_high * Z_LOW
    n_cols = n_x // Z_LOW
    n_plane = n_cols * n_z

    def kernel(
        coarse_in, cot_in, edge_in_in, edge_out_in, node_in_in, node_out_in, biases_in, table_in,
        out,
        coarse, cot, edge_in, edge_out, node_in, node_out, biases, table, p0, zr, tb, xr, vx, yr, means, lhs_rows, rows, e_all, e_sum, s_all, hn_all, u_all, g_all, xf,
        gm, yb, gy_all, xb, gx_all, zb, payload, core_slot, col_slots, plane_slots, total,
        load_sem, zf_s, zf_r, xf_s, xf_r, yf_s, yf_r, yb_s, yb_r, xb_s, xb_r, zb_s, zb_r,
        core_s, core_r, col_s, col_r, plane_s, plane_r, cast_s, cast_r,
    ):
        ix, iy, iz = lax.axis_index("gx"), lax.axis_index("gy"), lax.axis_index("gz")
        low = lax.rem(ix, Z_LOW)
        core = lax.rem(iy, CORES)
        layer = (iy // CORES) * Z_LOW + low
        on_core1 = core == 1
        is_root = on_core1 & (layer == 0)
        is_leaf = on_core1 & (layer != 0)

        def at_x(d):
            return (lax.rem(ix + (d + n_x), n_x), iy, iz)

        def at_y(d):
            return (ix, lax.rem(iy + (d + n_y), n_y), iz)

        def at_z(d):
            return (ix, iy, lax.rem(iz + (d + n_z), n_z))

        sibling = (ix, iy + 1 - 2 * core, iz)
        column_root = (ix - low, 1, iz)

        def in_column(k, c):
            return (ix + k % Z_LOW, (k // Z_LOW) * CORES + c, iz)

        def in_plane(k):
            col, row = k // n_z, k % n_z
            return (lax.rem(ix + Z_LOW * col, n_x), iy, lax.rem(iz + row, n_z))

        def send(src, dst, send_sem, recv_sem, device):
            return pltpu.make_async_remote_copy(
                src_ref=src, dst_ref=dst, send_sem=send_sem, recv_sem=recv_sem, device_id=device, device_id_type=MESH
            )

        def signal(device):
            pl.semaphore_signal(barrier, inc=1, device_id=device, device_id_type=MESH)

        loads = [
            pltpu.make_async_copy(src, dst, load_sem.at[i])
            for i, (src, dst) in enumerate(
                (
                    (coarse_in, coarse),
                    (edge_in_in, edge_in),
                    (edge_out_in, edge_out),
                    (node_in_in, node_in),
                    (node_out_in, node_out),
                    (biases_in, biases),
                    (table_in, table),
                    (cot_in, cot),
                )
            )
        ]
        loads[0].start()
        barrier = pltpu.get_barrier_semaphore()
        for d in (-1, 1):
            signal(at_z(d))
        for d in STEPS:
            signal(at_x(d))
        for d in STEPS:
            signal(at_y(d))

        @pl.when(is_root)
        def _():
            for k in range(1, n_layers):
                signal(in_column(k, 1))
            for k in range(1, n_plane):
                signal(in_plane(k))

        for c in loads[1:]:
            c.start()
        expected = 10 + jnp.where(is_leaf, 1, 0) + jnp.where(is_root, n_plane - 1, 0)

        loads[0].wait()
        block = coarse[...]
        p0[...] = jnp.concatenate([block[:, p, q, :] for q in (0, 1) for p in (0, 1)], axis=1)
        pl.semaphore_wait(barrier, expected)

        z_sends = [
            send(p0, zr.at[0], zf_s.at[0], zf_r.at[0], at_z(1)),
            send(p0, zr.at[1], zf_s.at[1], zf_r.at[1], at_z(-1)),
        ]
        for c in z_sends:
            c.start()

        for c in loads[1:7]:
            c.wait()
        w_own, w_other = edge_in[:, 0:16], edge_in[:, 16:32]
        col_x, col_y, col_z = edge_in[:, 32:33], edge_in[:, 33:34], edge_in[:, 34:35]
        n_own, n_gathered = node_in[:, 0:16], node_in[:, 16:32]
        eye = ones_where(iota((16, 16), 0) == iota((16, 16), 1)).astype(BF16)
        delta = table[DELTA : DELTA + 16, :].astype(BF16)
        same_y = iota((128, 128), 0) % 8 == iota((128, 128), 1) % 8

        def transposed(w):
            return exact_mm(eye, split(w), NT)

        def widen(w):
            parts = []
            for part in split(w):
                left = dot(delta, part, (((0,), (0,)), ((), ()))).astype(BF16)
                parts.append(jnp.where(same_y, dot(left, delta), 0.0).astype(BF16))
            return tuple(parts)

        m1 = mm(split(n_gathered), split(edge_out[...]))
        m1_wide = widen(m1)
        m1_back = widen(transposed(m1))
        out_back = widen(transposed(node_out[...]))
        mix = split(jnp.concatenate([w_own, n_own, w_other], axis=0))
        mix_back = split(jnp.concatenate([transposed(n_own), transposed(w_own), transposed(w_other)], axis=1))
        bias_rows = biases[...]
        bias_cols = exact_mm(eye, split(bias_rows), NT)
        b0_col, b1_row, b2_col = bias_cols[:, 0:1], bias_rows[1:2, :], bias_cols[:, 2:3]
        nb_col = jnp.sum(n_gathered * b1_row, axis=1, keepdims=True)
        maps = vertex_maps()
        lane = iota((16, 128), 1)
        group, place = lane // 32, lane % 32
        gap_lane = ones_where((place == 20) & (group < 2))

        def blocks4(first):
            t = table[first : first + 32, :]
            zero = jnp.zeros((32, 128), F32)
            return split(
                jnp.concatenate(
                    [jnp.concatenate([t if i == j else zero for j in range(4)], axis=1) for i in range(4)], axis=0
                )
            )

        rz, rz_up, rz_down = blocks4(RZ), blocks4(RZ_UP), blocks4(RZ_DOWN)

        z_sends[0].wait_recv()
        z_sends[1].wait_recv()
        tb[...] = (
            mm_exact(split(p0[...]), maps[0])
            + mm_exact(split(zr[0]), maps[1])
            + mm_exact(split(zr[1]), maps[2])
        )
        x_sends = []
        for d in STEPS:
            i = STEPS.index(-d)
            x_sends.append(send(tb, xr.at[i], xf_s.at[i], xf_r.at[i], at_x(d)))
        for c in x_sends:
            c.start()

        loads[7].wait()
        for k in range(4):
            wide = jnp.concatenate([cot[:, 2 * k + i].reshape(128, 128) for i in (0, 1)], axis=1)
            u_all[:, :, 256 * k : 256 * k + 256] = mm(out_back, split(wide)).reshape(16, 8, 256)
        sum_all, sum_one = cot[:, 0], jnp.zeros((16, 8, 128), F32)
        for x in range(1, 8):
            sum_all = sum_all + cot[:, x]
            sum_one = sum_one + float(L1[x]) * cot[:, x]
        xf[:, :, 0:128] = sum_all - sum_one
        xf[:, :, 128:256] = sum_one

        for c in x_sends:
            c.wait_recv()
        x_blocks = {0: tb[...]}
        for i, d in enumerate(STEPS):
            x_blocks[d] = xr[i]
        for q in (0, 1):
            acc = jnp.zeros((16, 128), F32)
            for vertex in (-1, 0, 1, 2):
                for d in (vertex - 1, vertex):
                    moved = spread(x_blocks[d], SLOT[vertex] - (2 * q + vertex - d))
                    acc = acc + jnp.where(group == SLOT[vertex], moved, 0.0)
            vx[q] = acc
        y_sends = []
        for d in STEPS:
            i = STEPS.index(-d)
            qs = pl.ds(0, 2) if abs(d) == 1 else pl.ds(1 if d == 2 else 0, 1)
            y_sends.append(send(vx.at[qs], yr.at[i, qs], yf_s.at[i], yf_r.at[i], at_y(d)))
        for c in y_sends:
            c.start()

        def exists(d):
            return jnp.where((iy + d >= 0) & (iy + d < n_y), 1.0, 0.0).astype(F32)

        there = {d: exists(d) for d in (-2, -1, 0, 1, 2)}
        wall_low, wall_high = 1.0 - there[-1], 1.0 - there[1]
        y_index = iota((8, 128), 0)
        count = 6.0 - wall_low * ones_where(y_index == 0) - wall_high * ones_where(y_index == 7)
        ly, up1, up2, down1, down0 = (table[PROFILES + 8 * i : PROFILES + 8 * i + 8, :] for i in range(5))

        for c in y_sends:
            c.wait_recv()

        def y_block(d, q):
            return vx[q] if d == 0 else yr[STEPS.index(d), q] * there[d]

        for q in (-1, 0, 1, 2):
            copies = jnp.maximum(there[q - 1] + there[q], 1.0)
            means[q + 1] = (y_block(q - 1, 1) + y_block(q, 0)) * (0.25 / copies)

        mixed = mm(mix, split(jnp.concatenate([means[i] for i in range(4)], axis=1)))
        for i in range(4):
            lanes = slice(128 * i, 128 * i + 128)
            if i in (1, 2):
                lhs_rows[48 * (i - 1) : 48 * (i - 1) + 32, :] = mixed[0:32, lanes]
                lhs_rows[48 * (i - 1) + 32 : 48 * i, :] = mixed[32:48, lanes] + col_z * gap_lane
            else:
                first = 96 if i == 0 else 112
                lhs_rows[first : first + 16, :] = mixed[32:48, lanes]
        along = mm(split(lhs_rows[...]), rz)
        other01 = split(jnp.concatenate([lhs_rows[32:48, :], lhs_rows[80:96, :]], axis=0))
        along_up = mm(other01, (rz_up[0][:, 0:256], rz_up[1][:, 0:256]))
        along_down = mm(other01, (rz_down[0][:, 0:256], rz_down[1][:, 0:256]))

        def vertex_rows(field, q, vertex):
            first = {0: 0, 1: 48}[q] + 16 * field if q in (0, 1) else (96 if q == -1 else 112)
            s = SLOT[vertex]
            return along[first : first + 16, 128 * s : 128 * s + 128]

        def next_rows(source, q, vertex):
            return source[16 * q : 16 * q + 16, 128 * vertex : 128 * vertex + 128]

        def put(field, x, value):
            rows[pl.ds(128 * field + x, 16, stride=8), :] = value

        def line(a, b, t):
            return a + t * (b - a)

        for x in range(8):
            t = float(L1[x])
            here = float(T[x]) * col_x
            own = [
                (line(vertex_rows(0, q, 0), vertex_rows(0, q, 1), t) + (b0_col - here - (2 * q - 1.0) * col_y)) * LOG2E
                for q in (0, 1)
            ]
            put(0, x, own[0])
            put(1, x, own[1] - own[0])
            other = {
                q: (line(vertex_rows(2, q, 0), vertex_rows(2, q, 1), t) + (here + (2 * q - 1.0) * col_y)) * LOG2E
                for q in (-1, 0, 1, 2)
            }
            put(2, x, other[0])
            put(3, x, other[1] - other[0])
            put(5, x, (other[2] - other[0]) * there[1] + ABSENT * wall_high)
            put(6, x, (other[-1] - other[0]) * there[-1] + ABSENT * wall_low)
            for f, source in ((7, along_up), (9, along_down)):
                z = [
                    (line(next_rows(source, q, 0), next_rows(source, q, 1), t) + (here + (2 * q - 1.0) * col_y)) * LOG2E
                    for q in (0, 1)
                ]
                put(f, x, z[0])
                put(f + 1, x, z[1] - z[0])
            hn = [line(vertex_rows(1, q, 0), vertex_rows(1, q, 1), t) for q in (0, 1)]
            put(11, x, hn[0] + b2_col)
            put(12, x, hn[1] - hn[0])
            put(13, x, jnp.broadcast_to(nb_col, (16, 128)))
        for side, (a, b, t, at) in enumerate(((-1, 0, float(L1[6]), float(T[6]) - 2.0), (1, 2, float(L1[1]), float(T[1]) + 2.0))):
            other = [
                (line(vertex_rows(2, q, a), vertex_rows(2, q, b), t) + (at * col_x + (2 * q - 1.0) * col_y)) * LOG2E
                for q in (0, 1)
            ]
            put(4, 2 * side, other[0])
            put(4, 2 * side + 1, other[1] - other[0])

        def forward(c, carry):
            def row(field, x):
                return rows[pl.ds(128 * field + 8 * c + x, 1), :]

            other = [row(4, 0) + ly * row(4, 1)]
            for x in range(8):
                other.append(row(2, x) + ly * row(3, x))
            other.append(row(4, 2) + ly * row(4, 3))
            for x in range(8):
                own = row(0, x) + ly * row(1, x)
                a, d = row(2, x), row(3, x)
                senders = (
                    other[x + 2],
                    other[x],
                    a + up1 * d + up2 * row(5, x),
                    a + down1 * d + down0 * row(6, x),
                    row(7, x) + ly * row(8, x),
                    row(9, x) + ly * row(10, x),
                )
                tops, decays = None, None
                for k, sender in enumerate(senders):
                    z = own + sender
                    decay = jnp.exp2(jnp.minimum(z, 0.0))
                    top = jnp.maximum(z, 0.0)
                    e_all[k, x, c] = decay
                    tops = top if tops is None else tops + top
                    decays = decay if decays is None else decays + decay
                e_sum[x, c] = decays
                s_all[c, :, 128 * x : 128 * x + 128] = LN2 * tops + (decays - count)
                hn_all[c, :, 128 * x : 128 * x + 128] = row(11, x) + ly * row(12, x) + count * row(13, x)
            return carry

        lax.fori_loop(0, 16, forward, 0)

        outer_out = jnp.zeros((128, 128), F32)
        outer_in = jnp.zeros((128, 128), F32)
        dh_all = jnp.zeros((16, 8, 128), F32)
        dh_one = jnp.zeros((16, 8, 128), F32)
        for k in range(4):
            lanes = slice(256 * k, 256 * k + 256)
            s = split(s_all[:, :, lanes].reshape(128, 256))
            h = mm(m1_wide, s) + hn_all[:, :, lanes].reshape(128, 256)
            decay = jnp.exp(jnp.minimum(h, 0.0))
            a = jnp.maximum(h, 0.0) + (decay - 1.0)
            dh = decay * u_all[:, :, lanes].reshape(128, 256)
            dh_parts = split(dh)
            g_all[:, :, lanes] = mm(m1_back, dh_parts).reshape(16, 8, 256)
            wide = jnp.concatenate([cot[:, 2 * k + i].reshape(128, 128) for i in (0, 1)], axis=1)
            outer_out = outer_out + mm(split(wide), split(a), NT)
            outer_in = outer_in + mm(dh_parts, s, NT)
            for i in (0, 1):
                part = dh[:, 128 * i : 128 * i + 128].reshape(16, 8, 128)
                dh_all = dh_all + part
                dh_one = dh_one + float(L1[2 * k + i]) * part
        xf[:, :, 256:384] = dh_all - dh_one
        xf[:, :, 384:512] = dh_one

        def backward(c, carry):
            g = [g_all[c, :, 128 * x : 128 * x + 128] for x in range(8)]
            own = [g[x] * e_sum[x, c] for x in range(8)]

            def bz(k, x):
                return g[x] * e_all[k, x, c]

            def save(i, value):
                xf[c, :, 128 * i : 128 * i + 128] = value

            def reduce(first, values):
                everything, one = values[0], float(L1[1]) * values[1]
                for x in range(1, 8):
                    everything = everything + values[x]
                for x in range(2, 8):
                    one = one + float(L1[x]) * values[x]
                save(first, everything - one)
                save(first + 1, one)

            reduce(4, own)
            ups = [bz(0, x) for x in range(8)]
            downs = [bz(1, x) for x in range(8)]
            acc = GAP_UP[0] * ups[0] + GAP_DOWN[0] * downs[0]
            for x in range(1, 8):
                acc = acc + GAP_UP[x] * ups[x] + GAP_DOWN[x] * downs[x]
            save(6, acc)
            at = [downs[1]] + [ups[x - 1] + downs[x + 1] for x in range(1, 7)] + [ups[6]]
            everything, one = at[0], float(L1[1]) * at[1]
            for x in range(1, 8):
                everything = everything + at[x]
            for x in range(2, 8):
                one = one + float(L1[x]) * at[x]
            save(7, everything - one + float(L1[6]) * downs[0])
            save(8, one + float(L0[1]) * ups[7])
            save(9, float(L0[6]) * downs[0])
            save(10, float(L1[1]) * ups[7])
            for k in range(4):
                reduce(11 + 2 * k, [bz(2 + k, x) for x in range(8)])
            return carry

        lax.fori_loop(0, 16, backward, 0)

        def along_z(first, n, by):
            return mm(
                split(xf[:, :, 128 * first : 128 * (first + n)].reshape(128, 128 * n)),
                (by[0][:, 0 : 128 * n], by[1][:, 0 : 128 * n]),
                NT,
            )

        z1 = along_z(0, 4, rz)
        z2 = along_z(4, 3, rz)
        z3 = along_z(7, 4, rz) + along_z(15, 2, rz_up) + along_z(17, 2, rz_down)
        z4 = along_z(11, 4, rz)
        counting = (
            6.0 * table[DELTA : DELTA + 16, :]
            - wall_low * table[DELTA + 16 : DELTA + 32, :]
            - wall_high * table[DELTA + 32 : DELTA + 48, :]
        )
        left = split(jnp.concatenate([table[Y_STD : Y_STD + 32, :], counting], axis=0))
        std = mm(left, split(jnp.concatenate([z1, z2, z3], axis=1)))
        nxt = mm(split(table[Y_NEXT : Y_NEXT + 160, :]), split(z4))

        low_half, low_lanes = group < 2, ones_where(group < 2)
        fields = {}
        for q in (0, 1):
            r = slice(16 * q, 16 * q + 16)
            fields[q] = (std[r, 0:128], std[r, 128:256], std[r, 256:384])
        others = {}
        for q in (-1, 0, 1, 2):
            r_up = slice(16 * (q + 1), 16 * (q + 1) + 16)
            r_down = slice(64 + 16 * (q + 1), 64 + 16 * (q + 1) + 16)
            both = jnp.where(low_half, nxt[r_up, :] + pltpu.roll(nxt[r_down, :], 64, 1), 0.0)
            others[q] = both + fields[q][2] if q in (0, 1) else both

        summed_out = jnp.where(same_y, outer_out, 0.0)
        summed_in = jnp.where(same_y, outer_in, 0.0)
        big = exact_mm(delta, split(jnp.concatenate([summed_out, summed_in], axis=1)))
        r2, c2 = iota((128, 256), 0), iota((128, 256), 1)
        placing = ones_where((c2 // 128 * 16 + c2 % 128 // 8) == r2).astype(BF16)
        part = mm_exact(split(big), placing, NT)
        r8, l8 = iota((8, 128), 0), iota((8, 128), 1)

        def marked(r, mask):
            return ones_where((r8 == r) & mask)

        def right(first, rows16, special):
            pieces = []
            if rows16 is None:
                pieces.append(jnp.zeros((80, 128), F32))
            else:
                if first > 0:
                    pieces.append(jnp.zeros((first, 128), F32))
                pieces.append(rows16)
                if first < 64:
                    pieces.append(jnp.zeros((64 - first, 128), F32))
            pieces += [special, jnp.zeros((40, 128), F32)]
            return jnp.concatenate(pieces, axis=0)

        lefts, rights = [], []
        none8 = jnp.zeros((8, 128), F32)
        for q in (-1, 0, 1, 2):
            m = means[q + 1]
            if q in (0, 1):
                lefts.append(fields[q][0])
                rights.append(right(32, jnp.where(low_half, 0.0, pltpu.roll(m, 64, 1)), marked(4, l8 >= 64)))
                lefts.append(fields[q][1])
                rights.append(right(48, m * low_lanes, marked(3, l8 < 64) + marked(0, (l8 >= 64) & (l8 < 96))))
            lefts.append(others[q])
            rights.append(right(64, m, marked(2, (l8 % 32 == 20) & (l8 < 64)) if q in (0, 1) else none8))
        lefts += [std[32:48, 0:128], nxt[128:144, :], nxt[144:160, :]]
        rights += [
            right(0, None, marked(5, l8 >= 64)),
            right(0, None, marked(1, l8 < 64)),
            right(0, None, marked(1, l8 >= 64)),
        ]
        payload[...] = part + mm(split(jnp.concatenate(lefts, axis=1)), split(jnp.concatenate(rights, axis=1)), NT)

        to_second = send(payload, core_slot, core_s, core_r, sibling)
        to_first = send(total, total, cast_s.at[0], cast_r, sibling)
        slot = jnp.maximum(layer - 1, 0)
        to_root = send(payload, col_slots.at[slot], col_s, col_r.at[slot], column_root)

        @pl.when(core == 0)
        def _():
            to_second.start()

        zero = jnp.zeros((16, 128), F32)
        stacked = []
        for q in (-1, 0, 1, 2):
            if q in (0, 1):
                dh_q = jnp.where(low_half, pltpu.roll(fields[q][0], 64, 1), 0.0)
                own_q = jnp.where(low_half, fields[q][1], 0.0)
            else:
                dh_q, own_q = zero, zero
            stacked.append(jnp.concatenate([dh_q, own_q, others[q]], axis=0))
        back = mm(mix_back, split(jnp.concatenate(stacked, axis=1)))
        for q in (-1, 0, 1, 2):
            value = back[:, 128 * (q + 1) : 128 * (q + 2)]
            if q in (0, 1):
                value = value + jnp.where(low_half, fields[q][0], 0.0)
            gm[q + 1] = value
        y_back = []
        for d in STEPS:
            i = STEPS.index(-d)
            if abs(d) == 1:
                src, dst = gm.at[pl.ds(2 if d == 1 else 0, 2)], yb.at[i]
            else:
                src, dst = gm.at[pl.ds(3 if d == 2 else 0, 1)], yb.at[i, pl.ds(0 if d == 2 else 1, 1)]
            y_back.append(send(src, dst, yb_s.at[i], yb_r.at[i], at_y(d)))
        for c in y_back:
            c.start()

        @pl.when(on_core1)
        def _():
            to_second.wait_recv()
            payload[...] = payload[...] + core_slot[...]

        @pl.when(is_leaf)
        def _():
            to_root.start()

        for c in y_back:
            c.wait_recv()
        for q in (0, 1):
            value = gm[q + 1]
            for d in (-2, -1, 1, 2):
                if (d, q) not in ((-2, 1), (2, 0)):
                    value = value + yb[STEPS.index(d), q] * there[d]
            gy_all[q] = value
        x_back = []
        for d in STEPS:
            i = STEPS.index(-d)
            x_back.append(send(gy_all, xb.at[i], xb_s.at[i], xb_r.at[i], at_x(d)))
        for c in x_back:
            c.start()

        my_place = (ix // Z_LOW) * n_z + iz
        to_plane = [
            send(plane_slots.at[my_place], plane_slots.at[my_place], plane_s.at[k], plane_r.at[k], in_plane(k))
            for k in range(1, n_plane)
        ]

        @pl.when(is_root)
        def _():
            value = payload[...]
            for k in range(n_layers - 1):
                send(payload, col_slots.at[k], col_s, col_r.at[k], in_column(k + 1, 1)).wait_recv()
                value = value + col_slots[k]
            plane_slots[my_place] = value
            for c in to_plane:
                c.start()

        for c in x_back:
            c.wait_recv()
        for q in (0, 1):
            value = gy_all[q]
            for d in (-2, -1, 1, 2):
                for p in (0, 1):
                    vertex = p - d
                    if vertex in SLOT:
                        moved = spread(xb[STEPS.index(d), q], p - SLOT[vertex])
                        value = value + jnp.where(group == p, moved, 0.0)
            gx_all[q] = jnp.where(low_half, value, 0.0)
        z_back = [
            send(gx_all, zb.at[0], zb_s.at[0], zb_r.at[0], at_z(1)),
            send(gx_all, zb.at[1], zb_s.at[1], zb_r.at[1], at_z(-1)),
        ]
        for c in z_back:
            c.start()

        up_column = [send(total, total, cast_s.at[k], cast_r, in_column(k, 1)) for k in range(1, n_layers)]

        @pl.when(is_root)
        def _():
            for k, c in enumerate(to_plane):
                c.wait_recv()
            value = plane_slots[0]
            for k in range(1, n_plane):
                value = value + plane_slots[k]
            total[...] = value
            for c in [to_first] + up_column:
                c.start()

        for c in z_back:
            c.wait_recv()
        for q in (0, 1):
            value = (
                mm_exact(split(gx_all[q]), maps[0], NT)
                + mm_exact(split(zb[0, q]), maps[2], NT)
                + mm_exact(split(zb[1, q]), maps[1], NT)
            )
            neighbour = there[-1] if q == 0 else there[1]
            out[16 * q : 16 * q + 16, :] = value * (0.25 / (1.0 + neighbour))

        @pl.when(jnp.logical_not(is_root))
        def _():
            to_first.wait_recv()

        @pl.when(is_leaf)
        def _():
            to_first.start()

        out[32:48, :] = total[...]
        out[48:64, 0:32] = node_in[...]
        out[48:64, 32:48] = edge_out[...]
        out[64:67, 0:16] = biases[...]

        for c in z_sends + x_sends + y_sends + y_back + x_back + z_back:
            c.wait_send()

        @pl.when(core == 0)
        def _():
            to_second.wait_send()

        @pl.when(on_core1)
        def _():
            to_first.wait_send()

        @pl.when(is_leaf)
        def _():
            to_root.wait_send()

        @pl.when(is_root)
        def _():
            for c in to_plane + up_column:
                c.wait_send()

    block = pltpu.VMEM((16, 128), F32)

    def blocks(*lead):
        return pltpu.VMEM(lead + (16, 128), F32)

    dma = pltpu.SemaphoreType.DMA
    scratch = [
        pltpu.VMEM((16, 2, 2, 32), F32),
        pltpu.VMEM((16, 8, 8, 128), F32),
        pltpu.VMEM((16, 35), F32),
        pltpu.VMEM((16, 16), F32),
        pltpu.VMEM((16, 32), F32),
        pltpu.VMEM((16, 16), F32),
        pltpu.VMEM((3, 16), F32),
        pltpu.VMEM((TABLE_ROWS, 128), F32),
        block,
        blocks(2),
        block,
        blocks(4),
        blocks(2),
        blocks(4, 2),
        blocks(4),
        pltpu.VMEM((128, 128), F32),
        pltpu.VMEM((14 * 128, 128), F32),
        pltpu.VMEM((6, 8, 16, 8, 128), F32),
        pltpu.VMEM((8, 16, 8, 128), F32),
        pltpu.VMEM((16, 8, 1024), F32),
        pltpu.VMEM((16, 8, 1024), F32),
        pltpu.VMEM((16, 8, 1024), F32),
        pltpu.VMEM((16, 8, 1024), F32),
        pltpu.VMEM((16, 8, 19 * 128), F32),
        blocks(4),
        blocks(4, 2),
        blocks(2),
        blocks(4, 2),
        blocks(2),
        blocks(2, 2),
        block,
        block,
        blocks(n_layers - 1),
        blocks(n_plane),
        block,
        dma((8,)),
        dma((2,)), dma((2,)), dma((4,)), dma((4,)), dma((4,)), dma((4,)),
        dma((4,)), dma((4,)), dma((4,)), dma((4,)), dma((2,)), dma((2,)),
        dma, dma, dma, dma((n_layers - 1,)), dma((n_plane,)), dma((n_plane,)), dma((n_layers,)), dma,
    ]
    vmem = pl.BlockSpec(memory_space=pltpu.VMEM)
    return pl.pallas_call(
        kernel,
        out_shape=jax.ShapeDtypeStruct((72, 128), F32),
        in_specs=[pl.BlockSpec(memory_space=pltpu.HBM)] * 8,
        out_specs=vmem,
        scratch_shapes=scratch,
        compiler_params=pltpu.CompilerParams(
            collective_id=0, has_side_effects=True, vmem_limit_bytes=60 * 1024 * 1024
        ),
    )


def make_finish(factor):
    shapes = ((16, 2, 2, 32), (16, 35), (16, 16), (16, 32), (16, 16), (3, 16))

    def kernel(packed, *refs):
        outs, buffers, sem = refs[:6], refs[6:12], refs[12]
        grad_coarse, g_edge_in, g_edge_out, g_node_in, g_node_out, g_biases = buffers
        copies = [pltpu.make_async_copy(src, dst, sem.at[i]) for i, (src, dst) in enumerate(zip(buffers, outs))]
        for q in (0, 1):
            block = packed[16 * q : 16 * q + 16, :]
            for p in (0, 1):
                grad_coarse[:, p, q, :] = block[:, 32 * p : 32 * p + 32]
        copies[0].start()
        total = packed[32:48, :] * factor
        g_node_out[...] = total[:, 0:16]
        copies[4].start()
        g_edge_in[...] = total[:, 48:83]
        copies[1].start()
        n_gathered, edge_out, b1_row = packed[48:64, 16:32], packed[48:64, 32:48], packed[65:66, 0:16]
        eye = ones_where(iota((16, 16), 0) == iota((16, 16), 1)).astype(BF16)
        n_back = exact_mm(eye, split(n_gathered), NT)
        back = mm(split(n_back), split(total))
        g_edge_out[...] = back[:, 16:32]
        copies[2].start()
        outer_in = total[:, 16:32]
        g_node_in[:, 0:16] = total[:, 32:48]
        g_node_in[:, 16:32] = mm(split(outer_in), split(edge_out), NT) + total[:, 85:86] * b1_row
        copies[3].start()
        rows = jnp.concatenate([total, back], axis=1)
        r, c = iota((8, 256), 0), iota((8, 256), 1)
        pick = ones_where(((r == 0) & (c == 83)) | ((r == 1) & (c == 128 + 85)) | ((r == 2) & (c == 84))).astype(BF16)
        g_biases[...] = exact_mm(pick, split(rows), NT)[0:3, :]
        copies[5].start()
        for c in copies:
            c.wait()

    return pl.pallas_call(
        kernel,
        out_shape=[jax.ShapeDtypeStruct(s, F32) for s in shapes],
        in_specs=[pl.BlockSpec(memory_space=pltpu.VMEM)],
        out_specs=[pl.BlockSpec(memory_space=pltpu.HBM)] * 6,
        scratch_shapes=[pltpu.VMEM(s, F32) for s in shapes] + [pltpu.SemaphoreType.DMA((6,))],
        compiler_params=pltpu.CompilerParams(vmem_limit_bytes=4 * 1024 * 1024),
    )


def solution(mesh):
    sizes = (mesh.shape["gx"], mesh.shape["gy"], mesh.shape["gz"])
    table = make_table()

    def on_device(coarse, cotangent, edge_in, edge_out, node_in, node_out, biases):
        nodes = cotangent.shape[1] * cotangent.shape[2] * cotangent.shape[3] * sizes[0] * sizes[1] * sizes[2]
        packed = make_main(sizes)(
            coarse, cotangent, edge_in, edge_out, node_in, node_out, biases, jnp.asarray(table)
        )
        return tuple(make_finish(float(nodes) ** -0.5)(packed))

    placed = (P(None, "gx", "gy", "gz"), P(None, "gx", "gy", "gz"), P(), P(), P(), P(), P())
    return jax.shard_map(
        on_device,
        mesh=mesh,
        in_specs=placed,
        out_specs=(P(None, "gx", "gy", "gz"), P(), P(), P(), P(), P()),
        check_vma=False,
    )
```

```python
import jax
import jax.numpy as jnp
import numpy as np
from jax import lax
from jax.experimental import pallas as pl
from jax.experimental.pallas import tpu as pltpu
from jax.sharding import PartitionSpec as P

MESH = pl.DeviceIdType.MESH
F32 = jnp.float32
BF16 = jnp.bfloat16
T = np.array(
    [
        -1.0,
        -0.8717401485096066,
        -0.5917001814331423,
        -0.2092992179024789,
        0.2092992179024789,
        0.5917001814331423,
        0.8717401485096066,
        1.0,
    ]
)
L0, L1 = (1.0 - T) / 2.0, (1.0 + T) / 2.0
LOG2E = float(np.log2(np.e))
LN2 = float(np.log(2.0))
GAP_UP = [float(T[i + 1] - T[i]) if i < 7 else float(T[1] - T[0]) for i in range(8)]
GAP_DOWN = [float(T[i - 1] - T[i]) if i > 0 else float(T[6] - T[7]) for i in range(8)]
Z_LOW = 4
CORES = 2
ABSENT = -1.0e5
SLOT = {0: 0, 1: 1, -1: 2, 2: 3}
STEPS = (-2, -1, 1, 2)
WIDE = (-2, -1, 0, 1, 2)
XZ = tuple((x, z) for x in WIDE for z in (-1, 0, 1) if (x, z) != (0, 0))
ROUND = tuple(d for d in XZ if d[1] != 0)
LEVEL = tuple(d for d in XZ if d[1] == 0)

RZ, RZ_UP, RZ_DOWN, PROFILES, Y_STD, Y_NEXT, Y_GAP, DELTA = 0, 32, 64, 96, 136, 168, 296, 328
ALONG_Z = 376
TABLE_ROWS = 504


def make_table():
    table = np.zeros((TABLE_ROWS, 128))
    for lane in range(128):
        e, a = divmod(lane, 8)
        table[RZ + e + 1, lane] += L0[a]
        table[RZ + e + 2, lane] += L1[a]
        if a < 7:
            table[RZ_UP + e + 1, lane] += L0[a + 1]
            table[RZ_UP + e + 2, lane] += L1[a + 1]
        else:
            table[RZ_UP + e + 2, lane] += L0[1]
            table[RZ_UP + e + 3, lane] += L1[1]
        if a > 0:
            table[RZ_DOWN + e + 1, lane] += L0[a - 1]
            table[RZ_DOWN + e + 2, lane] += L1[a - 1]
        else:
            table[RZ_DOWN + e, lane] += L0[6]
            table[RZ_DOWN + e + 1, lane] += L1[6]
        table[RZ_UP + 20, lane] = GAP_UP[a]
        table[RZ_DOWN + 20, lane] = GAP_DOWN[a]
    up = np.zeros((4, 8))
    down = np.zeros((4, 8))
    for y in range(8):
        if y < 7:
            up[1, y], up[2, y] = L0[y + 1], L1[y + 1]
        else:
            up[2, y], up[3, y] = L0[1], L1[1]
        if y > 0:
            down[1, y], down[2, y] = L0[y - 1], L1[y - 1]
        else:
            down[0, y], down[1, y] = L0[6], L1[6]
    for i, profile in enumerate((L1, up[2], up[3], down[2], down[0])):
        table[PROFILES + 8 * i : PROFILES + 8 * i + 8] = profile[:, None]
    for c in range(16):
        for y in range(8):
            lane = 8 * c + y
            table[Y_STD + c, lane] = L0[y]
            table[Y_STD + 16 + c, lane] = L1[y]
            for q in range(4):
                table[Y_NEXT + 16 * q + c, lane] = up[q, y]
                table[Y_NEXT + 64 + 16 * q + c, lane] = down[q, y]
            table[Y_GAP + c, lane] = GAP_UP[y]
            table[Y_GAP + 16 + c, lane] = GAP_DOWN[y]
            table[DELTA + c, lane] = 1.0
            table[DELTA + 16 + c, lane] = 1.0 if y == 0 else 0.0
            table[DELTA + 32 + c, lane] = 1.0 if y == 7 else 0.0
    table[ALONG_Z : ALONG_Z + 128, 0:96] = table[RZ : RZ + 96].T
    return table.astype(np.float32)


NN = (((1,), (0,)), ((), ()))
NT = (((1,), (1,)), ((), ()))


def dot(a, b, dims=NN):
    return lax.dot_general(a, b, dims, preferred_element_type=F32)


def split(a):
    high = a.astype(BF16)
    return high, (a - high.astype(F32)).astype(BF16)


def mm(a, b, dims=NN):
    (ah, al), (bh, bl) = a, b
    at = dims[0][1][0]
    return dot(jnp.concatenate([ah, ah, al], axis=1), jnp.concatenate([bh, bl, bh], axis=at), dims)


def mm_exact(a, b, dims=NN):
    return dot(jnp.concatenate([a[0], a[1]], axis=1), jnp.concatenate([b, b], axis=dims[0][1][0]), dims)


def exact_mm(a, b, dims=NN):
    return dot(a, b[0], dims) + dot(a, b[1], dims)


def iota(shape, dim):
    return lax.broadcasted_iota(jnp.int32, shape, dim)


def ones_where(mask):
    return jnp.where(mask, 1.0, 0.0).astype(F32)


def spread(a, k):
    k = k % 4
    return a if k == 0 else pltpu.roll(a, 32 * k, 1)


def vertex_maps():
    row, col = iota((128, 128), 0), iota((128, 128), 1)
    layer, vertex = row % 32, col % 32 - 1
    same = (row // 32 == col // 32) & (vertex < 18)
    maps = []
    for shift in (0, 16, -16):
        v = vertex + shift
        maps.append(ones_where(same & ((layer == 2 * v - 1) | (layer == 2 * v))).astype(BF16))
    return maps


def make_main(sizes):
    n_x, n_y, n_z = sizes
    z_high = n_y // CORES
    n_layers = z_high * Z_LOW
    n_cols = n_x // Z_LOW
    n_plane = n_cols * n_z

    def kernel(
        coarse_in, cot_in, edge_in_in, edge_out_in, node_in_in, node_out_in, biases_in, table_in,
        out,
        coarse, cot, edge_in, edge_out, node_in, node_out, biases, table, p0, p0_rim, xr, rim_r, vx, yr, means, lhs_rows, rows, e_all, e_sum, s_all, hn_all, u_all, g_all, xf,
        gm, yb, back_blocks, back_rims, xb, rim_b, payload, core_slot, col_slots, plane_slots, total,
        load_sem, xf_s, xf_r, yf_s, yf_r, yb_s, yb_r, xb_s, xb_r,
        core_s, core_r, col_s, col_r, plane_s, plane_r, cast_s, cast_r,
    ):
        ix, iy, iz = lax.axis_index("gx"), lax.axis_index("gy"), lax.axis_index("gz")
        low = lax.rem(ix, Z_LOW)
        core = lax.rem(iy, CORES)
        layer = (iy // CORES) * Z_LOW + low
        on_core1 = core == 1
        is_root = on_core1 & (layer == 0)
        is_leaf = on_core1 & (layer != 0)

        def at_xz(d):
            return (lax.rem(ix + (d[0] + n_x), n_x), iy, lax.rem(iz + (d[1] + n_z), n_z))

        def at_y(d):
            return (ix, lax.rem(iy + (d + n_y), n_y), iz)

        sibling = (ix, iy + 1 - 2 * core, iz)
        column_root = (ix - low, 1, iz)

        def in_column(k, c):
            return (ix + k % Z_LOW, (k // Z_LOW) * CORES + c, iz)

        def in_plane(k):
            col, row = k // n_z, k % n_z
            return (lax.rem(ix + Z_LOW * col, n_x), iy, lax.rem(iz + row, n_z))

        def send(src, dst, send_sem, recv_sem, device):
            return pltpu.make_async_remote_copy(
                src_ref=src, dst_ref=dst, send_sem=send_sem, recv_sem=recv_sem, device_id=device, device_id_type=MESH
            )

        def signal(device):
            pl.semaphore_signal(barrier, inc=1, device_id=device, device_id_type=MESH)

        loads = [
            pltpu.make_async_copy(src, dst, load_sem.at[i])
            for i, (src, dst) in enumerate(
                (
                    (coarse_in, coarse),
                    (edge_in_in, edge_in),
                    (edge_out_in, edge_out),
                    (node_in_in, node_in),
                    (node_out_in, node_out),
                    (biases_in, biases),
                    (table_in, table),
                    (cot_in, cot),
                )
            )
        ]
        loads[0].start()
        barrier = pltpu.get_barrier_semaphore()
        for d in XZ:
            signal(at_xz(d))
        for d in STEPS:
            signal(at_y(d))

        @pl.when(is_root)
        def _():
            for k in range(1, n_layers):
                signal(in_column(k, 1))
            for k in range(1, n_plane):
                signal(in_plane(k))

        for c in loads[1:]:
            c.start()
        expected = len(XZ) + len(STEPS) + jnp.where(is_leaf, 1, 0) + jnp.where(is_root, n_plane - 1, 0)

        lane = iota((16, 128), 1)
        group, place = lane // 32, lane % 32
        rim = (place[0:8] < 3) | (place[0:8] >= 29)

        def pack_rims(block):
            return jnp.where(rim, block[0:8, :], pltpu.roll(block[8:16, :], 120, 1))

        def unpack_rims(block):
            return jnp.concatenate([block, pltpu.roll(block, 8, 1)], axis=0)

        loads[0].wait()
        block = coarse[...]
        block = jnp.concatenate([block[:, p, q, :] for q in (0, 1) for p in (0, 1)], axis=1)
        p0[...] = block
        p0_rim[...] = pack_rims(block)
        pl.semaphore_wait(barrier, expected)

        def round_xz(level_src, level_dst, rim_src, rim_dst, send_sems, recv_sems):
            copies = []
            for d in ROUND + LEVEL:
                back = (-d[0], -d[1])
                i = XZ.index(back)
                if d[1] == 0:
                    src, dst = level_src(d[0]), level_dst.at[LEVEL.index(back)]
                else:
                    src, dst = rim_src(d[0]), rim_dst.at[ROUND.index(back)]
                copies.append(send(src, dst, send_sems.at[i], recv_sems.at[i], at_xz(d)))
            return copies

        x_sends = round_xz(lambda d: p0, xr, lambda d: p0_rim, rim_r, xf_s, xf_r)
        for c in x_sends:
            c.start()

        for c in loads[1:7]:
            c.wait()
        w_own, w_other = edge_in[:, 0:16], edge_in[:, 16:32]
        col_x, col_y, col_z = edge_in[:, 32:33], edge_in[:, 33:34], edge_in[:, 34:35]
        n_own, n_gathered = node_in[:, 0:16], node_in[:, 16:32]
        eye = ones_where(iota((16, 16), 0) == iota((16, 16), 1)).astype(BF16)
        delta = table[DELTA : DELTA + 16, :].astype(BF16)
        same_y = iota((128, 128), 0) % 8 == iota((128, 128), 1) % 8

        def transposed(w):
            return exact_mm(eye, split(w), NT)

        def widen(w):
            parts = []
            for part in split(w):
                left = dot(delta, part, (((0,), (0,)), ((), ()))).astype(BF16)
                parts.append(jnp.where(same_y, dot(left, delta), 0.0).astype(BF16))
            return tuple(parts)

        m1 = mm(split(n_gathered), split(edge_out[...]))
        m1_wide = widen(m1)
        m1_back = widen(transposed(m1))
        out_back = widen(transposed(node_out[...]))
        mix = split(jnp.concatenate([w_own, n_own, w_other], axis=0))
        mix_back = split(jnp.concatenate([transposed(n_own), transposed(w_own), transposed(w_other)], axis=1))
        bias_rows = biases[...]
        bias_cols = exact_mm(eye, split(bias_rows), NT)
        b0_col, b1_row, b2_col = bias_cols[:, 0:1], bias_rows[1:2, :], bias_cols[:, 2:3]
        nb_col = jnp.sum(n_gathered * b1_row, axis=1, keepdims=True)
        maps = vertex_maps()
        gap_lane = ones_where((place == 20) & (group < 2))

        def blocks4(first):
            t = table[first : first + 32, :]
            zero = jnp.zeros((32, 128), F32)
            return split(
                jnp.concatenate(
                    [jnp.concatenate([t if i == j else zero for j in range(4)], axis=1) for i in range(4)], axis=0
                )
            )

        rz, rz_up, rz_down = blocks4(RZ), blocks4(RZ_UP), blocks4(RZ_DOWN)
        back_z = table[ALONG_Z : ALONG_Z + 128, :]
        group_z = iota((128, 128), 1) // 32

        def back_blocks_z(kind, n):
            return split(jnp.concatenate([jnp.where(group_z == i, spread(back_z, i - kind), 0.0) for i in range(n)], axis=0))

        to_rz, to_rz_up, to_rz_down = back_blocks_z(0, 4), back_blocks_z(1, 2), back_blocks_z(2, 2)

        loads[7].wait()
        for k in range(4):
            wide = jnp.concatenate([cot[:, 2 * k + i].reshape(128, 128) for i in (0, 1)], axis=1)
            u_all[:, :, 256 * k : 256 * k + 256] = mm(out_back, split(wide)).reshape(16, 8, 256)
        sum_all, sum_one = cot[:, 0], jnp.zeros((16, 8, 128), F32)
        for x in range(1, 8):
            sum_all = sum_all + cot[:, x]
            sum_one = sum_one + float(L1[x]) * cot[:, x]
        xf[:, :, 0:128] = sum_all - sum_one
        xf[:, :, 128:256] = sum_one

        for c in x_sends:
            c.wait_recv()
        pieces = []
        for d in WIDE:
            level = p0[...] if d == 0 else xr[LEVEL.index((d, 0))]
            rims = [unpack_rims(rim_r[ROUND.index((d, z))]) for z in (-1, 1)]
            pieces.append(jnp.concatenate([level] + rims, axis=1))
        summed = mm_exact(split(jnp.concatenate(pieces, axis=0)), jnp.concatenate(maps, axis=0))
        x_blocks = {d: summed[16 * i : 16 * i + 16, :] for i, d in enumerate(WIDE)}
        for q in (0, 1):
            acc = jnp.zeros((16, 128), F32)
            for vertex in (-1, 0, 1, 2):
                for d in (vertex - 1, vertex):
                    moved = spread(x_blocks[d], SLOT[vertex] - (2 * q + vertex - d))
                    acc = acc + jnp.where(group == SLOT[vertex], moved, 0.0)
            vx[q] = acc
        y_sends = []
        for d in STEPS:
            i = STEPS.index(-d)
            qs = pl.ds(0, 2) if abs(d) == 1 else pl.ds(1 if d == 2 else 0, 1)
            y_sends.append(send(vx.at[qs], yr.at[i, qs], yf_s.at[i], yf_r.at[i], at_y(d)))
        for c in y_sends:
            c.start()

        def exists(d):
            return jnp.where((iy + d >= 0) & (iy + d < n_y), 1.0, 0.0).astype(F32)

        there = {d: exists(d) for d in (-2, -1, 0, 1, 2)}
        wall_low, wall_high = 1.0 - there[-1], 1.0 - there[1]
        y_index = iota((8, 128), 0)
        count = 6.0 - wall_low * ones_where(y_index == 0) - wall_high * ones_where(y_index == 7)
        ly, up1, up2, down1, down0 = (table[PROFILES + 8 * i : PROFILES + 8 * i + 8, :] for i in range(5))

        for c in y_sends:
            c.wait_recv()

        def y_block(d, q):
            return vx[q] if d == 0 else yr[STEPS.index(d), q] * there[d]

        for q in (-1, 0, 1, 2):
            copies = jnp.maximum(there[q - 1] + there[q], 1.0)
            means[q + 1] = (y_block(q - 1, 1) + y_block(q, 0)) * (0.25 / copies)

        mixed = mm(mix, split(jnp.concatenate([means[i] for i in range(4)], axis=1)))
        for i in range(4):
            lanes = slice(128 * i, 128 * i + 128)
            if i in (1, 2):
                lhs_rows[48 * (i - 1) : 48 * (i - 1) + 32, :] = mixed[0:32, lanes]
                lhs_rows[48 * (i - 1) + 32 : 48 * i, :] = mixed[32:48, lanes] + col_z * gap_lane
            else:
                first = 96 if i == 0 else 112
                lhs_rows[first : first + 16, :] = mixed[32:48, lanes]
        along = mm(split(lhs_rows[...]), rz)
        other01 = split(jnp.concatenate([lhs_rows[32:48, :], lhs_rows[80:96, :]], axis=0))
        along_up = mm(other01, (rz_up[0][:, 0:256], rz_up[1][:, 0:256]))
        along_down = mm(other01, (rz_down[0][:, 0:256], rz_down[1][:, 0:256]))

        def vertex_rows(field, q, vertex):
            first = {0: 0, 1: 48}[q] + 16 * field if q in (0, 1) else (96 if q == -1 else 112)
            s = SLOT[vertex]
            return along[first : first + 16, 128 * s : 128 * s + 128]

        def next_rows(source, q, vertex):
            return source[16 * q : 16 * q + 16, 128 * vertex : 128 * vertex + 128]

        def put(field, x, value):
            rows[pl.ds(128 * field + x, 16, stride=8), :] = value

        def line(a, b, t):
            return a + t * (b - a)

        for x in range(8):
            t = float(L1[x])
            here = float(T[x]) * col_x
            own = [
                (line(vertex_rows(0, q, 0), vertex_rows(0, q, 1), t) + (b0_col - here - (2 * q - 1.0) * col_y)) * LOG2E
                for q in (0, 1)
            ]
            put(0, x, own[0])
            put(1, x, own[1] - own[0])
            other = {
                q: (line(vertex_rows(2, q, 0), vertex_rows(2, q, 1), t) + (here + (2 * q - 1.0) * col_y)) * LOG2E
                for q in (-1, 0, 1, 2)
            }
            put(2, x, other[0])
            put(3, x, other[1] - other[0])
            put(5, x, (other[2] - other[0]) * there[1] + ABSENT * wall_high)
            put(6, x, (other[-1] - other[0]) * there[-1] + ABSENT * wall_low)
            for f, source in ((7, along_up), (9, along_down)):
                z = [
                    (line(next_rows(source, q, 0), next_rows(source, q, 1), t) + (here + (2 * q - 1.0) * col_y)) * LOG2E
                    for q in (0, 1)
                ]
                put(f, x, z[0])
                put(f + 1, x, z[1] - z[0])
            hn = [line(vertex_rows(1, q, 0), vertex_rows(1, q, 1), t) for q in (0, 1)]
            put(11, x, hn[0] + b2_col)
            put(12, x, hn[1] - hn[0])
            put(13, x, jnp.broadcast_to(nb_col, (16, 128)))
        for side, (a, b, t, at) in enumerate(((-1, 0, float(L1[6]), float(T[6]) - 2.0), (1, 2, float(L1[1]), float(T[1]) + 2.0))):
            other = [
                (line(vertex_rows(2, q, a), vertex_rows(2, q, b), t) + (at * col_x + (2 * q - 1.0) * col_y)) * LOG2E
                for q in (0, 1)
            ]
            put(4, 2 * side, other[0])
            put(4, 2 * side + 1, other[1] - other[0])

        def forward(c, carry):
            def row(field, x):
                return rows[pl.ds(128 * field + 8 * c + x, 1), :]

            other = [row(4, 0) + ly * row(4, 1)]
            for x in range(8):
                other.append(row(2, x) + ly * row(3, x))
            other.append(row(4, 2) + ly * row(4, 3))
            for x in range(8):
                own = row(0, x) + ly * row(1, x)
                a, d = row(2, x), row(3, x)
                senders = (
                    other[x + 2],
                    other[x],
                    a + up1 * d + up2 * row(5, x),
                    a + down1 * d + down0 * row(6, x),
                    row(7, x) + ly * row(8, x),
                    row(9, x) + ly * row(10, x),
                )
                tops, decays = None, None
                for k, sender in enumerate(senders):
                    z = own + sender
                    decay = jnp.exp2(jnp.minimum(z, 0.0))
                    top = jnp.maximum(z, 0.0)
                    e_all[k, x, c] = decay
                    tops = top if tops is None else tops + top
                    decays = decay if decays is None else decays + decay
                e_sum[x, c] = decays
                s_all[c, :, 128 * x : 128 * x + 128] = LN2 * tops + (decays - count)
                hn_all[c, :, 128 * x : 128 * x + 128] = row(11, x) + ly * row(12, x) + count * row(13, x)
            return carry

        lax.fori_loop(0, 16, forward, 0)

        outer_out = jnp.zeros((128, 128), F32)
        outer_in = jnp.zeros((128, 128), F32)
        dh_all = jnp.zeros((16, 8, 128), F32)
        dh_one = jnp.zeros((16, 8, 128), F32)
        for k in range(4):
            lanes = slice(256 * k, 256 * k + 256)
            s = split(s_all[:, :, lanes].reshape(128, 256))
            h = mm(m1_wide, s) + hn_all[:, :, lanes].reshape(128, 256)
            decay = jnp.exp(jnp.minimum(h, 0.0))
            a = jnp.maximum(h, 0.0) + (decay - 1.0)
            dh = decay * u_all[:, :, lanes].reshape(128, 256)
            dh_parts = split(dh)
            g_all[:, :, lanes] = mm(m1_back, dh_parts).reshape(16, 8, 256)
            wide = jnp.concatenate([cot[:, 2 * k + i].reshape(128, 128) for i in (0, 1)], axis=1)
            outer_out = outer_out + mm(split(wide), split(a), NT)
            outer_in = outer_in + mm(dh_parts, s, NT)
            for i in (0, 1):
                part = dh[:, 128 * i : 128 * i + 128].reshape(16, 8, 128)
                dh_all = dh_all + part
                dh_one = dh_one + float(L1[2 * k + i]) * part
        xf[:, :, 256:384] = dh_all - dh_one
        xf[:, :, 384:512] = dh_one

        def backward(c, carry):
            g = [g_all[c, :, 128 * x : 128 * x + 128] for x in range(8)]
            own = [g[x] * e_sum[x, c] for x in range(8)]

            def bz(k, x):
                return g[x] * e_all[k, x, c]

            def save(i, value):
                xf[c, :, 128 * i : 128 * i + 128] = value

            def reduce(first, values):
                everything, one = values[0], float(L1[1]) * values[1]
                for x in range(1, 8):
                    everything = everything + values[x]
                for x in range(2, 8):
                    one = one + float(L1[x]) * values[x]
                save(first, everything - one)
                save(first + 1, one)

            reduce(4, own)
            ups = [bz(0, x) for x in range(8)]
            downs = [bz(1, x) for x in range(8)]
            acc = GAP_UP[0] * ups[0] + GAP_DOWN[0] * downs[0]
            for x in range(1, 8):
                acc = acc + GAP_UP[x] * ups[x] + GAP_DOWN[x] * downs[x]
            save(6, acc)
            at = [downs[1]] + [ups[x - 1] + downs[x + 1] for x in range(1, 7)] + [ups[6]]
            everything, one = at[0], float(L1[1]) * at[1]
            for x in range(1, 8):
                everything = everything + at[x]
            for x in range(2, 8):
                one = one + float(L1[x]) * at[x]
            save(7, everything - one + float(L1[6]) * downs[0])
            save(8, one + float(L0[1]) * ups[7])
            save(9, float(L0[6]) * downs[0])
            save(10, float(L1[1]) * ups[7])
            for k in range(4):
                reduce(11 + 2 * k, [bz(2 + k, x) for x in range(8)])
            return carry

        lax.fori_loop(0, 16, backward, 0)

        def along_z(first, n, by):
            return mm(
                split(xf[:, :, 128 * first : 128 * (first + n)].reshape(128, 128 * n)),
                (by[0][0 : 128 * n, :], by[1][0 : 128 * n, :]),
            )

        z1 = along_z(0, 4, to_rz)
        z2 = along_z(4, 3, to_rz)
        z3 = along_z(7, 4, to_rz) + along_z(15, 2, to_rz_up) + along_z(17, 2, to_rz_down)
        z4 = along_z(11, 4, to_rz)
        counting = (
            6.0 * table[DELTA : DELTA + 16, :]
            - wall_low * table[DELTA + 16 : DELTA + 32, :]
            - wall_high * table[DELTA + 32 : DELTA + 48, :]
        )
        left = split(jnp.concatenate([table[Y_STD : Y_STD + 32, :], counting], axis=0))
        std = mm(left, split(jnp.concatenate([z1, z2, z3], axis=1)))
        nxt = mm(split(table[Y_NEXT : Y_NEXT + 160, :]), split(z4))

        low_half, low_lanes = group < 2, ones_where(group < 2)
        fields = {}
        for q in (0, 1):
            r = slice(16 * q, 16 * q + 16)
            fields[q] = (std[r, 0:128], std[r, 128:256], std[r, 256:384])
        others = {}
        for q in (-1, 0, 1, 2):
            r_up = slice(16 * (q + 1), 16 * (q + 1) + 16)
            r_down = slice(64 + 16 * (q + 1), 64 + 16 * (q + 1) + 16)
            both = jnp.where(low_half, nxt[r_up, :] + pltpu.roll(nxt[r_down, :], 64, 1), 0.0)
            others[q] = both + fields[q][2] if q in (0, 1) else both

        summed_out = jnp.where(same_y, outer_out, 0.0)
        summed_in = jnp.where(same_y, outer_in, 0.0)
        big = exact_mm(delta, split(jnp.concatenate([summed_out, summed_in], axis=1)))
        r2, c2 = iota((128, 256), 0), iota((128, 256), 1)
        placing = ones_where((c2 // 128 * 16 + c2 % 128 // 8) == r2).astype(BF16)
        part = mm_exact(split(big), placing, NT)
        r8, l8 = iota((8, 128), 0), iota((8, 128), 1)

        def marked(r, mask):
            return ones_where((r8 == r) & mask)

        def right(first, rows16, special):
            pieces = []
            if rows16 is None:
                pieces.append(jnp.zeros((80, 128), F32))
            else:
                if first > 0:
                    pieces.append(jnp.zeros((first, 128), F32))
                pieces.append(rows16)
                if first < 64:
                    pieces.append(jnp.zeros((64 - first, 128), F32))
            pieces += [special, jnp.zeros((40, 128), F32)]
            return jnp.concatenate(pieces, axis=0)

        lefts, rights = [], []
        none8 = jnp.zeros((8, 128), F32)
        for q in (-1, 0, 1, 2):
            m = means[q + 1]
            if q in (0, 1):
                lefts.append(fields[q][0])
                rights.append(right(32, jnp.where(low_half, 0.0, pltpu.roll(m, 64, 1)), marked(4, l8 >= 64)))
                lefts.append(fields[q][1])
                rights.append(right(48, m * low_lanes, marked(3, l8 < 64) + marked(0, (l8 >= 64) & (l8 < 96))))
            lefts.append(others[q])
            rights.append(right(64, m, marked(2, (l8 % 32 == 20) & (l8 < 64)) if q in (0, 1) else none8))
        lefts += [std[32:48, 0:128], nxt[128:144, :], nxt[144:160, :]]
        rights += [
            right(0, None, marked(5, l8 >= 64)),
            right(0, None, marked(1, l8 < 64)),
            right(0, None, marked(1, l8 >= 64)),
        ]
        payload[...] = part + mm(split(jnp.concatenate(lefts, axis=1)), split(jnp.concatenate(rights, axis=1)), NT)

        to_second = send(payload, core_slot, core_s, core_r, sibling)
        to_first = send(total, total, cast_s.at[0], cast_r, sibling)
        slot = jnp.maximum(layer - 1, 0)
        to_root = send(payload, col_slots.at[slot], col_s, col_r.at[slot], column_root)

        @pl.when(core == 0)
        def _():
            to_second.start()

        zero = jnp.zeros((16, 128), F32)
        stacked = []
        for q in (-1, 0, 1, 2):
            if q in (0, 1):
                dh_q = jnp.where(low_half, pltpu.roll(fields[q][0], 64, 1), 0.0)
                own_q = jnp.where(low_half, fields[q][1], 0.0)
            else:
                dh_q, own_q = zero, zero
            stacked.append(jnp.concatenate([dh_q, own_q, others[q]], axis=0))
        back = mm(mix_back, split(jnp.concatenate(stacked, axis=1)))
        for q in (-1, 0, 1, 2):
            value = back[:, 128 * (q + 1) : 128 * (q + 2)]
            if q in (0, 1):
                value = value + jnp.where(low_half, fields[q][0], 0.0)
            gm[q + 1] = value
        y_back = []
        for d in STEPS:
            i = STEPS.index(-d)
            if abs(d) == 1:
                src, dst = gm.at[pl.ds(2 if d == 1 else 0, 2)], yb.at[i]
            else:
                src, dst = gm.at[pl.ds(3 if d == 2 else 0, 1)], yb.at[i, pl.ds(0 if d == 2 else 1, 1)]
            y_back.append(send(src, dst, yb_s.at[i], yb_r.at[i], at_y(d)))
        for c in y_back:
            c.start()

        @pl.when(on_core1)
        def _():
            to_second.wait_recv()
            payload[...] = payload[...] + core_slot[...]

        @pl.when(is_leaf)
        def _():
            to_root.start()

        edge_place = (place[0:8] < 2) | (place[0:8] == 17) | (place[0:8] == 18)

        def pack_back(block):
            return jnp.where(edge_place, block[0:8, :], pltpu.roll(block[8:16, :], 8, 1))

        def unpack_back(block):
            return jnp.concatenate([block, pltpu.roll(block, 120, 1)], axis=0)

        for c in y_back:
            c.wait_recv()
        own_rows = []
        for q in (0, 1):
            value = gm[q + 1]
            for d in (-2, -1, 1, 2):
                if (d, q) not in ((-2, 1), (2, 0)):
                    value = value + yb[STEPS.index(d), q] * there[d]
            own_rows.append(value)
        for i, d in enumerate(WIDE):
            value = jnp.zeros((16, 128), F32)
            for q in (0, 1):
                for p in (0, 1):
                    if p + d in SLOT:
                        moved = spread(own_rows[q], 2 * q + p - SLOT[p + d])
                        value = value + jnp.where(group == 2 * q + p, moved, 0.0)
            back_blocks[i] = value
            back_rims[i] = pack_back(value)
        x_back = round_xz(
            lambda d: back_blocks.at[WIDE.index(d)], xb, lambda d: back_rims.at[WIDE.index(d)], rim_b, xb_s, xb_r
        )
        for c in x_back:
            c.start()

        my_place = (ix // Z_LOW) * n_z + iz
        to_plane = [
            send(plane_slots.at[my_place], plane_slots.at[my_place], plane_s.at[k], plane_r.at[k], in_plane(k))
            for k in range(1, n_plane)
        ]

        @pl.when(is_root)
        def _():
            value = payload[...]
            for k in range(n_layers - 1):
                send(payload, col_slots.at[k], col_s, col_r.at[k], in_column(k + 1, 1)).wait_recv()
                value = value + col_slots[k]
            plane_slots[my_place] = value
            for c in to_plane:
                c.start()

        up_column = [send(total, total, cast_s.at[k], cast_r, in_column(k, 1)) for k in range(1, n_layers)]

        @pl.when(is_root)
        def _():
            for k, c in enumerate(to_plane):
                c.wait_recv()
            value = plane_slots[0]
            for k in range(1, n_plane):
                value = value + plane_slots[k]
            total[...] = value
            for c in [to_first] + up_column:
                c.start()

        for c in x_back:
            c.wait_recv()
        level = back_blocks[WIDE.index(0)]
        for i in range(len(LEVEL)):
            level = level + xb[i]
        sides = []
        for z in (-1, 1):
            value = rim_b[ROUND.index((-2, z))]
            for d in WIDE[1:]:
                value = value + rim_b[ROUND.index((d, z))]
            sides.append(unpack_back(value))
        level, sides = split(level), [split(v) for v in sides]
        value = mm_exact(level, maps[0], NT) + mm_exact(sides[0], maps[2], NT) + mm_exact(sides[1], maps[1], NT)
        out[0:16, :] = value * jnp.where(group < 2, 0.25 / (1.0 + there[-1]), 0.25 / (1.0 + there[1]))

        @pl.when(jnp.logical_not(is_root))
        def _():
            to_first.wait_recv()

        @pl.when(is_leaf)
        def _():
            to_first.start()

        out[16:32, :] = total[...]
        out[32:48, 0:32] = node_in[...]
        out[32:48, 32:48] = edge_out[...]
        out[48:51, 0:16] = biases[...]

        for c in x_sends + y_sends + y_back + x_back:
            c.wait_send()

        @pl.when(core == 0)
        def _():
            to_second.wait_send()

        @pl.when(on_core1)
        def _():
            to_first.wait_send()

        @pl.when(is_leaf)
        def _():
            to_root.wait_send()

        @pl.when(is_root)
        def _():
            for c in to_plane + up_column:
                c.wait_send()

    block = pltpu.VMEM((16, 128), F32)

    def blocks(*lead):
        return pltpu.VMEM(lead + (16, 128), F32)

    dma = pltpu.SemaphoreType.DMA
    scratch = [
        pltpu.VMEM((16, 2, 2, 32), F32),
        pltpu.VMEM((16, 8, 8, 128), F32),
        pltpu.VMEM((16, 35), F32),
        pltpu.VMEM((16, 16), F32),
        pltpu.VMEM((16, 32), F32),
        pltpu.VMEM((16, 16), F32),
        pltpu.VMEM((3, 16), F32),
        pltpu.VMEM((TABLE_ROWS, 128), F32),
        block,
        pltpu.VMEM((8, 128), F32),
        blocks(len(LEVEL)),
        pltpu.VMEM((len(ROUND), 8, 128), F32),
        blocks(2),
        blocks(4, 2),
        blocks(4),
        pltpu.VMEM((128, 128), F32),
        pltpu.VMEM((14 * 128, 128), F32),
        pltpu.VMEM((6, 8, 16, 8, 128), F32),
        pltpu.VMEM((8, 16, 8, 128), F32),
        pltpu.VMEM((16, 8, 1024), F32),
        pltpu.VMEM((16, 8, 1024), F32),
        pltpu.VMEM((16, 8, 1024), F32),
        pltpu.VMEM((16, 8, 1024), F32),
        pltpu.VMEM((16, 8, 19 * 128), F32),
        blocks(4),
        blocks(4, 2),
        blocks(len(WIDE)),
        pltpu.VMEM((len(WIDE), 8, 128), F32),
        blocks(len(LEVEL)),
        pltpu.VMEM((len(ROUND), 8, 128), F32),
        block,
        block,
        blocks(n_layers - 1),
        blocks(n_plane),
        block,
        dma((8,)),
        dma((len(XZ),)), dma((len(XZ),)), dma((4,)), dma((4,)), dma((4,)), dma((4,)), dma((len(XZ),)), dma((len(XZ),)),
        dma, dma, dma, dma((n_layers - 1,)), dma((n_plane,)), dma((n_plane,)), dma((n_layers,)), dma,
    ]
    vmem = pl.BlockSpec(memory_space=pltpu.VMEM)
    return pl.pallas_call(
        kernel,
        out_shape=jax.ShapeDtypeStruct((56, 128), F32),
        in_specs=[pl.BlockSpec(memory_space=pltpu.HBM)] * 8,
        out_specs=vmem,
        scratch_shapes=scratch,
        compiler_params=pltpu.CompilerParams(
            collective_id=0, has_side_effects=True, vmem_limit_bytes=60 * 1024 * 1024
        ),
    )


def make_finish(factor):
    shapes = ((16, 2, 2, 32), (16, 35), (16, 16), (16, 32), (16, 16), (3, 16))

    def kernel(packed, *refs):
        outs, buffers, sem = refs[:6], refs[6:12], refs[12]
        grad_coarse, g_edge_in, g_edge_out, g_node_in, g_node_out, g_biases = buffers
        copies = [pltpu.make_async_copy(src, dst, sem.at[i]) for i, (src, dst) in enumerate(zip(buffers, outs))]
        block = packed[0:16, :]
        for q in (0, 1):
            for p in (0, 1):
                grad_coarse[:, p, q, :] = block[:, 32 * (2 * q + p) : 32 * (2 * q + p) + 32]
        copies[0].start()
        total = packed[16:32, :] * factor
        g_node_out[...] = total[:, 0:16]
        copies[4].start()
        g_edge_in[...] = total[:, 48:83]
        copies[1].start()
        n_gathered, edge_out, b1_row = packed[32:48, 16:32], packed[32:48, 32:48], packed[49:50, 0:16]
        eye = ones_where(iota((16, 16), 0) == iota((16, 16), 1)).astype(BF16)
        n_back = exact_mm(eye, split(n_gathered), NT)
        back = mm(split(n_back), split(total))
        g_edge_out[...] = back[:, 16:32]
        copies[2].start()
        outer_in = total[:, 16:32]
        g_node_in[:, 0:16] = total[:, 32:48]
        g_node_in[:, 16:32] = mm(split(outer_in), split(edge_out), NT) + total[:, 85:86] * b1_row
        copies[3].start()
        rows = jnp.concatenate([total, back], axis=1)
        r, c = iota((8, 256), 0), iota((8, 256), 1)
        pick = ones_where(((r == 0) & (c == 83)) | ((r == 1) & (c == 128 + 85)) | ((r == 2) & (c == 84))).astype(BF16)
        g_biases[...] = exact_mm(pick, split(rows), NT)[0:3, :]
        copies[5].start()
        for c in copies:
            c.wait()

    return pl.pallas_call(
        kernel,
        out_shape=[jax.ShapeDtypeStruct(s, F32) for s in shapes],
        in_specs=[pl.BlockSpec(memory_space=pltpu.VMEM)],
        out_specs=[pl.BlockSpec(memory_space=pltpu.HBM)] * 6,
        scratch_shapes=[pltpu.VMEM(s, F32) for s in shapes] + [pltpu.SemaphoreType.DMA((6,))],
        compiler_params=pltpu.CompilerParams(vmem_limit_bytes=4 * 1024 * 1024),
    )


def solution(mesh):
    sizes = (mesh.shape["gx"], mesh.shape["gy"], mesh.shape["gz"])
    table = make_table()

    def on_device(coarse, cotangent, edge_in, edge_out, node_in, node_out, biases):
        nodes = cotangent.shape[1] * cotangent.shape[2] * cotangent.shape[3] * sizes[0] * sizes[1] * sizes[2]
        packed = make_main(sizes)(
            coarse, cotangent, edge_in, edge_out, node_in, node_out, biases, jnp.asarray(table)
        )
        return tuple(make_finish(float(nodes) ** -0.5)(packed))

    placed = (P(None, "gx", "gy", "gz"), P(None, "gx", "gy", "gz"), P(), P(), P(), P(), P())
    return jax.shard_map(
        on_device,
        mesh=mesh,
        in_specs=placed,
        out_specs=(P(None, "gx", "gy", "gz"), P(), P(), P(), P(), P()),
        check_vma=False,
    )
```

```python
import jax
import jax.numpy as jnp
import numpy as np
from jax import lax
from jax.experimental import pallas as pl
from jax.experimental.pallas import tpu as pltpu
from jax.sharding import PartitionSpec as P

MESH = pl.DeviceIdType.MESH
F32 = jnp.float32
BF16 = jnp.bfloat16
T = np.array(
    [
        -1.0,
        -0.8717401485096066,
        -0.5917001814331423,
        -0.2092992179024789,
        0.2092992179024789,
        0.5917001814331423,
        0.8717401485096066,
        1.0,
    ]
)
L0, L1 = (1.0 - T) / 2.0, (1.0 + T) / 2.0
LOG2E = float(np.log2(np.e))
LN2 = float(np.log(2.0))
GAP_UP = [float(T[i + 1] - T[i]) if i < 7 else float(T[1] - T[0]) for i in range(8)]
GAP_DOWN = [float(T[i - 1] - T[i]) if i > 0 else float(T[6] - T[7]) for i in range(8)]
Z_LOW = 4
CORES = 2
ABSENT = -1.0e5
SLOT = {0: 0, 1: 1, -1: 2, 2: 3}
STEPS = (-2, -1, 1, 2)
WIDE = (-2, -1, 0, 1, 2)
XZ = tuple((x, z) for x in WIDE for z in (-1, 0, 1) if (x, z) != (0, 0))
ROUND = tuple(d for d in XZ if d[1] != 0)
LEVEL = tuple(d for d in XZ if d[1] == 0)

RZ, RZ_UP, RZ_DOWN, PROFILES, Y_STD, Y_NEXT, Y_GAP, DELTA = 0, 32, 64, 96, 136, 168, 296, 328
ALONG_Z = 376
TABLE_ROWS = 504


def make_table():
    table = np.zeros((TABLE_ROWS, 128))
    for lane in range(128):
        e, a = divmod(lane, 8)
        table[RZ + e + 1, lane] += L0[a]
        table[RZ + e + 2, lane] += L1[a]
        if a < 7:
            table[RZ_UP + e + 1, lane] += L0[a + 1]
            table[RZ_UP + e + 2, lane] += L1[a + 1]
        else:
            table[RZ_UP + e + 2, lane] += L0[1]
            table[RZ_UP + e + 3, lane] += L1[1]
        if a > 0:
            table[RZ_DOWN + e + 1, lane] += L0[a - 1]
            table[RZ_DOWN + e + 2, lane] += L1[a - 1]
        else:
            table[RZ_DOWN + e, lane] += L0[6]
            table[RZ_DOWN + e + 1, lane] += L1[6]
        table[RZ_UP + 20, lane] = GAP_UP[a]
        table[RZ_DOWN + 20, lane] = GAP_DOWN[a]
    up = np.zeros((4, 8))
    down = np.zeros((4, 8))
    for y in range(8):
        if y < 7:
            up[1, y], up[2, y] = L0[y + 1], L1[y + 1]
        else:
            up[2, y], up[3, y] = L0[1], L1[1]
        if y > 0:
            down[1, y], down[2, y] = L0[y - 1], L1[y - 1]
        else:
            down[0, y], down[1, y] = L0[6], L1[6]
    for i, profile in enumerate((L1, up[2], up[3], down[2], down[0])):
        table[PROFILES + 8 * i : PROFILES + 8 * i + 8] = profile[:, None]
    for c in range(16):
        for y in range(8):
            lane = 8 * c + y
            table[Y_STD + c, lane] = L0[y]
            table[Y_STD + 16 + c, lane] = L1[y]
            for q in range(4):
                table[Y_NEXT + 16 * q + c, lane] = up[q, y]
                table[Y_NEXT + 64 + 16 * q + c, lane] = down[q, y]
            table[Y_GAP + c, lane] = GAP_UP[y]
            table[Y_GAP + 16 + c, lane] = GAP_DOWN[y]
            table[DELTA + c, lane] = 1.0
            table[DELTA + 16 + c, lane] = 1.0 if y == 0 else 0.0
            table[DELTA + 32 + c, lane] = 1.0 if y == 7 else 0.0
    table[ALONG_Z : ALONG_Z + 128, 0:96] = table[RZ : RZ + 96].T
    return table.astype(np.float32)


RESULTS = ((16, 2, 2, 32), (16, 35), (16, 16), (16, 32), (16, 16), (3, 16))
NN = (((1,), (0,)), ((), ()))
NT = (((1,), (1,)), ((), ()))


def dot(a, b, dims=NN):
    return lax.dot_general(a, b, dims, preferred_element_type=F32)


def split(a):
    high = a.astype(BF16)
    return high, (a - high.astype(F32)).astype(BF16)


def mm(a, b, dims=NN):
    (ah, al), (bh, bl) = a, b
    at = dims[0][1][0]
    return dot(jnp.concatenate([ah, ah, al], axis=1), jnp.concatenate([bh, bl, bh], axis=at), dims)


def mm_exact(a, b, dims=NN):
    return dot(jnp.concatenate([a[0], a[1]], axis=1), jnp.concatenate([b, b], axis=dims[0][1][0]), dims)


def exact_mm(a, b, dims=NN):
    return dot(a, b[0], dims) + dot(a, b[1], dims)


def iota(shape, dim):
    return lax.broadcasted_iota(jnp.int32, shape, dim)


def ones_where(mask):
    return jnp.where(mask, 1.0, 0.0).astype(F32)


def spread(a, k):
    k = k % 4
    return a if k == 0 else pltpu.roll(a, 32 * k, 1)


def vertex_maps():
    row, col = iota((128, 128), 0), iota((128, 128), 1)
    layer, vertex = row % 32, col % 32 - 1
    same = (row // 32 == col // 32) & (vertex < 18)
    maps = []
    for shift in (0, 16, -16):
        v = vertex + shift
        maps.append(ones_where(same & ((layer == 2 * v - 1) | (layer == 2 * v))).astype(BF16))
    return maps


def make_main(sizes, factor):
    n_x, n_y, n_z = sizes
    z_high = n_y // CORES
    n_layers = z_high * Z_LOW
    n_cols = n_x // Z_LOW
    n_plane = n_cols * n_z

    def kernel(
        coarse_in, cot_in, edge_in_in, edge_out_in, node_in_in, node_out_in, biases_in, table_in,
        *refs,
    ):
        results, outs, refs = refs[0:6], refs[6:12], refs[12:]
        (
        coarse, cot, edge_in, edge_out, node_in, node_out, biases, table, p0, p0_rim, xr, rim_r, vx, yr, means, lhs_rows, rows, e_all, e_sum, s_all, hn_all, u_all, g_all, xf,
        gm, yb, back_blocks, back_rims, xb, rim_b, payload, col_slots, plane_slots, total,
        load_sem, xf_s, xf_r, yf_s, yf_r, yb_s, yb_r, xb_s, xb_r,
        col_s, col_r, plane_s, plane_r, cast_s, cast_r, save_sem,
        ) = refs
        g_coarse, g_edge_in, g_edge_out, g_node_in, g_node_out, g_biases = outs
        saves = [pltpu.make_async_copy(src, dst, save_sem.at[i]) for i, (src, dst) in enumerate(zip(outs, results))]
        ix, iy, iz = lax.axis_index("gx"), lax.axis_index("gy"), lax.axis_index("gz")
        low = lax.rem(ix, Z_LOW)
        core = lax.rem(iy, CORES)
        layer = (iy // CORES) * Z_LOW + low
        on_core1 = core == 1
        is_root = on_core1 & (layer == 0)
        member = layer * CORES + core

        def at_xz(d):
            return (lax.rem(ix + (d[0] + n_x), n_x), iy, lax.rem(iz + (d[1] + n_z), n_z))

        def at_y(d):
            return (ix, lax.rem(iy + (d + n_y), n_y), iz)

        sibling = (ix, iy + 1 - 2 * core, iz)
        column_root = (ix - low, 1, iz)

        def in_column(k, c):
            return (ix + k % Z_LOW, (k // Z_LOW) * CORES + c, iz)

        def in_plane(k):
            col, row = k // n_z, k % n_z
            return (lax.rem(ix + Z_LOW * col, n_x), iy, lax.rem(iz + row, n_z))

        def send(src, dst, send_sem, recv_sem, device):
            return pltpu.make_async_remote_copy(
                src_ref=src, dst_ref=dst, send_sem=send_sem, recv_sem=recv_sem, device_id=device, device_id_type=MESH
            )

        def signal(device):
            pl.semaphore_signal(barrier, inc=1, device_id=device, device_id_type=MESH)

        loads = [
            pltpu.make_async_copy(src, dst, load_sem.at[i])
            for i, (src, dst) in enumerate(
                (
                    (coarse_in, coarse),
                    (edge_in_in, edge_in),
                    (edge_out_in, edge_out),
                    (node_in_in, node_in),
                    (node_out_in, node_out),
                    (biases_in, biases),
                    (table_in, table),
                    (cot_in, cot),
                )
            )
        ]
        loads[0].start()
        barrier = pltpu.get_barrier_semaphore()
        for d in XZ:
            signal(at_xz(d))
        for d in STEPS:
            signal(at_y(d))

        @pl.when(is_root)
        def _():
            for k in range(1, n_layers):
                for c in range(CORES):
                    signal(in_column(k, c))
            for k in range(1, n_plane):
                signal(in_plane(k))

        for c in loads[1:]:
            c.start()
        expected = len(XZ) + len(STEPS) + jnp.where(layer != 0, 1, 0) + jnp.where(is_root, n_plane - 1, 0)

        lane = iota((16, 128), 1)
        group, place = lane // 32, lane % 32
        rim = (place[0:8] < 3) | (place[0:8] >= 29)

        def pack_rims(block):
            return jnp.where(rim, block[0:8, :], pltpu.roll(block[8:16, :], 120, 1))

        def unpack_rims(block):
            return jnp.concatenate([block, pltpu.roll(block, 8, 1)], axis=0)

        loads[0].wait()
        block = coarse[...]
        block = jnp.concatenate([block[:, p, q, :] for q in (0, 1) for p in (0, 1)], axis=1)
        p0[...] = block
        p0_rim[...] = pack_rims(block)
        pl.semaphore_wait(barrier, expected)

        def round_xz(level_src, level_dst, rim_src, rim_dst, send_sems, recv_sems):
            copies = []
            for d in ROUND + LEVEL:
                back = (-d[0], -d[1])
                i = XZ.index(back)
                if d[1] == 0:
                    src, dst = level_src(d[0]), level_dst.at[LEVEL.index(back)]
                else:
                    src, dst = rim_src(d[0]), rim_dst.at[ROUND.index(back)]
                copies.append(send(src, dst, send_sems.at[i], recv_sems.at[i], at_xz(d)))
            return copies

        x_sends = round_xz(lambda d: p0, xr, lambda d: p0_rim, rim_r, xf_s, xf_r)
        for c in x_sends:
            c.start()

        for c in loads[1:7]:
            c.wait()
        w_own, w_other = edge_in[:, 0:16], edge_in[:, 16:32]
        col_x, col_y, col_z = edge_in[:, 32:33], edge_in[:, 33:34], edge_in[:, 34:35]
        n_own, n_gathered = node_in[:, 0:16], node_in[:, 16:32]
        eye = ones_where(iota((16, 16), 0) == iota((16, 16), 1)).astype(BF16)
        delta = table[DELTA : DELTA + 16, :].astype(BF16)
        same_y = iota((128, 128), 0) % 8 == iota((128, 128), 1) % 8

        def transposed(w):
            return exact_mm(eye, split(w), NT)

        def widen(w):
            parts = []
            for part in split(w):
                left = dot(delta, part, (((0,), (0,)), ((), ()))).astype(BF16)
                parts.append(jnp.where(same_y, dot(left, delta), 0.0).astype(BF16))
            return tuple(parts)

        m1 = mm(split(n_gathered), split(edge_out[...]))
        m1_wide = widen(m1)
        n_back = split(transposed(n_gathered))
        m1_back = widen(transposed(m1))
        out_back = widen(transposed(node_out[...]))
        mix = split(jnp.concatenate([w_own, n_own, w_other], axis=0))
        mix_back = split(jnp.concatenate([transposed(n_own), transposed(w_own), transposed(w_other)], axis=1))
        bias_rows = biases[...]
        bias_cols = exact_mm(eye, split(bias_rows), NT)
        b0_col, b1_row, b2_col = bias_cols[:, 0:1], bias_rows[1:2, :], bias_cols[:, 2:3]
        nb_col = jnp.sum(n_gathered * b1_row, axis=1, keepdims=True)
        maps = vertex_maps()
        gap_lane = ones_where((place == 20) & (group < 2))

        def blocks4(first):
            t = table[first : first + 32, :]
            zero = jnp.zeros((32, 128), F32)
            return split(
                jnp.concatenate(
                    [jnp.concatenate([t if i == j else zero for j in range(4)], axis=1) for i in range(4)], axis=0
                )
            )

        rz, rz_up, rz_down = blocks4(RZ), blocks4(RZ_UP), blocks4(RZ_DOWN)
        back_z = table[ALONG_Z : ALONG_Z + 128, :]
        group_z = iota((128, 128), 1) // 32

        def back_blocks_z(kind, n):
            return split(jnp.concatenate([jnp.where(group_z == i, spread(back_z, i - kind), 0.0) for i in range(n)], axis=0))

        to_rz, to_rz_up, to_rz_down = back_blocks_z(0, 4), back_blocks_z(1, 2), back_blocks_z(2, 2)

        loads[7].wait()
        for k in range(4):
            wide = jnp.concatenate([cot[:, 2 * k + i].reshape(128, 128) for i in (0, 1)], axis=1)
            u_all[:, :, 256 * k : 256 * k + 256] = mm(out_back, split(wide)).reshape(16, 8, 256)
        sum_all, sum_one = cot[:, 0], jnp.zeros((16, 8, 128), F32)
        for x in range(1, 8):
            sum_all = sum_all + cot[:, x]
            sum_one = sum_one + float(L1[x]) * cot[:, x]
        xf[:, :, 0:128] = sum_all - sum_one
        xf[:, :, 128:256] = sum_one

        for c in x_sends:
            c.wait_recv()
        pieces = []
        for d in WIDE:
            level = p0[...] if d == 0 else xr[LEVEL.index((d, 0))]
            rims = [unpack_rims(rim_r[ROUND.index((d, z))]) for z in (-1, 1)]
            pieces.append(jnp.concatenate([level] + rims, axis=1))
        summed = mm_exact(split(jnp.concatenate(pieces, axis=0)), jnp.concatenate(maps, axis=0))
        x_blocks = {d: summed[16 * i : 16 * i + 16, :] for i, d in enumerate(WIDE)}
        for q in (0, 1):
            acc = jnp.zeros((16, 128), F32)
            for vertex in (-1, 0, 1, 2):
                for d in (vertex - 1, vertex):
                    moved = spread(x_blocks[d], SLOT[vertex] - (2 * q + vertex - d))
                    acc = acc + jnp.where(group == SLOT[vertex], moved, 0.0)
            vx[q] = acc
        y_sends = []
        for d in STEPS:
            i = STEPS.index(-d)
            qs = pl.ds(0, 2) if abs(d) == 1 else pl.ds(1 if d == 2 else 0, 1)
            y_sends.append(send(vx.at[qs], yr.at[i, qs], yf_s.at[i], yf_r.at[i], at_y(d)))
        for c in y_sends:
            c.start()

        def exists(d):
            return jnp.where((iy + d >= 0) & (iy + d < n_y), 1.0, 0.0).astype(F32)

        there = {d: exists(d) for d in (-2, -1, 0, 1, 2)}
        wall_low, wall_high = 1.0 - there[-1], 1.0 - there[1]
        y_index = iota((8, 128), 0)
        count = 6.0 - wall_low * ones_where(y_index == 0) - wall_high * ones_where(y_index == 7)
        ly, up1, up2, down1, down0 = (table[PROFILES + 8 * i : PROFILES + 8 * i + 8, :] for i in range(5))

        for c in y_sends:
            c.wait_recv()

        def y_block(d, q):
            return vx[q] if d == 0 else yr[STEPS.index(d), q] * there[d]

        for q in (-1, 0, 1, 2):
            copies = jnp.maximum(there[q - 1] + there[q], 1.0)
            means[q + 1] = (y_block(q - 1, 1) + y_block(q, 0)) * (0.25 / copies)

        mixed = mm(mix, split(jnp.concatenate([means[i] for i in range(4)], axis=1)))
        for i in range(4):
            lanes = slice(128 * i, 128 * i + 128)
            if i in (1, 2):
                lhs_rows[48 * (i - 1) : 48 * (i - 1) + 32, :] = mixed[0:32, lanes]
                lhs_rows[48 * (i - 1) + 32 : 48 * i, :] = mixed[32:48, lanes] + col_z * gap_lane
            else:
                first = 96 if i == 0 else 112
                lhs_rows[first : first + 16, :] = mixed[32:48, lanes]
        along = mm(split(lhs_rows[...]), rz)
        other01 = split(jnp.concatenate([lhs_rows[32:48, :], lhs_rows[80:96, :]], axis=0))
        along_up = mm(other01, (rz_up[0][:, 0:256], rz_up[1][:, 0:256]))
        along_down = mm(other01, (rz_down[0][:, 0:256], rz_down[1][:, 0:256]))

        def vertex_rows(field, q, vertex):
            first = {0: 0, 1: 48}[q] + 16 * field if q in (0, 1) else (96 if q == -1 else 112)
            s = SLOT[vertex]
            return along[first : first + 16, 128 * s : 128 * s + 128]

        def next_rows(source, q, vertex):
            return source[16 * q : 16 * q + 16, 128 * vertex : 128 * vertex + 128]

        def put(field, x, value):
            rows[pl.ds(128 * field + x, 16, stride=8), :] = value

        def line(a, b, t):
            return a + t * (b - a)

        for x in range(8):
            t = float(L1[x])
            here = float(T[x]) * col_x
            own = [
                (line(vertex_rows(0, q, 0), vertex_rows(0, q, 1), t) + (b0_col - here - (2 * q - 1.0) * col_y)) * LOG2E
                for q in (0, 1)
            ]
            put(0, x, own[0])
            put(1, x, own[1] - own[0])
            other = {
                q: (line(vertex_rows(2, q, 0), vertex_rows(2, q, 1), t) + (here + (2 * q - 1.0) * col_y)) * LOG2E
                for q in (-1, 0, 1, 2)
            }
            put(2, x, other[0])
            put(3, x, other[1] - other[0])
            put(5, x, (other[2] - other[0]) * there[1] + ABSENT * wall_high)
            put(6, x, (other[-1] - other[0]) * there[-1] + ABSENT * wall_low)
            for f, source in ((7, along_up), (9, along_down)):
                z = [
                    (line(next_rows(source, q, 0), next_rows(source, q, 1), t) + (here + (2 * q - 1.0) * col_y)) * LOG2E
                    for q in (0, 1)
                ]
                put(f, x, z[0])
                put(f + 1, x, z[1] - z[0])
            hn = [line(vertex_rows(1, q, 0), vertex_rows(1, q, 1), t) for q in (0, 1)]
            put(11, x, hn[0] + b2_col)
            put(12, x, hn[1] - hn[0])
        put(13, 0, jnp.broadcast_to(nb_col, (16, 128)))
        for side, (a, b, t, at) in enumerate(((-1, 0, float(L1[6]), float(T[6]) - 2.0), (1, 2, float(L1[1]), float(T[1]) + 2.0))):
            other = [
                (line(vertex_rows(2, q, a), vertex_rows(2, q, b), t) + (at * col_x + (2 * q - 1.0) * col_y)) * LOG2E
                for q in (0, 1)
            ]
            put(4, 2 * side, other[0])
            put(4, 2 * side + 1, other[1] - other[0])

        def forward(c, carry):
            def row(field, x):
                return rows[pl.ds(128 * field + 8 * c + x, 1), :]

            other = [row(4, 0) + ly * row(4, 1)]
            counted = count * row(13, 0)
            for x in range(8):
                other.append(row(2, x) + ly * row(3, x))
            other.append(row(4, 2) + ly * row(4, 3))
            for x in range(8):
                own = row(0, x) + ly * row(1, x)
                a, d = row(2, x), row(3, x)
                senders = (
                    other[x + 2],
                    other[x],
                    a + up1 * d + up2 * row(5, x),
                    a + down1 * d + down0 * row(6, x),
                    row(7, x) + ly * row(8, x),
                    row(9, x) + ly * row(10, x),
                )
                tops, decays = None, None
                for k, sender in enumerate(senders):
                    z = own + sender
                    decay = jnp.exp2(jnp.minimum(z, 0.0))
                    top = jnp.maximum(z, 0.0)
                    e_all[k, x, c] = decay
                    tops = top if tops is None else tops + top
                    decays = decay if decays is None else decays + decay
                e_sum[x, c] = decays
                s_all[c, :, 128 * x : 128 * x + 128] = LN2 * tops + (decays - count)
                hn_all[c, :, 128 * x : 128 * x + 128] = row(11, x) + ly * row(12, x) + counted
            return carry

        lax.fori_loop(0, 16, forward, 0)

        outer_out = jnp.zeros((128, 128), F32)
        outer_in = jnp.zeros((128, 128), F32)
        dh_all = jnp.zeros((16, 8, 128), F32)
        dh_one = jnp.zeros((16, 8, 128), F32)
        for k in range(4):
            lanes = slice(256 * k, 256 * k + 256)
            s = split(s_all[:, :, lanes].reshape(128, 256))
            h = mm(m1_wide, s) + hn_all[:, :, lanes].reshape(128, 256)
            decay = jnp.exp(jnp.minimum(h, 0.0))
            a = jnp.maximum(h, 0.0) + (decay - 1.0)
            dh = decay * u_all[:, :, lanes].reshape(128, 256)
            dh_parts = split(dh)
            g_all[:, :, lanes] = mm(m1_back, dh_parts).reshape(16, 8, 256)
            wide = jnp.concatenate([cot[:, 2 * k + i].reshape(128, 128) for i in (0, 1)], axis=1)
            outer_out = outer_out + mm(split(wide), split(a), NT)
            outer_in = outer_in + mm(dh_parts, s, NT)
            for i in (0, 1):
                part = dh[:, 128 * i : 128 * i + 128].reshape(16, 8, 128)
                dh_all = dh_all + part
                dh_one = dh_one + float(L1[2 * k + i]) * part
        xf[:, :, 256:384] = dh_all - dh_one
        xf[:, :, 384:512] = dh_one

        def backward(c, carry):
            g = [g_all[c, :, 128 * x : 128 * x + 128] for x in range(8)]
            own = [g[x] * e_sum[x, c] for x in range(8)]

            def bz(k, x):
                return g[x] * e_all[k, x, c]

            def save(i, value):
                xf[c, :, 128 * i : 128 * i + 128] = value

            def reduce(first, values):
                everything, one = values[0], float(L1[1]) * values[1]
                for x in range(1, 8):
                    everything = everything + values[x]
                for x in range(2, 8):
                    one = one + float(L1[x]) * values[x]
                save(first, everything - one)
                save(first + 1, one)

            reduce(4, own)
            ups = [bz(0, x) for x in range(8)]
            downs = [bz(1, x) for x in range(8)]
            acc = GAP_UP[0] * ups[0] + GAP_DOWN[0] * downs[0]
            for x in range(1, 8):
                acc = acc + GAP_UP[x] * ups[x] + GAP_DOWN[x] * downs[x]
            save(6, acc)
            at = [downs[1]] + [ups[x - 1] + downs[x + 1] for x in range(1, 7)] + [ups[6]]
            everything, one = at[0], float(L1[1]) * at[1]
            for x in range(1, 8):
                everything = everything + at[x]
            for x in range(2, 8):
                one = one + float(L1[x]) * at[x]
            save(7, everything - one + float(L1[6]) * downs[0])
            save(8, one + float(L0[1]) * ups[7])
            save(9, float(L0[6]) * downs[0])
            save(10, float(L1[1]) * ups[7])
            for k in range(4):
                reduce(11 + 2 * k, [bz(2 + k, x) for x in range(8)])
            return carry

        lax.fori_loop(0, 16, backward, 0)

        def along_z(first, n, by):
            return mm(
                split(xf[:, :, 128 * first : 128 * (first + n)].reshape(128, 128 * n)),
                (by[0][0 : 128 * n, :], by[1][0 : 128 * n, :]),
            )

        z1 = along_z(0, 4, to_rz)
        z2 = along_z(4, 3, to_rz)
        z3 = along_z(7, 4, to_rz) + along_z(15, 2, to_rz_up) + along_z(17, 2, to_rz_down)
        z4 = along_z(11, 4, to_rz)
        counting = (
            6.0 * table[DELTA : DELTA + 16, :]
            - wall_low * table[DELTA + 16 : DELTA + 32, :]
            - wall_high * table[DELTA + 32 : DELTA + 48, :]
        )
        left = split(jnp.concatenate([table[Y_STD : Y_STD + 32, :], counting], axis=0))
        std = mm(left, split(jnp.concatenate([z1, z2, z3], axis=1)))
        nxt = mm(split(table[Y_NEXT : Y_NEXT + 160, :]), split(z4))

        low_half, low_lanes = group < 2, ones_where(group < 2)
        fields = {}
        for q in (0, 1):
            r = slice(16 * q, 16 * q + 16)
            fields[q] = (std[r, 0:128], std[r, 128:256], std[r, 256:384])
        others = {}
        for q in (-1, 0, 1, 2):
            r_up = slice(16 * (q + 1), 16 * (q + 1) + 16)
            r_down = slice(64 + 16 * (q + 1), 64 + 16 * (q + 1) + 16)
            both = jnp.where(low_half, nxt[r_up, :] + pltpu.roll(nxt[r_down, :], 64, 1), 0.0)
            others[q] = both + fields[q][2] if q in (0, 1) else both

        summed_out = jnp.where(same_y, outer_out, 0.0)
        summed_in = jnp.where(same_y, outer_in, 0.0)
        big = exact_mm(delta, split(jnp.concatenate([summed_out, summed_in], axis=1)))
        r2, c2 = iota((128, 256), 0), iota((128, 256), 1)
        placing = ones_where((c2 // 128 * 16 + c2 % 128 // 8) == r2).astype(BF16)
        part = mm_exact(split(big), placing, NT)
        r8, l8 = iota((8, 128), 0), iota((8, 128), 1)

        def marked(r, mask):
            return ones_where((r8 == r) & mask)

        def right(first, rows16, special):
            pieces = []
            if rows16 is None:
                pieces.append(jnp.zeros((80, 128), F32))
            else:
                if first > 0:
                    pieces.append(jnp.zeros((first, 128), F32))
                pieces.append(rows16)
                if first < 64:
                    pieces.append(jnp.zeros((64 - first, 128), F32))
            pieces += [special, jnp.zeros((40, 128), F32)]
            return jnp.concatenate(pieces, axis=0)

        lefts, rights = [], []
        none8 = jnp.zeros((8, 128), F32)
        for q in (-1, 0, 1, 2):
            m = means[q + 1]
            if q in (0, 1):
                lefts.append(fields[q][0])
                rights.append(right(32, jnp.where(low_half, 0.0, pltpu.roll(m, 64, 1)), marked(4, l8 >= 64)))
                lefts.append(fields[q][1])
                rights.append(right(48, m * low_lanes, marked(3, l8 < 64) + marked(0, (l8 >= 64) & (l8 < 96))))
            lefts.append(others[q])
            rights.append(right(64, m, marked(2, (l8 % 32 == 20) & (l8 < 64)) if q in (0, 1) else none8))
        lefts += [std[32:48, 0:128], nxt[128:144, :], nxt[144:160, :]]
        rights += [
            right(0, None, marked(5, l8 >= 64)),
            right(0, None, marked(1, l8 < 64)),
            right(0, None, marked(1, l8 >= 64)),
        ]
        payload[...] = part + mm(split(jnp.concatenate(lefts, axis=1)), split(jnp.concatenate(rights, axis=1)), NT)

        to_first = send(total, total, cast_s.at[0], cast_r, sibling)
        to_root = send(payload, col_slots.at[member], col_s, col_r.at[member], column_root)

        @pl.when(jnp.logical_not(is_root))
        def _():
            to_root.start()

        zero = jnp.zeros((16, 128), F32)
        stacked = []
        for q in (-1, 0, 1, 2):
            if q in (0, 1):
                dh_q = jnp.where(low_half, pltpu.roll(fields[q][0], 64, 1), 0.0)
                own_q = jnp.where(low_half, fields[q][1], 0.0)
            else:
                dh_q, own_q = zero, zero
            stacked.append(jnp.concatenate([dh_q, own_q, others[q]], axis=0))
        back = mm(mix_back, split(jnp.concatenate(stacked, axis=1)))
        for q in (-1, 0, 1, 2):
            value = back[:, 128 * (q + 1) : 128 * (q + 2)]
            if q in (0, 1):
                value = value + jnp.where(low_half, fields[q][0], 0.0)
            gm[q + 1] = value
        y_back = []
        for d in STEPS:
            i = STEPS.index(-d)
            if abs(d) == 1:
                src, dst = gm.at[pl.ds(2 if d == 1 else 0, 2)], yb.at[i]
            else:
                src, dst = gm.at[pl.ds(3 if d == 2 else 0, 1)], yb.at[i, pl.ds(0 if d == 2 else 1, 1)]
            y_back.append(send(src, dst, yb_s.at[i], yb_r.at[i], at_y(d)))
        for c in y_back:
            c.start()

        edge_place = (place[0:8] < 2) | (place[0:8] == 17) | (place[0:8] == 18)

        def pack_back(block):
            return jnp.where(edge_place, block[0:8, :], pltpu.roll(block[8:16, :], 8, 1))

        def unpack_back(block):
            return jnp.concatenate([block, pltpu.roll(block, 120, 1)], axis=0)

        for c in y_back:
            c.wait_recv()
        own_rows = []
        for q in (0, 1):
            value = gm[q + 1]
            for d in (-2, -1, 1, 2):
                if (d, q) not in ((-2, 1), (2, 0)):
                    value = value + yb[STEPS.index(d), q] * there[d]
            own_rows.append(value)
        for i, d in enumerate(WIDE):
            value = jnp.zeros((16, 128), F32)
            for q in (0, 1):
                for p in (0, 1):
                    if p + d in SLOT:
                        moved = spread(own_rows[q], 2 * q + p - SLOT[p + d])
                        value = value + jnp.where(group == 2 * q + p, moved, 0.0)
            back_blocks[i] = value
            back_rims[i] = pack_back(value)
        x_back = round_xz(
            lambda d: back_blocks.at[WIDE.index(d)], xb, lambda d: back_rims.at[WIDE.index(d)], rim_b, xb_s, xb_r
        )
        for c in x_back:
            c.start()

        my_place = (ix // Z_LOW) * n_z + iz
        to_plane = [
            send(plane_slots.at[my_place], plane_slots.at[my_place], plane_s.at[k], plane_r.at[k], in_plane(k))
            for k in range(1, n_plane)
        ]

        @pl.when(is_root)
        def _():
            value = payload[...]
            for k in range(CORES * n_layers):
                if k != 1:
                    send(payload, col_slots.at[k], col_s, col_r.at[k], sibling).wait_recv()
                    value = value + col_slots[k]
            plane_slots[my_place] = value
            for c in to_plane:
                c.start()

        for c in x_back:
            c.wait_recv()
        level = back_blocks[WIDE.index(0)]
        for i in range(len(LEVEL)):
            level = level + xb[i]
        sides = []
        for z in (-1, 1):
            value = rim_b[ROUND.index((-2, z))]
            for d in WIDE[1:]:
                value = value + rim_b[ROUND.index((d, z))]
            sides.append(unpack_back(value))
        level, sides = split(level), [split(v) for v in sides]
        value = mm_exact(level, maps[0], NT) + mm_exact(sides[0], maps[2], NT) + mm_exact(sides[1], maps[1], NT)
        value = value * jnp.where(group < 2, 0.25 / (1.0 + there[-1]), 0.25 / (1.0 + there[1]))
        for q in (0, 1):
            for p in (0, 1):
                g_coarse[:, p, q, :] = value[:, 32 * (2 * q + p) : 32 * (2 * q + p) + 32]
        saves[0].start()

        half = n_layers // 2
        up_column = [send(total, total, cast_s.at[k], cast_r, in_column(k, 1)) for k in range(1, n_layers)]
        is_helper = (core == 0) & (layer == 0)

        @pl.when(is_root)
        def _():
            for k, c in enumerate(to_plane):
                c.wait_recv()
            value = plane_slots[0]
            for k in range(1, n_plane):
                value = value + plane_slots[k]
            total[...] = value
            for c in [to_first] + up_column[0 : half - 1]:
                c.start()

        @pl.when(jnp.logical_not(is_root))
        def _():
            to_first.wait_recv()

        @pl.when(on_core1 & (layer != 0))
        def _():
            to_first.start()

        @pl.when(is_helper)
        def _():
            for c in up_column[half - 1 :]:
                c.start()

        sums = total[...] * factor
        g_node_out[...] = sums[:, 0:16]
        g_edge_in[...] = sums[:, 48:83]
        back = mm(n_back, split(sums))
        g_edge_out[...] = back[:, 16:32]
        g_node_in[:, 0:16] = sums[:, 32:48]
        g_node_in[:, 16:32] = mm(split(sums[:, 16:32]), split(edge_out[...]), NT) + sums[:, 85:86] * biases[1:2, :]
        r, c = iota((8, 256), 0), iota((8, 256), 1)
        pick = ones_where(((r == 0) & (c == 83)) | ((r == 1) & (c == 128 + 85)) | ((r == 2) & (c == 84))).astype(BF16)
        g_biases[...] = exact_mm(pick, split(jnp.concatenate([sums, back], axis=1)), NT)[0:3, :]
        for c in saves[1:]:
            c.start()

        for c in x_sends + y_sends + y_back + x_back:
            c.wait_send()

        @pl.when(on_core1)
        def _():
            to_first.wait_send()

        @pl.when(jnp.logical_not(is_root))
        def _():
            to_root.wait_send()

        @pl.when(is_root)
        def _():
            for c in to_plane + up_column[0 : half - 1]:
                c.wait_send()

        @pl.when(is_helper)
        def _():
            for c in up_column[half - 1 :]:
                c.wait_send()

        for c in saves:
            c.wait()

    block = pltpu.VMEM((16, 128), F32)

    def blocks(*lead):
        return pltpu.VMEM(lead + (16, 128), F32)

    dma = pltpu.SemaphoreType.DMA
    scratch = [
        *(pltpu.VMEM(s, F32) for s in RESULTS),
        pltpu.VMEM((16, 2, 2, 32), F32),
        pltpu.VMEM((16, 8, 8, 128), F32),
        pltpu.VMEM((16, 35), F32),
        pltpu.VMEM((16, 16), F32),
        pltpu.VMEM((16, 32), F32),
        pltpu.VMEM((16, 16), F32),
        pltpu.VMEM((3, 16), F32),
        pltpu.VMEM((TABLE_ROWS, 128), F32),
        block,
        pltpu.VMEM((8, 128), F32),
        blocks(len(LEVEL)),
        pltpu.VMEM((len(ROUND), 8, 128), F32),
        blocks(2),
        blocks(4, 2),
        blocks(4),
        pltpu.VMEM((128, 128), F32),
        pltpu.VMEM((14 * 128, 128), F32),
        pltpu.VMEM((6, 8, 16, 8, 128), F32),
        pltpu.VMEM((8, 16, 8, 128), F32),
        pltpu.VMEM((16, 8, 1024), F32),
        pltpu.VMEM((16, 8, 1024), F32),
        pltpu.VMEM((16, 8, 1024), F32),
        pltpu.VMEM((16, 8, 1024), F32),
        pltpu.VMEM((16, 8, 19 * 128), F32),
        blocks(4),
        blocks(4, 2),
        blocks(len(WIDE)),
        pltpu.VMEM((len(WIDE), 8, 128), F32),
        blocks(len(LEVEL)),
        pltpu.VMEM((len(ROUND), 8, 128), F32),
        block,
        blocks(CORES * n_layers),
        blocks(n_plane),
        block,
        dma((8,)),
        dma((len(XZ),)), dma((len(XZ),)), dma((4,)), dma((4,)), dma((4,)), dma((4,)), dma((len(XZ),)), dma((len(XZ),)),
        dma, dma((CORES * n_layers,)), dma((n_plane,)), dma((n_plane,)), dma((n_layers,)), dma, dma((6,)),
    ]
    return pl.pallas_call(
        kernel,
        out_shape=[jax.ShapeDtypeStruct(s, F32) for s in RESULTS],
        in_specs=[pl.BlockSpec(memory_space=pltpu.HBM)] * 8,
        out_specs=[pl.BlockSpec(memory_space=pltpu.HBM)] * 6,
        scratch_shapes=scratch,
        compiler_params=pltpu.CompilerParams(
            collective_id=0, has_side_effects=True, vmem_limit_bytes=60 * 1024 * 1024
        ),
    )


def make_hand_over():
    def kernel(*refs):
        sources, outs, buffers, sem = refs[0:6], refs[6:12], refs[12:18], refs[18]
        reads = [pltpu.make_async_copy(sources[i], buffers[i], sem.at[0, i]) for i in range(6)]
        writes = [pltpu.make_async_copy(buffers[i], outs[i], sem.at[1, i]) for i in range(6)]
        for c in reads:
            c.start()
        for read, write in zip(reads, writes):
            read.wait()
            write.start()
        for c in writes:
            c.wait()

    return pl.pallas_call(
        kernel,
        out_shape=[jax.ShapeDtypeStruct(s, F32) for s in RESULTS],
        in_specs=[pl.BlockSpec(memory_space=pltpu.HBM)] * 6,
        out_specs=[pl.BlockSpec(memory_space=pltpu.HBM)] * 6,
        scratch_shapes=[pltpu.VMEM(s, F32) for s in RESULTS] + [pltpu.SemaphoreType.DMA((2, 6))],
        compiler_params=pltpu.CompilerParams(vmem_limit_bytes=60 * 1024 * 1024),
    )


def solution(mesh):
    sizes = (mesh.shape["gx"], mesh.shape["gy"], mesh.shape["gz"])
    table = make_table()

    def on_device(coarse, cotangent, edge_in, edge_out, node_in, node_out, biases):
        nodes = cotangent.shape[1] * cotangent.shape[2] * cotangent.shape[3] * sizes[0] * sizes[1] * sizes[2]
        results = make_main(sizes, float(nodes) ** -0.5)(
            coarse, cotangent, edge_in, edge_out, node_in, node_out, biases, jnp.asarray(table)
        )
        return tuple(make_hand_over()(*results))

    placed = (P(None, "gx", "gy", "gz"), P(None, "gx", "gy", "gz"), P(), P(), P(), P(), P())
    return jax.shard_map(
        on_device,
        mesh=mesh,
        in_specs=placed,
        out_specs=(P(None, "gx", "gy", "gz"), P(), P(), P(), P(), P()),
        check_vma=False,
    )
```

```python
import jax
import jax.numpy as jnp
import numpy as np
from jax import lax
from jax.experimental import pallas as pl
from jax.experimental.pallas import tpu as pltpu
from jax.sharding import PartitionSpec as P

MESH = pl.DeviceIdType.MESH
F32 = jnp.float32
BF16 = jnp.bfloat16
T = np.array(
    [
        -1.0,
        -0.8717401485096066,
        -0.5917001814331423,
        -0.2092992179024789,
        0.2092992179024789,
        0.5917001814331423,
        0.8717401485096066,
        1.0,
    ]
)
L0, L1 = (1.0 - T) / 2.0, (1.0 + T) / 2.0
LOG2E = float(np.log2(np.e))
LN2 = float(np.log(2.0))
GAP_UP = [float(T[i + 1] - T[i]) if i < 7 else float(T[1] - T[0]) for i in range(8)]
GAP_DOWN = [float(T[i - 1] - T[i]) if i > 0 else float(T[6] - T[7]) for i in range(8)]
Z_LOW = 4
CORES = 2
ABSENT = -1.0e5
SLOT = {0: 0, 1: 1, -1: 2, 2: 3}
STEPS = (-2, -1, 1, 2)
WIDE = (-2, -1, 0, 1, 2)
XZ = tuple((x, z) for x in WIDE for z in (-1, 0, 1) if (x, z) != (0, 0))
ROUND = tuple(d for d in XZ if d[1] != 0)
LEVEL = tuple(d for d in XZ if d[1] == 0)

RZ, RZ_UP, RZ_DOWN, PROFILES, Y_STD, Y_NEXT, Y_GAP, DELTA = 0, 32, 64, 96, 136, 168, 296, 328
ALONG_Z = 376
TABLE_ROWS = 504


def make_table():
    table = np.zeros((TABLE_ROWS, 128))
    for lane in range(128):
        e, a = divmod(lane, 8)
        table[RZ + e + 1, lane] += L0[a]
        table[RZ + e + 2, lane] += L1[a]
        if a < 7:
            table[RZ_UP + e + 1, lane] += L0[a + 1]
            table[RZ_UP + e + 2, lane] += L1[a + 1]
        else:
            table[RZ_UP + e + 2, lane] += L0[1]
            table[RZ_UP + e + 3, lane] += L1[1]
        if a > 0:
            table[RZ_DOWN + e + 1, lane] += L0[a - 1]
            table[RZ_DOWN + e + 2, lane] += L1[a - 1]
        else:
            table[RZ_DOWN + e, lane] += L0[6]
            table[RZ_DOWN + e + 1, lane] += L1[6]
        table[RZ_UP + 20, lane] = GAP_UP[a]
        table[RZ_DOWN + 20, lane] = GAP_DOWN[a]
    up = np.zeros((4, 8))
    down = np.zeros((4, 8))
    for y in range(8):
        if y < 7:
            up[1, y], up[2, y] = L0[y + 1], L1[y + 1]
        else:
            up[2, y], up[3, y] = L0[1], L1[1]
        if y > 0:
            down[1, y], down[2, y] = L0[y - 1], L1[y - 1]
        else:
            down[0, y], down[1, y] = L0[6], L1[6]
    for i, profile in enumerate((L1, up[2], up[3], down[2], down[0])):
        table[PROFILES + 8 * i : PROFILES + 8 * i + 8] = profile[:, None]
    for c in range(16):
        for y in range(8):
            lane = 8 * c + y
            table[Y_STD + c, lane] = L0[y]
            table[Y_STD + 16 + c, lane] = L1[y]
            for q in range(4):
                table[Y_NEXT + 16 * q + c, lane] = up[q, y]
                table[Y_NEXT + 64 + 16 * q + c, lane] = down[q, y]
            table[Y_GAP + c, lane] = GAP_UP[y]
            table[Y_GAP + 16 + c, lane] = GAP_DOWN[y]
            table[DELTA + c, lane] = 1.0
            table[DELTA + 16 + c, lane] = 1.0 if y == 0 else 0.0
            table[DELTA + 32 + c, lane] = 1.0 if y == 7 else 0.0
    table[ALONG_Z : ALONG_Z + 128, 0:96] = table[RZ : RZ + 96].T
    return table.astype(np.float32)


RESULTS = ((16, 2, 2, 32), (16, 35), (16, 16), (16, 32), (16, 16), (3, 16))
NN = (((1,), (0,)), ((), ()))
NT = (((1,), (1,)), ((), ()))


def dot(a, b, dims=NN):
    return lax.dot_general(a, b, dims, preferred_element_type=F32)


def split(a):
    high = a.astype(BF16)
    return high, (a - high.astype(F32)).astype(BF16)


def mm(a, b, dims=NN):
    (ah, al), (bh, bl) = a, b
    at = dims[0][1][0]
    return dot(jnp.concatenate([ah, ah, al], axis=1), jnp.concatenate([bh, bl, bh], axis=at), dims)


def mm_exact(a, b, dims=NN):
    return dot(jnp.concatenate([a[0], a[1]], axis=1), jnp.concatenate([b, b], axis=dims[0][1][0]), dims)


def exact_mm(a, b, dims=NN):
    return dot(a, b[0], dims) + dot(a, b[1], dims)


def iota(shape, dim):
    return lax.broadcasted_iota(jnp.int32, shape, dim)


def ones_where(mask):
    return jnp.where(mask, 1.0, 0.0).astype(F32)


def spread(a, k):
    k = k % 4
    return a if k == 0 else pltpu.roll(a, 32 * k, 1)


def vertex_maps():
    row, col = iota((128, 128), 0), iota((128, 128), 1)
    layer, vertex = row % 32, col % 32 - 1
    same = (row // 32 == col // 32) & (vertex < 18)
    maps = []
    for shift in (0, 16, -16):
        v = vertex + shift
        maps.append(ones_where(same & ((layer == 2 * v - 1) | (layer == 2 * v))).astype(BF16))
    return maps


def make_main(sizes, factor):
    n_x, n_y, n_z = sizes
    z_high = n_y // CORES
    n_layers = z_high * Z_LOW
    n_cols = n_x // Z_LOW
    n_plane = n_cols * n_z

    def kernel(
        coarse_in, cot_in, edge_in_in, edge_out_in, node_in_in, node_out_in, biases_in, table_in,
        *refs,
    ):
        results, outs, refs = refs[0:6], refs[6:12], refs[12:]
        (
        coarse, cot, edge_in, edge_out, node_in, node_out, biases, table, p0, p0_rim, xr, rim_r, vx, yr, means, lhs_rows, rows, e_all, e_sum, s_all, hn_all, u_all, g_all, xf,
        gm, yb, back_blocks, back_rims, xb, rim_b, payload, col_slots, plane_slots, total,
        load_sem, xf_s, xf_r, yf_s, yf_r, yb_s, yb_r, xb_s, xb_r,
        col_s, col_r, plane_s, plane_r, cast_s, cast_r, save_sem,
        ) = refs
        g_coarse, g_edge_in, g_edge_out, g_node_in, g_node_out, g_biases = outs
        saves = [pltpu.make_async_copy(src, dst, save_sem.at[i]) for i, (src, dst) in enumerate(zip(outs, results))]
        ix, iy, iz = lax.axis_index("gx"), lax.axis_index("gy"), lax.axis_index("gz")
        low = lax.rem(ix, Z_LOW)
        core = lax.rem(iy, CORES)
        layer = (iy // CORES) * Z_LOW + low
        on_core1 = core == 1
        is_root = on_core1 & (layer == 0)
        member = layer * CORES + core

        def at_xz(d):
            return (lax.rem(ix + (d[0] + n_x), n_x), iy, lax.rem(iz + (d[1] + n_z), n_z))

        def at_y(d):
            return (ix, lax.rem(iy + (d + n_y), n_y), iz)

        sibling = (ix, iy + 1 - 2 * core, iz)
        column_root = (ix - low, 1, iz)

        def in_column(k, c):
            return (ix + k % Z_LOW, (k // Z_LOW) * CORES + c, iz)

        def in_plane(k):
            col, row = k // n_z, k % n_z
            return (lax.rem(ix + Z_LOW * col, n_x), iy, lax.rem(iz + row, n_z))

        def send(src, dst, send_sem, recv_sem, device):
            return pltpu.make_async_remote_copy(
                src_ref=src, dst_ref=dst, send_sem=send_sem, recv_sem=recv_sem, device_id=device, device_id_type=MESH
            )

        def signal(device):
            pl.semaphore_signal(barrier, inc=1, device_id=device, device_id_type=MESH)

        loads = [
            pltpu.make_async_copy(src, dst, load_sem.at[i])
            for i, (src, dst) in enumerate(
                (
                    (coarse_in, coarse),
                    (edge_in_in, edge_in),
                    (edge_out_in, edge_out),
                    (node_in_in, node_in),
                    (node_out_in, node_out),
                    (biases_in, biases),
                    (table_in, table),
                    (cot_in, cot),
                )
            )
        ]
        loads[0].start()
        barrier = pltpu.get_barrier_semaphore()
        for d in XZ:
            signal(at_xz(d))
        for d in STEPS:
            signal(at_y(d))

        @pl.when(is_root)
        def _():
            for k in range(1, n_layers):
                for c in range(CORES):
                    signal(in_column(k, c))
            for k in range(1, n_plane):
                signal(in_plane(k))

        for c in loads[1:]:
            c.start()
        expected = len(XZ) + len(STEPS) + jnp.where(layer != 0, 1, 0) + jnp.where(is_root, n_plane - 1, 0)

        lane = iota((16, 128), 1)
        group, place = lane // 32, lane % 32
        rim = (place[0:8] < 3) | (place[0:8] >= 29)

        def pack_rims(block):
            return jnp.where(rim, block[0:8, :], pltpu.roll(block[8:16, :], 120, 1))

        def unpack_rims(block):
            return jnp.concatenate([block, pltpu.roll(block, 8, 1)], axis=0)

        loads[0].wait()
        block = coarse[...]
        block = jnp.concatenate([block[:, p, q, :] for q in (0, 1) for p in (0, 1)], axis=1)
        p0[...] = block
        p0_rim[...] = pack_rims(block)
        pl.semaphore_wait(barrier, expected)

        def round_xz(level_src, level_dst, rim_src, rim_dst, send_sems, recv_sems):
            copies = []
            for d in ROUND + LEVEL:
                back = (-d[0], -d[1])
                i = XZ.index(back)
                if d[1] == 0:
                    src, dst = level_src(d[0]), level_dst.at[LEVEL.index(back)]
                else:
                    src, dst = rim_src(d[0]), rim_dst.at[ROUND.index(back)]
                copies.append(send(src, dst, send_sems.at[i], recv_sems.at[i], at_xz(d)))
            return copies

        x_sends = round_xz(lambda d: p0, xr, lambda d: p0_rim, rim_r, xf_s, xf_r)
        for c in x_sends:
            c.start()

        for c in loads[1:7]:
            c.wait()
        w_own, w_other = edge_in[:, 0:16], edge_in[:, 16:32]
        col_x, col_y, col_z = edge_in[:, 32:33], edge_in[:, 33:34], edge_in[:, 34:35]
        n_own, n_gathered = node_in[:, 0:16], node_in[:, 16:32]
        eye = ones_where(iota((16, 16), 0) == iota((16, 16), 1)).astype(BF16)
        delta = table[DELTA : DELTA + 16, :].astype(BF16)
        same_y = iota((128, 128), 0) % 8 == iota((128, 128), 1) % 8

        def transposed(w):
            return exact_mm(eye, split(w), NT)

        def widen(w):
            parts = []
            for part in split(w):
                left = dot(delta, part, (((0,), (0,)), ((), ()))).astype(BF16)
                parts.append(jnp.where(same_y, dot(left, delta), 0.0).astype(BF16))
            return tuple(parts)

        m1 = mm(split(n_gathered), split(edge_out[...]))
        m1_wide = widen(m1)
        n_back = split(transposed(n_gathered))
        m1_back = widen(transposed(m1))
        out_back = widen(transposed(node_out[...]))
        mix = split(jnp.concatenate([w_own, n_own, w_other], axis=0))
        mix_back = split(jnp.concatenate([transposed(n_own), transposed(w_own), transposed(w_other)], axis=1))
        bias_rows = biases[...]
        bias_cols = exact_mm(eye, split(bias_rows), NT)
        b0_col, b1_row, b2_col = bias_cols[:, 0:1], bias_rows[1:2, :], bias_cols[:, 2:3]
        nb_col = jnp.sum(n_gathered * b1_row, axis=1, keepdims=True)
        maps = vertex_maps()
        gap_lane = ones_where((place == 20) & (group < 2))

        def blocks4(first):
            t = table[first : first + 32, :]
            zero = jnp.zeros((32, 128), F32)
            return split(
                jnp.concatenate(
                    [jnp.concatenate([t if i == j else zero for j in range(4)], axis=1) for i in range(4)], axis=0
                )
            )

        rz, rz_up, rz_down = blocks4(RZ), blocks4(RZ_UP), blocks4(RZ_DOWN)
        back_z = table[ALONG_Z : ALONG_Z + 128, :]
        group_z = iota((128, 128), 1) // 32

        def back_blocks_z(kind, n):
            return split(jnp.concatenate([jnp.where(group_z == i, spread(back_z, i - kind), 0.0) for i in range(n)], axis=0))

        to_rz, to_rz_up, to_rz_down = back_blocks_z(0, 4), back_blocks_z(1, 2), back_blocks_z(2, 2)

        loads[7].wait()
        for k in range(4):
            wide = jnp.concatenate([cot[:, 2 * k + i].reshape(128, 128) for i in (0, 1)], axis=1)
            u_all[:, :, 256 * k : 256 * k + 256] = mm(out_back, split(wide)).reshape(16, 8, 256)
        sum_all, sum_one = cot[:, 0], jnp.zeros((16, 8, 128), F32)
        for x in range(1, 8):
            sum_all = sum_all + cot[:, x]
            sum_one = sum_one + float(L1[x]) * cot[:, x]
        xf[:, :, 0:128] = sum_all - sum_one
        xf[:, :, 128:256] = sum_one

        for c in x_sends:
            c.wait_recv()
        pieces = []
        for d in WIDE:
            level = p0[...] if d == 0 else xr[LEVEL.index((d, 0))]
            rims = [unpack_rims(rim_r[ROUND.index((d, z))]) for z in (-1, 1)]
            pieces.append(jnp.concatenate([level] + rims, axis=1))
        summed = mm_exact(split(jnp.concatenate(pieces, axis=0)), jnp.concatenate(maps, axis=0))
        x_blocks = {d: summed[16 * i : 16 * i + 16, :] for i, d in enumerate(WIDE)}
        for q in (0, 1):
            acc = jnp.zeros((16, 128), F32)
            for vertex in (-1, 0, 1, 2):
                for d in (vertex - 1, vertex):
                    moved = spread(x_blocks[d], SLOT[vertex] - (2 * q + vertex - d))
                    acc = acc + jnp.where(group == SLOT[vertex], moved, 0.0)
            vx[q] = acc
        y_sends = []
        for d in STEPS:
            i = STEPS.index(-d)
            qs = pl.ds(0, 2) if abs(d) == 1 else pl.ds(1 if d == 2 else 0, 1)
            y_sends.append(send(vx.at[qs], yr.at[i, qs], yf_s.at[i], yf_r.at[i], at_y(d)))
        for c in y_sends:
            c.start()

        def exists(d):
            return jnp.where((iy + d >= 0) & (iy + d < n_y), 1.0, 0.0).astype(F32)

        there = {d: exists(d) for d in (-2, -1, 0, 1, 2)}
        wall_low, wall_high = 1.0 - there[-1], 1.0 - there[1]
        y_index = iota((8, 128), 0)
        count = 6.0 - wall_low * ones_where(y_index == 0) - wall_high * ones_where(y_index == 7)
        ly, up1, up2, down1, down0 = (table[PROFILES + 8 * i : PROFILES + 8 * i + 8, :] for i in range(5))

        for c in y_sends:
            c.wait_recv()

        def y_block(d, q):
            return vx[q] if d == 0 else yr[STEPS.index(d), q] * there[d]

        for q in (-1, 0, 1, 2):
            copies = jnp.maximum(there[q - 1] + there[q], 1.0)
            means[q + 1] = (y_block(q - 1, 1) + y_block(q, 0)) * (0.25 / copies)

        mixed = mm(mix, split(jnp.concatenate([means[i] for i in range(4)], axis=1)))
        for i in range(4):
            lanes = slice(128 * i, 128 * i + 128)
            if i in (1, 2):
                lhs_rows[48 * (i - 1) : 48 * (i - 1) + 32, :] = mixed[0:32, lanes]
                lhs_rows[48 * (i - 1) + 32 : 48 * i, :] = mixed[32:48, lanes] + col_z * gap_lane
            else:
                first = 96 if i == 0 else 112
                lhs_rows[first : first + 16, :] = mixed[32:48, lanes]
        along = mm(split(lhs_rows[...]), rz)
        other01 = split(jnp.concatenate([lhs_rows[32:48, :], lhs_rows[80:96, :]], axis=0))
        along_up = mm(other01, (rz_up[0][:, 0:256], rz_up[1][:, 0:256]))
        along_down = mm(other01, (rz_down[0][:, 0:256], rz_down[1][:, 0:256]))

        def vertex_rows(field, q, vertex):
            first = {0: 0, 1: 48}[q] + 16 * field if q in (0, 1) else (96 if q == -1 else 112)
            s = SLOT[vertex]
            return along[first : first + 16, 128 * s : 128 * s + 128]

        def next_rows(source, q, vertex):
            return source[16 * q : 16 * q + 16, 128 * vertex : 128 * vertex + 128]

        def put(field, x, value):
            rows[pl.ds(128 * field + x, 16, stride=8), :] = value

        def line(a, b, t):
            return a + t * (b - a)

        for x in range(8):
            t = float(L1[x])
            here = float(T[x]) * col_x
            own = [
                (line(vertex_rows(0, q, 0), vertex_rows(0, q, 1), t) + (b0_col - here - (2 * q - 1.0) * col_y)) * LOG2E
                for q in (0, 1)
            ]
            put(0, x, own[0])
            put(1, x, own[1] - own[0])
            other = {
                q: (line(vertex_rows(2, q, 0), vertex_rows(2, q, 1), t) + (here + (2 * q - 1.0) * col_y)) * LOG2E
                for q in (-1, 0, 1, 2)
            }
            put(2, x, other[0])
            put(3, x, other[1] - other[0])
            put(5, x, (other[2] - other[0]) * there[1] + ABSENT * wall_high)
            put(6, x, (other[-1] - other[0]) * there[-1] + ABSENT * wall_low)
            for f, source in ((7, along_up), (9, along_down)):
                z = [
                    (line(next_rows(source, q, 0), next_rows(source, q, 1), t) + (here + (2 * q - 1.0) * col_y)) * LOG2E
                    for q in (0, 1)
                ]
                put(f, x, z[0])
                put(f + 1, x, z[1] - z[0])
            hn = [line(vertex_rows(1, q, 0), vertex_rows(1, q, 1), t) for q in (0, 1)]
            put(11, x, hn[0] + b2_col)
            put(12, x, hn[1] - hn[0])
        put(13, 0, jnp.broadcast_to(nb_col, (16, 128)))
        for side, (a, b, t, at) in enumerate(((-1, 0, float(L1[6]), float(T[6]) - 2.0), (1, 2, float(L1[1]), float(T[1]) + 2.0))):
            other = [
                (line(vertex_rows(2, q, a), vertex_rows(2, q, b), t) + (at * col_x + (2 * q - 1.0) * col_y)) * LOG2E
                for q in (0, 1)
            ]
            put(4, 2 * side, other[0])
            put(4, 2 * side + 1, other[1] - other[0])

        def forward(c, carry):
            def row(field, x):
                return rows[pl.ds(128 * field + 8 * c + x, 1), :]

            other = [row(4, 0) + ly * row(4, 1)]
            counted = count * row(13, 0)
            for x in range(8):
                other.append(row(2, x) + ly * row(3, x))
            other.append(row(4, 2) + ly * row(4, 3))
            for x in range(8):
                own = row(0, x) + ly * row(1, x)
                a, d = row(2, x), row(3, x)
                senders = (
                    other[x + 2],
                    other[x],
                    a + up1 * d + up2 * row(5, x),
                    a + down1 * d + down0 * row(6, x),
                    row(7, x) + ly * row(8, x),
                    row(9, x) + ly * row(10, x),
                )
                tops, decays = None, None
                for k, sender in enumerate(senders):
                    z = own + sender
                    decay = jnp.exp2(jnp.minimum(z, 0.0))
                    top = jnp.maximum(z, 0.0)
                    e_all[k, x, c] = decay
                    tops = top if tops is None else tops + top
                    decays = decay if decays is None else decays + decay
                e_sum[x, c] = decays
                s_all[c, :, 128 * x : 128 * x + 128] = LN2 * tops + (decays - count)
                hn_all[c, :, 128 * x : 128 * x + 128] = row(11, x) + ly * row(12, x) + counted
            return carry

        lax.fori_loop(0, 16, forward, 0, unroll=2)

        outer_out = jnp.zeros((128, 128), F32)
        outer_in = jnp.zeros((128, 128), F32)
        dh_all = jnp.zeros((16, 8, 128), F32)
        dh_one = jnp.zeros((16, 8, 128), F32)
        for k in range(4):
            lanes = slice(256 * k, 256 * k + 256)
            s = split(s_all[:, :, lanes].reshape(128, 256))
            h = mm(m1_wide, s) + hn_all[:, :, lanes].reshape(128, 256)
            decay = jnp.exp(jnp.minimum(h, 0.0))
            a = jnp.maximum(h, 0.0) + (decay - 1.0)
            dh = decay * u_all[:, :, lanes].reshape(128, 256)
            dh_parts = split(dh)
            g_all[:, :, lanes] = mm(m1_back, dh_parts).reshape(16, 8, 256)
            wide = jnp.concatenate([cot[:, 2 * k + i].reshape(128, 128) for i in (0, 1)], axis=1)
            outer_out = outer_out + mm(split(wide), split(a), NT)
            outer_in = outer_in + mm(dh_parts, s, NT)
            for i in (0, 1):
                part = dh[:, 128 * i : 128 * i + 128].reshape(16, 8, 128)
                dh_all = dh_all + part
                dh_one = dh_one + float(L1[2 * k + i]) * part
        xf[:, :, 256:384] = dh_all - dh_one
        xf[:, :, 384:512] = dh_one

        def backward(c, carry):
            g = [g_all[c, :, 128 * x : 128 * x + 128] for x in range(8)]
            own = [g[x] * e_sum[x, c] for x in range(8)]

            def bz(k, x):
                return g[x] * e_all[k, x, c]

            def save(i, value):
                xf[c, :, 128 * i : 128 * i + 128] = value

            def reduce(first, values):
                everything, one = values[0], float(L1[1]) * values[1]
                for x in range(1, 8):
                    everything = everything + values[x]
                for x in range(2, 8):
                    one = one + float(L1[x]) * values[x]
                save(first, everything - one)
                save(first + 1, one)

            reduce(4, own)
            ups = [bz(0, x) for x in range(8)]
            downs = [bz(1, x) for x in range(8)]
            acc = GAP_UP[0] * ups[0] + GAP_DOWN[0] * downs[0]
            for x in range(1, 8):
                acc = acc + GAP_UP[x] * ups[x] + GAP_DOWN[x] * downs[x]
            save(6, acc)
            at = [downs[1]] + [ups[x - 1] + downs[x + 1] for x in range(1, 7)] + [ups[6]]
            everything, one = at[0], float(L1[1]) * at[1]
            for x in range(1, 8):
                everything = everything + at[x]
            for x in range(2, 8):
                one = one + float(L1[x]) * at[x]
            save(7, everything - one + float(L1[6]) * downs[0])
            save(8, one + float(L0[1]) * ups[7])
            save(9, float(L0[6]) * downs[0])
            save(10, float(L1[1]) * ups[7])
            for k in range(4):
                reduce(11 + 2 * k, [bz(2 + k, x) for x in range(8)])
            return carry

        lax.fori_loop(0, 16, backward, 0, unroll=2)

        def along_z(first, n, by):
            return mm(
                split(xf[:, :, 128 * first : 128 * (first + n)].reshape(128, 128 * n)),
                (by[0][0 : 128 * n, :], by[1][0 : 128 * n, :]),
            )

        z1 = along_z(0, 4, to_rz)
        z2 = along_z(4, 3, to_rz)
        z3 = along_z(7, 4, to_rz) + along_z(15, 2, to_rz_up) + along_z(17, 2, to_rz_down)
        z4 = along_z(11, 4, to_rz)
        counting = (
            6.0 * table[DELTA : DELTA + 16, :]
            - wall_low * table[DELTA + 16 : DELTA + 32, :]
            - wall_high * table[DELTA + 32 : DELTA + 48, :]
        )
        left = split(jnp.concatenate([table[Y_STD : Y_STD + 32, :], counting], axis=0))
        std = mm(left, split(jnp.concatenate([z1, z2, z3], axis=1)))
        nxt = mm(split(table[Y_NEXT : Y_NEXT + 160, :]), split(z4))

        low_half, low_lanes = group < 2, ones_where(group < 2)
        fields = {}
        for q in (0, 1):
            r = slice(16 * q, 16 * q + 16)
            fields[q] = (std[r, 0:128], std[r, 128:256], std[r, 256:384])
        others = {}
        for q in (-1, 0, 1, 2):
            r_up = slice(16 * (q + 1), 16 * (q + 1) + 16)
            r_down = slice(64 + 16 * (q + 1), 64 + 16 * (q + 1) + 16)
            both = jnp.where(low_half, nxt[r_up, :] + pltpu.roll(nxt[r_down, :], 64, 1), 0.0)
            others[q] = both + fields[q][2] if q in (0, 1) else both

        summed_out = jnp.where(same_y, outer_out, 0.0)
        summed_in = jnp.where(same_y, outer_in, 0.0)
        big = exact_mm(delta, split(jnp.concatenate([summed_out, summed_in], axis=1)))
        r2, c2 = iota((128, 256), 0), iota((128, 256), 1)
        placing = ones_where((c2 // 128 * 16 + c2 % 128 // 8) == r2).astype(BF16)
        part = mm_exact(split(big), placing, NT)
        r8, l8 = iota((8, 128), 0), iota((8, 128), 1)

        def marked(r, mask):
            return ones_where((r8 == r) & mask)

        def right(first, rows16, special):
            pieces = []
            if rows16 is None:
                pieces.append(jnp.zeros((80, 128), F32))
            else:
                if first > 0:
                    pieces.append(jnp.zeros((first, 128), F32))
                pieces.append(rows16)
                if first < 64:
                    pieces.append(jnp.zeros((64 - first, 128), F32))
            pieces += [special, jnp.zeros((40, 128), F32)]
            return jnp.concatenate(pieces, axis=0)

        lefts, rights = [], []
        none8 = jnp.zeros((8, 128), F32)
        for q in (-1, 0, 1, 2):
            m = means[q + 1]
            if q in (0, 1):
                lefts.append(fields[q][0])
                rights.append(right(32, jnp.where(low_half, 0.0, pltpu.roll(m, 64, 1)), marked(4, l8 >= 64)))
                lefts.append(fields[q][1])
                rights.append(right(48, m * low_lanes, marked(3, l8 < 64) + marked(0, (l8 >= 64) & (l8 < 96))))
            lefts.append(others[q])
            rights.append(right(64, m, marked(2, (l8 % 32 == 20) & (l8 < 64)) if q in (0, 1) else none8))
        lefts += [std[32:48, 0:128], nxt[128:144, :], nxt[144:160, :]]
        rights += [
            right(0, None, marked(5, l8 >= 64)),
            right(0, None, marked(1, l8 < 64)),
            right(0, None, marked(1, l8 >= 64)),
        ]
        payload[...] = part + mm(split(jnp.concatenate(lefts, axis=1)), split(jnp.concatenate(rights, axis=1)), NT)

        to_first = send(total, total, cast_s.at[0], cast_r, sibling)
        to_root = send(payload, col_slots.at[member], col_s, col_r.at[member], column_root)

        @pl.when(jnp.logical_not(is_root))
        def _():
            to_root.start()

        zero = jnp.zeros((16, 128), F32)
        stacked = []
        for q in (-1, 0, 1, 2):
            if q in (0, 1):
                dh_q = jnp.where(low_half, pltpu.roll(fields[q][0], 64, 1), 0.0)
                own_q = jnp.where(low_half, fields[q][1], 0.0)
            else:
                dh_q, own_q = zero, zero
            stacked.append(jnp.concatenate([dh_q, own_q, others[q]], axis=0))
        back = mm(mix_back, split(jnp.concatenate(stacked, axis=1)))
        for q in (-1, 0, 1, 2):
            value = back[:, 128 * (q + 1) : 128 * (q + 2)]
            if q in (0, 1):
                value = value + jnp.where(low_half, fields[q][0], 0.0)
            gm[q + 1] = value
        y_back = []
        for d in STEPS:
            i = STEPS.index(-d)
            if abs(d) == 1:
                src, dst = gm.at[pl.ds(2 if d == 1 else 0, 2)], yb.at[i]
            else:
                src, dst = gm.at[pl.ds(3 if d == 2 else 0, 1)], yb.at[i, pl.ds(0 if d == 2 else 1, 1)]
            y_back.append(send(src, dst, yb_s.at[i], yb_r.at[i], at_y(d)))
        for c in y_back:
            c.start()

        edge_place = (place[0:8] < 2) | (place[0:8] == 17) | (place[0:8] == 18)

        def pack_back(block):
            return jnp.where(edge_place, block[0:8, :], pltpu.roll(block[8:16, :], 8, 1))

        def unpack_back(block):
            return jnp.concatenate([block, pltpu.roll(block, 120, 1)], axis=0)

        for c in y_back:
            c.wait_recv()
        own_rows = []
        for q in (0, 1):
            value = gm[q + 1]
            for d in (-2, -1, 1, 2):
                if (d, q) not in ((-2, 1), (2, 0)):
                    value = value + yb[STEPS.index(d), q] * there[d]
            own_rows.append(value)
        for i, d in enumerate(WIDE):
            value = jnp.zeros((16, 128), F32)
            for q in (0, 1):
                for p in (0, 1):
                    if p + d in SLOT:
                        moved = spread(own_rows[q], 2 * q + p - SLOT[p + d])
                        value = value + jnp.where(group == 2 * q + p, moved, 0.0)
            back_blocks[i] = value
            back_rims[i] = pack_back(value)
        x_back = round_xz(
            lambda d: back_blocks.at[WIDE.index(d)], xb, lambda d: back_rims.at[WIDE.index(d)], rim_b, xb_s, xb_r
        )
        for c in x_back:
            c.start()

        my_place = (ix // Z_LOW) * n_z + iz
        to_plane = [
            send(plane_slots.at[my_place], plane_slots.at[my_place], plane_s.at[k], plane_r.at[k], in_plane(k))
            for k in range(1, n_plane)
        ]

        @pl.when(is_root)
        def _():
            value = payload[...]
            for k in range(CORES * n_layers):
                if k != 1:
                    send(payload, col_slots.at[k], col_s, col_r.at[k], sibling).wait_recv()
                    value = value + col_slots[k]
            plane_slots[my_place] = value
            for c in to_plane:
                c.start()

        for c in x_back:
            c.wait_recv()
        level = back_blocks[WIDE.index(0)]
        for i in range(len(LEVEL)):
            level = level + xb[i]
        sides = []
        for z in (-1, 1):
            value = rim_b[ROUND.index((-2, z))]
            for d in WIDE[1:]:
                value = value + rim_b[ROUND.index((d, z))]
            sides.append(unpack_back(value))
        level, sides = split(level), [split(v) for v in sides]
        value = mm_exact(level, maps[0], NT) + mm_exact(sides[0], maps[2], NT) + mm_exact(sides[1], maps[1], NT)
        value = value * jnp.where(group < 2, 0.25 / (1.0 + there[-1]), 0.25 / (1.0 + there[1]))
        for q in (0, 1):
            for p in (0, 1):
                g_coarse[:, p, q, :] = value[:, 32 * (2 * q + p) : 32 * (2 * q + p) + 32]
        saves[0].start()

        half = n_layers // 2
        up_column = [send(total, total, cast_s.at[k], cast_r, in_column(k, 1)) for k in range(1, n_layers)]
        is_helper = (core == 0) & (layer == 0)

        @pl.when(is_root)
        def _():
            for k, c in enumerate(to_plane):
                c.wait_recv()
            value = plane_slots[0]
            for k in range(1, n_plane):
                value = value + plane_slots[k]
            total[...] = value
            for c in [to_first] + up_column[0 : half - 1]:
                c.start()

        @pl.when(jnp.logical_not(is_root))
        def _():
            to_first.wait_recv()

        @pl.when(on_core1 & (layer != 0))
        def _():
            to_first.start()

        @pl.when(is_helper)
        def _():
            for c in up_column[half - 1 :]:
                c.start()

        sums = total[...] * factor
        g_node_out[...] = sums[:, 0:16]
        g_edge_in[...] = sums[:, 48:83]
        back = mm(n_back, split(sums))
        g_edge_out[...] = back[:, 16:32]
        g_node_in[:, 0:16] = sums[:, 32:48]
        g_node_in[:, 16:32] = mm(split(sums[:, 16:32]), split(edge_out[...]), NT) + sums[:, 85:86] * biases[1:2, :]
        r, c = iota((8, 256), 0), iota((8, 256), 1)
        pick = ones_where(((r == 0) & (c == 83)) | ((r == 1) & (c == 128 + 85)) | ((r == 2) & (c == 84))).astype(BF16)
        g_biases[...] = exact_mm(pick, split(jnp.concatenate([sums, back], axis=1)), NT)[0:3, :]
        for c in saves[1:]:
            c.start()

        for c in x_sends + y_sends + y_back + x_back:
            c.wait_send()

        @pl.when(on_core1)
        def _():
            to_first.wait_send()

        @pl.when(jnp.logical_not(is_root))
        def _():
            to_root.wait_send()

        @pl.when(is_root)
        def _():
            for c in to_plane + up_column[0 : half - 1]:
                c.wait_send()

        @pl.when(is_helper)
        def _():
            for c in up_column[half - 1 :]:
                c.wait_send()

        for c in saves:
            c.wait()

    block = pltpu.VMEM((16, 128), F32)

    def blocks(*lead):
        return pltpu.VMEM(lead + (16, 128), F32)

    dma = pltpu.SemaphoreType.DMA
    scratch = [
        *(pltpu.VMEM(s, F32) for s in RESULTS),
        pltpu.VMEM((16, 2, 2, 32), F32),
        pltpu.VMEM((16, 8, 8, 128), F32),
        pltpu.VMEM((16, 35), F32),
        pltpu.VMEM((16, 16), F32),
        pltpu.VMEM((16, 32), F32),
        pltpu.VMEM((16, 16), F32),
        pltpu.VMEM((3, 16), F32),
        pltpu.VMEM((TABLE_ROWS, 128), F32),
        block,
        pltpu.VMEM((8, 128), F32),
        blocks(len(LEVEL)),
        pltpu.VMEM((len(ROUND), 8, 128), F32),
        blocks(2),
        blocks(4, 2),
        blocks(4),
        pltpu.VMEM((128, 128), F32),
        pltpu.VMEM((14 * 128, 128), F32),
        pltpu.VMEM((6, 8, 16, 8, 128), F32),
        pltpu.VMEM((8, 16, 8, 128), F32),
        pltpu.VMEM((16, 8, 1024), F32),
        pltpu.VMEM((16, 8, 1024), F32),
        pltpu.VMEM((16, 8, 1024), F32),
        pltpu.VMEM((16, 8, 1024), F32),
        pltpu.VMEM((16, 8, 19 * 128), F32),
        blocks(4),
        blocks(4, 2),
        blocks(len(WIDE)),
        pltpu.VMEM((len(WIDE), 8, 128), F32),
        blocks(len(LEVEL)),
        pltpu.VMEM((len(ROUND), 8, 128), F32),
        block,
        blocks(CORES * n_layers),
        blocks(n_plane),
        block,
        dma((8,)),
        dma((len(XZ),)), dma((len(XZ),)), dma((4,)), dma((4,)), dma((4,)), dma((4,)), dma((len(XZ),)), dma((len(XZ),)),
        dma, dma((CORES * n_layers,)), dma((n_plane,)), dma((n_plane,)), dma((n_layers,)), dma, dma((6,)),
    ]
    return pl.pallas_call(
        kernel,
        out_shape=[jax.ShapeDtypeStruct(s, F32) for s in RESULTS],
        in_specs=[pl.BlockSpec(memory_space=pltpu.HBM)] * 8,
        out_specs=[pl.BlockSpec(memory_space=pltpu.HBM)] * 6,
        scratch_shapes=scratch,
        compiler_params=pltpu.CompilerParams(
            collective_id=0, has_side_effects=True, vmem_limit_bytes=60 * 1024 * 1024
        ),
    )


def make_hand_over():
    def kernel(*refs):
        sources, outs, buffers, sem = refs[0:6], refs[6:12], refs[12:18], refs[18]
        reads = [pltpu.make_async_copy(sources[i], buffers[i], sem.at[0, i]) for i in range(6)]
        writes = [pltpu.make_async_copy(buffers[i], outs[i], sem.at[1, i]) for i in range(6)]
        for c in reads:
            c.start()
        for read, write in zip(reads, writes):
            read.wait()
            write.start()
        for c in writes:
            c.wait()

    return pl.pallas_call(
        kernel,
        out_shape=[jax.ShapeDtypeStruct(s, F32) for s in RESULTS],
        in_specs=[pl.BlockSpec(memory_space=pltpu.HBM)] * 6,
        out_specs=[pl.BlockSpec(memory_space=pltpu.HBM)] * 6,
        scratch_shapes=[pltpu.VMEM(s, F32) for s in RESULTS] + [pltpu.SemaphoreType.DMA((2, 6))],
        compiler_params=pltpu.CompilerParams(vmem_limit_bytes=60 * 1024 * 1024),
    )


def solution(mesh):
    sizes = (mesh.shape["gx"], mesh.shape["gy"], mesh.shape["gz"])
    table = make_table()

    def on_device(coarse, cotangent, edge_in, edge_out, node_in, node_out, biases):
        nodes = cotangent.shape[1] * cotangent.shape[2] * cotangent.shape[3] * sizes[0] * sizes[1] * sizes[2]
        results = make_main(sizes, float(nodes) ** -0.5)(
            coarse, cotangent, edge_in, edge_out, node_in, node_out, biases, jnp.asarray(table)
        )
        return tuple(make_hand_over()(*results))

    placed = (P(None, "gx", "gy", "gz"), P(None, "gx", "gy", "gz"), P(), P(), P(), P(), P())
    return jax.shard_map(
        on_device,
        mesh=mesh,
        in_specs=placed,
        out_specs=(P(None, "gx", "gy", "gz"), P(), P(), P(), P(), P()),
        check_vma=False,
    )
```

```python
import jax
import jax.numpy as jnp
import numpy as np
from jax import lax
from jax.experimental import pallas as pl
from jax.experimental.pallas import tpu as pltpu
from jax.sharding import PartitionSpec as P

MESH = pl.DeviceIdType.MESH
F32 = jnp.float32
BF16 = jnp.bfloat16
T = np.array(
    [
        -1.0,
        -0.8717401485096066,
        -0.5917001814331423,
        -0.2092992179024789,
        0.2092992179024789,
        0.5917001814331423,
        0.8717401485096066,
        1.0,
    ]
)
L0, L1 = (1.0 - T) / 2.0, (1.0 + T) / 2.0
LOG2E = float(np.log2(np.e))
LN2 = float(np.log(2.0))
GAP_UP = [float(T[i + 1] - T[i]) if i < 7 else float(T[1] - T[0]) for i in range(8)]
GAP_DOWN = [float(T[i - 1] - T[i]) if i > 0 else float(T[6] - T[7]) for i in range(8)]
Z_LOW = 4
CORES = 2
ABSENT = -1.0e5
SLOT = {0: 0, 1: 1, -1: 2, 2: 3}
STEPS = (-2, -1, 1, 2)
WIDE = (-2, -1, 0, 1, 2)
XZ = tuple((x, z) for x in WIDE for z in (-1, 0, 1) if (x, z) != (0, 0))
ROUND = tuple(d for d in XZ if d[1] != 0)
LEVEL = tuple(d for d in XZ if d[1] == 0)

RZ, RZ_UP, RZ_DOWN, PROFILES, Y_STD, Y_NEXT, Y_GAP, DELTA = 0, 32, 64, 96, 136, 168, 296, 328
ALONG_Z = 376
TABLE_ROWS = 504


def make_table():
    table = np.zeros((TABLE_ROWS, 128))
    for lane in range(128):
        e, a = divmod(lane, 8)
        table[RZ + e + 1, lane] += L0[a]
        table[RZ + e + 2, lane] += L1[a]
        if a < 7:
            table[RZ_UP + e + 1, lane] += L0[a + 1]
            table[RZ_UP + e + 2, lane] += L1[a + 1]
        else:
            table[RZ_UP + e + 2, lane] += L0[1]
            table[RZ_UP + e + 3, lane] += L1[1]
        if a > 0:
            table[RZ_DOWN + e + 1, lane] += L0[a - 1]
            table[RZ_DOWN + e + 2, lane] += L1[a - 1]
        else:
            table[RZ_DOWN + e, lane] += L0[6]
            table[RZ_DOWN + e + 1, lane] += L1[6]
        table[RZ_UP + 20, lane] = GAP_UP[a]
        table[RZ_DOWN + 20, lane] = GAP_DOWN[a]
    up = np.zeros((4, 8))
    down = np.zeros((4, 8))
    for y in range(8):
        if y < 7:
            up[1, y], up[2, y] = L0[y + 1], L1[y + 1]
        else:
            up[2, y], up[3, y] = L0[1], L1[1]
        if y > 0:
            down[1, y], down[2, y] = L0[y - 1], L1[y - 1]
        else:
            down[0, y], down[1, y] = L0[6], L1[6]
    for i, profile in enumerate((L1, up[2], up[3], down[2], down[0])):
        table[PROFILES + 8 * i : PROFILES + 8 * i + 8] = profile[:, None]
    for c in range(16):
        for y in range(8):
            lane = 8 * c + y
            table[Y_STD + c, lane] = L0[y]
            table[Y_STD + 16 + c, lane] = L1[y]
            for q in range(4):
                table[Y_NEXT + 16 * q + c, lane] = up[q, y]
                table[Y_NEXT + 64 + 16 * q + c, lane] = down[q, y]
            table[Y_GAP + c, lane] = GAP_UP[y]
            table[Y_GAP + 16 + c, lane] = GAP_DOWN[y]
            table[DELTA + c, lane] = 1.0
            table[DELTA + 16 + c, lane] = 1.0 if y == 0 else 0.0
            table[DELTA + 32 + c, lane] = 1.0 if y == 7 else 0.0
    table[ALONG_Z : ALONG_Z + 128, 0:96] = table[RZ : RZ + 96].T
    return table.astype(np.float32)


RESULTS = ((16, 2, 2, 32), (16, 35), (16, 16), (16, 32), (16, 16), (3, 16))
NN = (((1,), (0,)), ((), ()))
NT = (((1,), (1,)), ((), ()))


def dot(a, b, dims=NN):
    return lax.dot_general(a, b, dims, preferred_element_type=F32)


def split(a):
    high = a.astype(BF16)
    return high, (a - high.astype(F32)).astype(BF16)


def mm(a, b, dims=NN):
    (ah, al), (bh, bl) = a, b
    at = dims[0][1][0]
    return dot(jnp.concatenate([ah, ah, al], axis=1), jnp.concatenate([bh, bl, bh], axis=at), dims)


def mm_exact(a, b, dims=NN):
    return dot(jnp.concatenate([a[0], a[1]], axis=1), jnp.concatenate([b, b], axis=dims[0][1][0]), dims)


def exact_mm(a, b, dims=NN):
    return dot(a, b[0], dims) + dot(a, b[1], dims)


def iota(shape, dim):
    return lax.broadcasted_iota(jnp.int32, shape, dim)


def ones_where(mask):
    return jnp.where(mask, 1.0, 0.0).astype(F32)


def spread(a, k):
    k = k % 4
    return a if k == 0 else pltpu.roll(a, 32 * k, 1)


def vertex_maps():
    row, col = iota((128, 128), 0), iota((128, 128), 1)
    layer, vertex = row % 32, col % 32 - 1
    same = (row // 32 == col // 32) & (vertex < 18)
    maps = []
    for shift in (0, 16, -16):
        v = vertex + shift
        maps.append(ones_where(same & ((layer == 2 * v - 1) | (layer == 2 * v))).astype(BF16))
    return maps


def make_main(sizes, factor):
    n_x, n_y, n_z = sizes
    z_high = n_y // CORES
    n_layers = z_high * Z_LOW
    n_cols = n_x // Z_LOW
    n_plane = n_cols * n_z

    def kernel(
        coarse_in, cot_in, edge_in_in, edge_out_in, node_in_in, node_out_in, biases_in, table_in,
        *refs,
    ):
        results, outs, refs = refs[0:6], refs[6:12], refs[12:]
        (
        coarse, cot, edge_in, edge_out, node_in, node_out, biases, table, p0, p0_rim, xr, rim_r, vx, yr, means, lhs_rows, rows, e_all, e_sum, s_all, hn_all, u_all, g_all, xf,
        gm, yb, back_blocks, back_rims, xb, rim_b, payload, col_slots, plane_slots, total,
        load_sem, xf_s, xf_r, yf_s, yf_r, yb_s, yb_r, xb_s, xb_r,
        col_s, col_r, plane_s, plane_r, cast_s, cast_r, save_sem,
        ) = refs
        g_coarse, g_edge_in, g_edge_out, g_node_in, g_node_out, g_biases = outs
        saves = [pltpu.make_async_copy(src, dst, save_sem.at[i]) for i, (src, dst) in enumerate(zip(outs, results))]
        ix, iy, iz = lax.axis_index("gx"), lax.axis_index("gy"), lax.axis_index("gz")
        low = lax.rem(ix, Z_LOW)
        core = lax.rem(iy, CORES)
        layer = (iy // CORES) * Z_LOW + low
        on_core1 = core == 1
        is_root = on_core1 & (layer == 0)
        member = layer * CORES + core

        def at_xz(d):
            return (lax.rem(ix + (d[0] + n_x), n_x), iy, lax.rem(iz + (d[1] + n_z), n_z))

        def at_y(d):
            return (ix, lax.rem(iy + (d + n_y), n_y), iz)

        sibling = (ix, iy + 1 - 2 * core, iz)
        column_root = (ix - low, 1, iz)

        def in_column(k, c):
            return (ix + k % Z_LOW, (k // Z_LOW) * CORES + c, iz)

        def in_plane(k):
            col, row = k // n_z, k % n_z
            return (lax.rem(ix + Z_LOW * col, n_x), iy, lax.rem(iz + row, n_z))

        def send(src, dst, send_sem, recv_sem, device):
            return pltpu.make_async_remote_copy(
                src_ref=src, dst_ref=dst, send_sem=send_sem, recv_sem=recv_sem, device_id=device, device_id_type=MESH
            )

        def signal(device):
            pl.semaphore_signal(barrier, inc=1, device_id=device, device_id_type=MESH)

        loads = [
            pltpu.make_async_copy(src, dst, load_sem.at[i])
            for i, (src, dst) in enumerate(
                (
                    (coarse_in, coarse),
                    (edge_in_in, edge_in),
                    (edge_out_in, edge_out),
                    (node_in_in, node_in),
                    (node_out_in, node_out),
                    (biases_in, biases),
                    (table_in, table),
                    (cot_in, cot),
                )
            )
        ]
        loads[0].start()
        barrier = pltpu.get_barrier_semaphore()
        for d in STEPS:
            signal(at_y(d))
        for d in XZ:
            signal(at_xz(d))

        @pl.when(is_root)
        def _():
            for k in range(1, n_layers):
                for c in range(CORES):
                    signal(in_column(k, c))
            for k in range(1, n_plane):
                signal(in_plane(k))

        for c in loads[1:]:
            c.start()
        expected = len(XZ) + len(STEPS) + jnp.where(layer != 0, 1, 0) + jnp.where(is_root, n_plane - 1, 0)

        lane = iota((16, 128), 1)
        group, place = lane // 32, lane % 32
        rim = (place[0:8] < 3) | (place[0:8] >= 29)

        def pack_rims(block):
            return jnp.where(rim, block[0:8, :], pltpu.roll(block[8:16, :], 120, 1))

        def unpack_rims(block):
            return jnp.concatenate([block, pltpu.roll(block, 8, 1)], axis=0)

        loads[0].wait()
        block = coarse[...]
        block = jnp.concatenate([block[:, p, q, :] for q in (0, 1) for p in (0, 1)], axis=1)
        p0[...] = block
        p0_rim[...] = pack_rims(block)
        pl.semaphore_wait(barrier, expected)

        def round_xz(level_src, level_dst, rim_src, rim_dst, send_sems, recv_sems):
            copies = []
            for d in ROUND + LEVEL:
                back = (-d[0], -d[1])
                i = XZ.index(back)
                if d[1] == 0:
                    src, dst = level_src(d[0]), level_dst.at[LEVEL.index(back)]
                else:
                    src, dst = rim_src(d[0]), rim_dst.at[ROUND.index(back)]
                copies.append(send(src, dst, send_sems.at[i], recv_sems.at[i], at_xz(d)))
            return copies

        x_sends = round_xz(lambda d: p0, xr, lambda d: p0_rim, rim_r, xf_s, xf_r)
        for c in x_sends:
            c.start()

        for c in loads[1:7]:
            c.wait()
        w_own, w_other = edge_in[:, 0:16], edge_in[:, 16:32]
        col_x, col_y, col_z = edge_in[:, 32:33], edge_in[:, 33:34], edge_in[:, 34:35]
        n_own, n_gathered = node_in[:, 0:16], node_in[:, 16:32]
        eye = ones_where(iota((16, 16), 0) == iota((16, 16), 1)).astype(BF16)
        delta = table[DELTA : DELTA + 16, :].astype(BF16)
        same_y = iota((128, 128), 0) % 8 == iota((128, 128), 1) % 8

        def transposed(w):
            return exact_mm(eye, split(w), NT)

        def widen(w):
            parts = []
            for part in split(w):
                left = dot(delta, part, (((0,), (0,)), ((), ()))).astype(BF16)
                parts.append(jnp.where(same_y, dot(left, delta), 0.0).astype(BF16))
            return tuple(parts)

        m1 = mm(split(n_gathered), split(edge_out[...]))
        m1_wide = widen(m1)
        n_back = split(transposed(n_gathered))
        m1_back = widen(transposed(m1))
        out_back = widen(transposed(node_out[...]))
        mix = split(jnp.concatenate([w_own, n_own, w_other], axis=0))
        mix_back = split(jnp.concatenate([transposed(n_own), transposed(w_own), transposed(w_other)], axis=1))
        bias_rows = biases[...]
        bias_cols = exact_mm(eye, split(bias_rows), NT)
        b0_col, b1_row, b2_col = bias_cols[:, 0:1], bias_rows[1:2, :], bias_cols[:, 2:3]
        nb_col = jnp.sum(n_gathered * b1_row, axis=1, keepdims=True)
        maps = vertex_maps()
        gap_lane = ones_where((place == 20) & (group < 2))

        def blocks4(first):
            t = table[first : first + 32, :]
            zero = jnp.zeros((32, 128), F32)
            return split(
                jnp.concatenate(
                    [jnp.concatenate([t if i == j else zero for j in range(4)], axis=1) for i in range(4)], axis=0
                )
            )

        rz, rz_up, rz_down = blocks4(RZ), blocks4(RZ_UP), blocks4(RZ_DOWN)
        back_z = table[ALONG_Z : ALONG_Z + 128, :]
        group_z = iota((128, 128), 1) // 32

        def back_blocks_z(kind, n):
            return split(jnp.concatenate([jnp.where(group_z == i, spread(back_z, i - kind), 0.0) for i in range(n)], axis=0))

        to_rz, to_rz_up, to_rz_down = back_blocks_z(0, 4), back_blocks_z(1, 2), back_blocks_z(2, 2)

        loads[7].wait()
        for k in range(4):
            wide = jnp.concatenate([cot[:, 2 * k + i].reshape(128, 128) for i in (0, 1)], axis=1)
            u_all[:, :, 256 * k : 256 * k + 256] = mm(out_back, split(wide)).reshape(16, 8, 256)
        sum_all, sum_one = cot[:, 0], jnp.zeros((16, 8, 128), F32)
        for x in range(1, 8):
            sum_all = sum_all + cot[:, x]
            sum_one = sum_one + float(L1[x]) * cot[:, x]
        xf[:, :, 0:128] = sum_all - sum_one
        xf[:, :, 128:256] = sum_one

        for c in x_sends:
            c.wait_recv()
        pieces = []
        for d in WIDE:
            level = p0[...] if d == 0 else xr[LEVEL.index((d, 0))]
            rims = [unpack_rims(rim_r[ROUND.index((d, z))]) for z in (-1, 1)]
            pieces.append(jnp.concatenate([level] + rims, axis=1))
        summed = mm_exact(split(jnp.concatenate(pieces, axis=0)), jnp.concatenate(maps, axis=0))
        x_blocks = {d: summed[16 * i : 16 * i + 16, :] for i, d in enumerate(WIDE)}
        for q in (0, 1):
            acc = jnp.zeros((16, 128), F32)
            for vertex in (-1, 0, 1, 2):
                for d in (vertex - 1, vertex):
                    moved = spread(x_blocks[d], SLOT[vertex] - (2 * q + vertex - d))
                    acc = acc + jnp.where(group == SLOT[vertex], moved, 0.0)
            vx[q] = acc
        y_sends = []
        for d in STEPS:
            i = STEPS.index(-d)
            qs = pl.ds(0, 2) if abs(d) == 1 else pl.ds(1 if d == 2 else 0, 1)
            y_sends.append(send(vx.at[qs], yr.at[i, qs], yf_s.at[i], yf_r.at[i], at_y(d)))
        for c in y_sends:
            c.start()

        def exists(d):
            return jnp.where((iy + d >= 0) & (iy + d < n_y), 1.0, 0.0).astype(F32)

        there = {d: exists(d) for d in (-2, -1, 0, 1, 2)}
        wall_low, wall_high = 1.0 - there[-1], 1.0 - there[1]
        y_index = iota((8, 128), 0)
        count = 6.0 - wall_low * ones_where(y_index == 0) - wall_high * ones_where(y_index == 7)
        ly, up1, up2, down1, down0 = (table[PROFILES + 8 * i : PROFILES + 8 * i + 8, :] for i in range(5))

        for c in y_sends:
            c.wait_recv()

        def y_block(d, q):
            return vx[q] if d == 0 else yr[STEPS.index(d), q] * there[d]

        for q in (-1, 0, 1, 2):
            copies = jnp.maximum(there[q - 1] + there[q], 1.0)
            means[q + 1] = (y_block(q - 1, 1) + y_block(q, 0)) * (0.25 / copies)

        mixed = mm(mix, split(jnp.concatenate([means[i] for i in range(4)], axis=1)))
        for i in range(4):
            lanes = slice(128 * i, 128 * i + 128)
            if i in (1, 2):
                lhs_rows[48 * (i - 1) : 48 * (i - 1) + 32, :] = mixed[0:32, lanes]
                lhs_rows[48 * (i - 1) + 32 : 48 * i, :] = mixed[32:48, lanes] + col_z * gap_lane
            else:
                first = 96 if i == 0 else 112
                lhs_rows[first : first + 16, :] = mixed[32:48, lanes]
        along = mm(split(lhs_rows[...]), rz)
        other01 = split(jnp.concatenate([lhs_rows[32:48, :], lhs_rows[80:96, :]], axis=0))
        along_up = mm(other01, (rz_up[0][:, 0:256], rz_up[1][:, 0:256]))
        along_down = mm(other01, (rz_down[0][:, 0:256], rz_down[1][:, 0:256]))

        def vertex_rows(field, q, vertex):
            first = {0: 0, 1: 48}[q] + 16 * field if q in (0, 1) else (96 if q == -1 else 112)
            s = SLOT[vertex]
            return along[first : first + 16, 128 * s : 128 * s + 128]

        def next_rows(source, q, vertex):
            return source[16 * q : 16 * q + 16, 128 * vertex : 128 * vertex + 128]

        def put(field, x, value):
            rows[pl.ds(128 * field + x, 16, stride=8), :] = value

        def line(a, b, t):
            return a + t * (b - a)

        for x in range(8):
            t = float(L1[x])
            here = float(T[x]) * col_x
            own = [
                (line(vertex_rows(0, q, 0), vertex_rows(0, q, 1), t) + (b0_col - here - (2 * q - 1.0) * col_y)) * LOG2E
                for q in (0, 1)
            ]
            put(0, x, own[0])
            put(1, x, own[1] - own[0])
            other = {
                q: (line(vertex_rows(2, q, 0), vertex_rows(2, q, 1), t) + (here + (2 * q - 1.0) * col_y)) * LOG2E
                for q in (-1, 0, 1, 2)
            }
            put(2, x, other[0])
            put(3, x, other[1] - other[0])
            put(5, x, (other[2] - other[0]) * there[1] + ABSENT * wall_high)
            put(6, x, (other[-1] - other[0]) * there[-1] + ABSENT * wall_low)
            for f, source in ((7, along_up), (9, along_down)):
                z = [
                    (line(next_rows(source, q, 0), next_rows(source, q, 1), t) + (here + (2 * q - 1.0) * col_y)) * LOG2E
                    for q in (0, 1)
                ]
                put(f, x, z[0])
                put(f + 1, x, z[1] - z[0])
            hn = [line(vertex_rows(1, q, 0), vertex_rows(1, q, 1), t) for q in (0, 1)]
            put(11, x, hn[0] + b2_col)
            put(12, x, hn[1] - hn[0])
        put(13, 0, jnp.broadcast_to(nb_col, (16, 128)))
        for side, (a, b, t, at) in enumerate(((-1, 0, float(L1[6]), float(T[6]) - 2.0), (1, 2, float(L1[1]), float(T[1]) + 2.0))):
            other = [
                (line(vertex_rows(2, q, a), vertex_rows(2, q, b), t) + (at * col_x + (2 * q - 1.0) * col_y)) * LOG2E
                for q in (0, 1)
            ]
            put(4, 2 * side, other[0])
            put(4, 2 * side + 1, other[1] - other[0])

        def forward(c, carry):
            def row(field, x):
                return rows[pl.ds(128 * field + 8 * c + x, 1), :]

            other = [row(4, 0) + ly * row(4, 1)]
            counted = count * row(13, 0)
            for x in range(8):
                other.append(row(2, x) + ly * row(3, x))
            other.append(row(4, 2) + ly * row(4, 3))
            for x in range(8):
                own = row(0, x) + ly * row(1, x)
                a, d = row(2, x), row(3, x)
                senders = (
                    other[x + 2],
                    other[x],
                    a + up1 * d + up2 * row(5, x),
                    a + down1 * d + down0 * row(6, x),
                    row(7, x) + ly * row(8, x),
                    row(9, x) + ly * row(10, x),
                )
                tops, decays = None, None
                for k, sender in enumerate(senders):
                    z = own + sender
                    decay = jnp.exp2(jnp.minimum(z, 0.0))
                    top = jnp.maximum(z, 0.0)
                    e_all[k, x, c] = decay
                    tops = top if tops is None else tops + top
                    decays = decay if decays is None else decays + decay
                e_sum[x, c] = decays
                s_all[c, :, 128 * x : 128 * x + 128] = LN2 * tops + (decays - count)
                hn_all[c, :, 128 * x : 128 * x + 128] = row(11, x) + ly * row(12, x) + counted
            return carry

        lax.fori_loop(0, 16, forward, 0, unroll=2)

        outer_out = jnp.zeros((128, 128), F32)
        outer_in = jnp.zeros((128, 128), F32)
        dh_all = jnp.zeros((16, 8, 128), F32)
        dh_one = jnp.zeros((16, 8, 128), F32)
        for k in range(4):
            lanes = slice(256 * k, 256 * k + 256)
            s = split(s_all[:, :, lanes].reshape(128, 256))
            h = mm(m1_wide, s) + hn_all[:, :, lanes].reshape(128, 256)
            decay = jnp.exp(jnp.minimum(h, 0.0))
            a = jnp.maximum(h, 0.0) + (decay - 1.0)
            dh = decay * u_all[:, :, lanes].reshape(128, 256)
            dh_parts = split(dh)
            g_all[:, :, lanes] = mm(m1_back, dh_parts).reshape(16, 8, 256)
            wide = jnp.concatenate([cot[:, 2 * k + i].reshape(128, 128) for i in (0, 1)], axis=1)
            outer_out = outer_out + mm(split(wide), split(a), NT)
            outer_in = outer_in + mm(dh_parts, s, NT)
            for i in (0, 1):
                part = dh[:, 128 * i : 128 * i + 128].reshape(16, 8, 128)
                dh_all = dh_all + part
                dh_one = dh_one + float(L1[2 * k + i]) * part
        xf[:, :, 256:384] = dh_all - dh_one
        xf[:, :, 384:512] = dh_one

        def backward(c, carry):
            g = [g_all[c, :, 128 * x : 128 * x + 128] for x in range(8)]
            own = [g[x] * e_sum[x, c] for x in range(8)]

            def bz(k, x):
                return g[x] * e_all[k, x, c]

            def save(i, value):
                xf[c, :, 128 * i : 128 * i + 128] = value

            def reduce(first, values):
                everything, one = values[0], float(L1[1]) * values[1]
                for x in range(1, 8):
                    everything = everything + values[x]
                for x in range(2, 8):
                    one = one + float(L1[x]) * values[x]
                save(first, everything - one)
                save(first + 1, one)

            reduce(4, own)
            ups = [bz(0, x) for x in range(8)]
            downs = [bz(1, x) for x in range(8)]
            acc = GAP_UP[0] * ups[0] + GAP_DOWN[0] * downs[0]
            for x in range(1, 8):
                acc = acc + GAP_UP[x] * ups[x] + GAP_DOWN[x] * downs[x]
            save(6, acc)
            at = [downs[1]] + [ups[x - 1] + downs[x + 1] for x in range(1, 7)] + [ups[6]]
            everything, one = at[0], float(L1[1]) * at[1]
            for x in range(1, 8):
                everything = everything + at[x]
            for x in range(2, 8):
                one = one + float(L1[x]) * at[x]
            save(7, everything - one + float(L1[6]) * downs[0])
            save(8, one + float(L0[1]) * ups[7])
            save(9, float(L0[6]) * downs[0])
            save(10, float(L1[1]) * ups[7])
            for k in range(4):
                reduce(11 + 2 * k, [bz(2 + k, x) for x in range(8)])
            return carry

        lax.fori_loop(0, 16, backward, 0, unroll=2)

        def along_z(first, n, by):
            return mm(
                split(xf[:, :, 128 * first : 128 * (first + n)].reshape(128, 128 * n)),
                (by[0][0 : 128 * n, :], by[1][0 : 128 * n, :]),
            )

        z1 = along_z(0, 4, to_rz)
        z2 = along_z(4, 3, to_rz)
        z3 = along_z(7, 4, to_rz) + along_z(15, 2, to_rz_up) + along_z(17, 2, to_rz_down)
        z4 = along_z(11, 4, to_rz)
        counting = (
            6.0 * table[DELTA : DELTA + 16, :]
            - wall_low * table[DELTA + 16 : DELTA + 32, :]
            - wall_high * table[DELTA + 32 : DELTA + 48, :]
        )
        left = split(jnp.concatenate([table[Y_STD : Y_STD + 32, :], counting], axis=0))
        std = mm(left, split(jnp.concatenate([z1, z2, z3], axis=1)))
        nxt = mm(split(table[Y_NEXT : Y_NEXT + 160, :]), split(z4))

        low_half, low_lanes = group < 2, ones_where(group < 2)
        fields = {}
        for q in (0, 1):
            r = slice(16 * q, 16 * q + 16)
            fields[q] = (std[r, 0:128], std[r, 128:256], std[r, 256:384])
        others = {}
        for q in (-1, 0, 1, 2):
            r_up = slice(16 * (q + 1), 16 * (q + 1) + 16)
            r_down = slice(64 + 16 * (q + 1), 64 + 16 * (q + 1) + 16)
            both = jnp.where(low_half, nxt[r_up, :] + pltpu.roll(nxt[r_down, :], 64, 1), 0.0)
            others[q] = both + fields[q][2] if q in (0, 1) else both

        summed_out = jnp.where(same_y, outer_out, 0.0)
        summed_in = jnp.where(same_y, outer_in, 0.0)
        big = exact_mm(delta, split(jnp.concatenate([summed_out, summed_in], axis=1)))
        r2, c2 = iota((128, 256), 0), iota((128, 256), 1)
        placing = ones_where((c2 // 128 * 16 + c2 % 128 // 8) == r2).astype(BF16)
        part = mm_exact(split(big), placing, NT)
        r8, l8 = iota((8, 128), 0), iota((8, 128), 1)

        def marked(r, mask):
            return ones_where((r8 == r) & mask)

        def right(first, rows16, special):
            pieces = []
            if rows16 is None:
                pieces.append(jnp.zeros((80, 128), F32))
            else:
                if first > 0:
                    pieces.append(jnp.zeros((first, 128), F32))
                pieces.append(rows16)
                if first < 64:
                    pieces.append(jnp.zeros((64 - first, 128), F32))
            pieces += [special, jnp.zeros((40, 128), F32)]
            return jnp.concatenate(pieces, axis=0)

        lefts, rights = [], []
        none8 = jnp.zeros((8, 128), F32)
        for q in (-1, 0, 1, 2):
            m = means[q + 1]
            if q in (0, 1):
                lefts.append(fields[q][0])
                rights.append(right(32, jnp.where(low_half, 0.0, pltpu.roll(m, 64, 1)), marked(4, l8 >= 64)))
                lefts.append(fields[q][1])
                rights.append(right(48, m * low_lanes, marked(3, l8 < 64) + marked(0, (l8 >= 64) & (l8 < 96))))
            lefts.append(others[q])
            rights.append(right(64, m, marked(2, (l8 % 32 == 20) & (l8 < 64)) if q in (0, 1) else none8))
        lefts += [std[32:48, 0:128], nxt[128:144, :], nxt[144:160, :]]
        rights += [
            right(0, None, marked(5, l8 >= 64)),
            right(0, None, marked(1, l8 < 64)),
            right(0, None, marked(1, l8 >= 64)),
        ]
        payload[...] = part + mm(split(jnp.concatenate(lefts, axis=1)), split(jnp.concatenate(rights, axis=1)), NT)

        to_first = send(total, total, cast_s.at[0], cast_r, sibling)
        to_root = send(payload, col_slots.at[member], col_s, col_r.at[member], column_root)

        @pl.when(jnp.logical_not(is_root))
        def _():
            to_root.start()

        zero = jnp.zeros((16, 128), F32)
        stacked = []
        for q in (-1, 0, 1, 2):
            if q in (0, 1):
                dh_q = jnp.where(low_half, pltpu.roll(fields[q][0], 64, 1), 0.0)
                own_q = jnp.where(low_half, fields[q][1], 0.0)
            else:
                dh_q, own_q = zero, zero
            stacked.append(jnp.concatenate([dh_q, own_q, others[q]], axis=0))
        back = mm(mix_back, split(jnp.concatenate(stacked, axis=1)))
        for q in (-1, 0, 1, 2):
            value = back[:, 128 * (q + 1) : 128 * (q + 2)]
            if q in (0, 1):
                value = value + jnp.where(low_half, fields[q][0], 0.0)
            gm[q + 1] = value
        y_back = []
        for d in STEPS:
            i = STEPS.index(-d)
            if abs(d) == 1:
                src, dst = gm.at[pl.ds(2 if d == 1 else 0, 2)], yb.at[i]
            else:
                src, dst = gm.at[pl.ds(3 if d == 2 else 0, 1)], yb.at[i, pl.ds(0 if d == 2 else 1, 1)]
            y_back.append(send(src, dst, yb_s.at[i], yb_r.at[i], at_y(d)))
        for c in y_back:
            c.start()

        edge_place = (place[0:8] < 2) | (place[0:8] == 17) | (place[0:8] == 18)

        def pack_back(block):
            return jnp.where(edge_place, block[0:8, :], pltpu.roll(block[8:16, :], 8, 1))

        def unpack_back(block):
            return jnp.concatenate([block, pltpu.roll(block, 120, 1)], axis=0)

        for c in y_back:
            c.wait_recv()
        own_rows = []
        for q in (0, 1):
            value = gm[q + 1]
            for d in (-2, -1, 1, 2):
                if (d, q) not in ((-2, 1), (2, 0)):
                    value = value + yb[STEPS.index(d), q] * there[d]
            own_rows.append(value)
        for i, d in enumerate(WIDE):
            value = jnp.zeros((16, 128), F32)
            for q in (0, 1):
                for p in (0, 1):
                    if p + d in SLOT:
                        moved = spread(own_rows[q], 2 * q + p - SLOT[p + d])
                        value = value + jnp.where(group == 2 * q + p, moved, 0.0)
            back_blocks[i] = value
            back_rims[i] = pack_back(value)
        x_back = round_xz(
            lambda d: back_blocks.at[WIDE.index(d)], xb, lambda d: back_rims.at[WIDE.index(d)], rim_b, xb_s, xb_r
        )
        for c in x_back:
            c.start()

        my_place = (ix // Z_LOW) * n_z + iz
        to_plane = [
            send(plane_slots.at[my_place], plane_slots.at[my_place], plane_s.at[k], plane_r.at[k], in_plane(k))
            for k in range(1, n_plane)
        ]

        @pl.when(is_root)
        def _():
            value = payload[...]
            for k in range(CORES * n_layers):
                if k != 1:
                    send(payload, col_slots.at[k], col_s, col_r.at[k], sibling).wait_recv()
                    value = value + col_slots[k]
            plane_slots[my_place] = value
            for c in to_plane:
                c.start()

        for c in x_back:
            c.wait_recv()
        level = back_blocks[WIDE.index(0)]
        for i in range(len(LEVEL)):
            level = level + xb[i]
        sides = []
        for z in (-1, 1):
            value = rim_b[ROUND.index((-2, z))]
            for d in WIDE[1:]:
                value = value + rim_b[ROUND.index((d, z))]
            sides.append(unpack_back(value))
        level, sides = split(level), [split(v) for v in sides]
        value = mm_exact(level, maps[0], NT) + mm_exact(sides[0], maps[2], NT) + mm_exact(sides[1], maps[1], NT)
        value = value * jnp.where(group < 2, 0.25 / (1.0 + there[-1]), 0.25 / (1.0 + there[1]))
        for q in (0, 1):
            for p in (0, 1):
                g_coarse[:, p, q, :] = value[:, 32 * (2 * q + p) : 32 * (2 * q + p) + 32]
        saves[0].start()

        half = n_layers // 2
        up_column = [send(total, total, cast_s.at[k], cast_r, in_column(k, 1)) for k in range(1, n_layers)]
        is_helper = (core == 0) & (layer == 0)

        @pl.when(is_root)
        def _():
            for k, c in enumerate(to_plane):
                c.wait_recv()
            value = plane_slots[0]
            for k in range(1, n_plane):
                value = value + plane_slots[k]
            total[...] = value
            for c in [to_first] + up_column[0 : half - 1]:
                c.start()

        @pl.when(jnp.logical_not(is_root))
        def _():
            to_first.wait_recv()

        @pl.when(on_core1 & (layer != 0))
        def _():
            to_first.start()

        @pl.when(is_helper)
        def _():
            for c in up_column[half - 1 :]:
                c.start()

        sums = total[...] * factor
        g_node_out[...] = sums[:, 0:16]
        g_edge_in[...] = sums[:, 48:83]
        back = mm(n_back, split(sums))
        g_edge_out[...] = back[:, 16:32]
        g_node_in[:, 0:16] = sums[:, 32:48]
        g_node_in[:, 16:32] = mm(split(sums[:, 16:32]), split(edge_out[...]), NT) + sums[:, 85:86] * biases[1:2, :]
        r, c = iota((8, 256), 0), iota((8, 256), 1)
        pick = ones_where(((r == 0) & (c == 83)) | ((r == 1) & (c == 128 + 85)) | ((r == 2) & (c == 84))).astype(BF16)
        g_biases[...] = exact_mm(pick, split(jnp.concatenate([sums, back], axis=1)), NT)[0:3, :]
        for c in saves[1:]:
            c.start()

        for c in x_sends + y_sends + y_back + x_back:
            c.wait_send()

        @pl.when(on_core1)
        def _():
            to_first.wait_send()

        @pl.when(jnp.logical_not(is_root))
        def _():
            to_root.wait_send()

        @pl.when(is_root)
        def _():
            for c in to_plane + up_column[0 : half - 1]:
                c.wait_send()

        @pl.when(is_helper)
        def _():
            for c in up_column[half - 1 :]:
                c.wait_send()

        for c in saves:
            c.wait()

    block = pltpu.VMEM((16, 128), F32)

    def blocks(*lead):
        return pltpu.VMEM(lead + (16, 128), F32)

    dma = pltpu.SemaphoreType.DMA
    scratch = [
        *(pltpu.VMEM(s, F32) for s in RESULTS),
        pltpu.VMEM((16, 2, 2, 32), F32),
        pltpu.VMEM((16, 8, 8, 128), F32),
        pltpu.VMEM((16, 35), F32),
        pltpu.VMEM((16, 16), F32),
        pltpu.VMEM((16, 32), F32),
        pltpu.VMEM((16, 16), F32),
        pltpu.VMEM((3, 16), F32),
        pltpu.VMEM((TABLE_ROWS, 128), F32),
        block,
        pltpu.VMEM((8, 128), F32),
        blocks(len(LEVEL)),
        pltpu.VMEM((len(ROUND), 8, 128), F32),
        blocks(2),
        blocks(4, 2),
        blocks(4),
        pltpu.VMEM((128, 128), F32),
        pltpu.VMEM((14 * 128, 128), F32),
        pltpu.VMEM((6, 8, 16, 8, 128), F32),
        pltpu.VMEM((8, 16, 8, 128), F32),
        pltpu.VMEM((16, 8, 1024), F32),
        pltpu.VMEM((16, 8, 1024), F32),
        pltpu.VMEM((16, 8, 1024), F32),
        pltpu.VMEM((16, 8, 1024), F32),
        pltpu.VMEM((16, 8, 19 * 128), F32),
        blocks(4),
        blocks(4, 2),
        blocks(len(WIDE)),
        pltpu.VMEM((len(WIDE), 8, 128), F32),
        blocks(len(LEVEL)),
        pltpu.VMEM((len(ROUND), 8, 128), F32),
        block,
        blocks(CORES * n_layers),
        blocks(n_plane),
        block,
        dma((8,)),
        dma((len(XZ),)), dma((len(XZ),)), dma((4,)), dma((4,)), dma((4,)), dma((4,)), dma((len(XZ),)), dma((len(XZ),)),
        dma, dma((CORES * n_layers,)), dma((n_plane,)), dma((n_plane,)), dma((n_layers,)), dma, dma((6,)),
    ]
    return pl.pallas_call(
        kernel,
        out_shape=[jax.ShapeDtypeStruct(s, F32) for s in RESULTS],
        in_specs=[pl.BlockSpec(memory_space=pltpu.HBM)] * 8,
        out_specs=[pl.BlockSpec(memory_space=pltpu.HBM)] * 6,
        scratch_shapes=scratch,
        compiler_params=pltpu.CompilerParams(
            collective_id=0, has_side_effects=True, vmem_limit_bytes=60 * 1024 * 1024
        ),
    )


def make_hand_over():
    def kernel(*refs):
        sources, outs, buffers, sem = refs[0:6], refs[6:12], refs[12:18], refs[18]
        reads = [pltpu.make_async_copy(sources[i], buffers[i], sem.at[0, i]) for i in range(6)]
        writes = [pltpu.make_async_copy(buffers[i], outs[i], sem.at[1, i]) for i in range(6)]
        for c in reads:
            c.start()
        for read, write in zip(reads, writes):
            read.wait()
            write.start()
        for c in writes:
            c.wait()

    return pl.pallas_call(
        kernel,
        out_shape=[jax.ShapeDtypeStruct(s, F32) for s in RESULTS],
        in_specs=[pl.BlockSpec(memory_space=pltpu.HBM)] * 6,
        out_specs=[pl.BlockSpec(memory_space=pltpu.HBM)] * 6,
        scratch_shapes=[pltpu.VMEM(s, F32) for s in RESULTS] + [pltpu.SemaphoreType.DMA((2, 6))],
        compiler_params=pltpu.CompilerParams(vmem_limit_bytes=60 * 1024 * 1024),
    )


def solution(mesh):
    sizes = (mesh.shape["gx"], mesh.shape["gy"], mesh.shape["gz"])
    table = make_table()

    def on_device(coarse, cotangent, edge_in, edge_out, node_in, node_out, biases):
        nodes = cotangent.shape[1] * cotangent.shape[2] * cotangent.shape[3] * sizes[0] * sizes[1] * sizes[2]
        results = make_main(sizes, float(nodes) ** -0.5)(
            coarse, cotangent, edge_in, edge_out, node_in, node_out, biases, jnp.asarray(table)
        )
        return tuple(make_hand_over()(*results))

    placed = (P(None, "gx", "gy", "gz"), P(None, "gx", "gy", "gz"), P(), P(), P(), P(), P())
    return jax.shard_map(
        on_device,
        mesh=mesh,
        in_specs=placed,
        out_specs=(P(None, "gx", "gy", "gz"), P(), P(), P(), P(), P()),
        check_vma=False,
    )
```
